32 devices in a mesh: slab: 8 (over y, x, core), head: 4 (over z).
Axes of the slice: x: 2, y: 2, z: 4, core: 2. Of those that a mesh axis runs over, the one named last changes fastest.
Arguments:
- section_activations: bfloat16 [224, 384, 256], P('slab'), may hold values from -6 to 6
- kernel_weight: bfloat16 [27, 384, 384], replicated, may hold values from -0.0625 to 0.0625
- packed_output_gradient: bfloat16 [128, 384, 256], P('slab', 'head'), may hold values from -6 to 6
- clip_length: int32 [16], replicated, may hold values from 1 to 27, as said below
- clip_slab_index: int32 [16], replicated, may hold values from 0 to 7, as said below
- packed_clip_order: int32 [16], replicated, may hold values from 0 to 15, each once
Outputs:
- input_grad: bfloat16 [224, 384, 256], P('slab', 'head')
- weight_grad: bfloat16 [27, 384, 384], P(None, 'slab', 'head')
The draws below stay inside these ranges and needn't reach their ends.
Inputs may be any that keep to these rules, and one draw needn't show every extreme that they name: `clip_length`: the lengths of all clips sum to 128. `clip_slab_index`: every slab takes exactly two clips; the frames of a slab lie between 4 and 28, and in every draw one slab holds 28 frames and one holds 4. `packed_clip_order`: each clip appears once.
All inputs are finite; a program needn't handle non-finite values.
Results may differ from the reference program's by a relative error of at most 0.014.
Values may be sent and summed in bfloat16 or wider, within the bound.
No kernel may reach another device: no remote copies, remote signals or barrier semaphores. Data moves between devices by JAX's collectives and lax.ppermute only.
A program may use at most 448 MiB of HBM per device.

```python
import math
import jax
import jax.numpy as jnp
from jax import lax

CHANNEL_COUNT = 384
F_SEQ = 16
PIXEL_ROWS = 16
PIXEL_COLUMNS = 16
TAPS = 27
FRAME_PIXELS = 256
SLAB_FRAME_SLOTS = 28
FRAMES_OVERALL = 128
ENC_F = 224
CLIP_COUNT = 16
N_SLAB = 8


def clip_plan(key):
    key = jax.random.fold_in(key, 7)
    key_order, key_delta, key_first, key_place = jax.random.split(key, 4)
    slab_count = CLIP_COUNT // 2
    pair_count = slab_count // 2
    slab_order = jax.random.permutation(key_order, slab_count)
    delta = jax.random.randint(key_delta, (pair_count,), -(F_SEQ // 2), F_SEQ // 2 + 1)
    delta = delta.at[0].set(SLAB_FRAME_SLOTS - F_SEQ)
    loads = jnp.zeros((slab_count,), jnp.int32)
    loads = loads.at[slab_order[0::2]].set(F_SEQ + delta)
    loads = loads.at[slab_order[1::2]].set(F_SEQ - delta)
    first = jax.random.randint(key_first, (slab_count,), 1, loads)
    first = first.at[slab_order[0]].set(1)
    placing = jax.random.permutation(key_place, CLIP_COUNT)
    slab_of = placing // 2
    clip_lengths = jnp.where(placing % 2 == 0, first[slab_of], loads[slab_of] - first[slab_of])
    return (clip_lengths.astype(jnp.int32), slab_of.astype(jnp.int32))


def draw_clip_length(key, part):
    return clip_plan(key)[0]


def draw_clip_slab_index(key, part):
    return clip_plan(key)[1]


def levels(rng, extent, pieces, smallest, largest):
    loudness = 1.0
    for position, shards_of in pieces:
        steps = jax.random.uniform(jax.random.fold_in(jax.random.fold_in(rng, 6), position), (shards_of,), jnp.float32, smallest / len(pieces), largest / len(pieces))
        loudness = loudness * jnp.repeat(jnp.exp(steps), extent[position] // shards_of).reshape((-1,) + (1,) * (len(extent) - 1 - position))
    return loudness


def noise(rng, dims, spread, limit, cuts=(), held_as=jnp.bfloat16):
    level = levels(rng, dims, cuts, -0.22, 0.18) if cuts else 1.0
    array = jax.random.normal(rng, dims, jnp.float32) * spread * level
    return jnp.minimum(jnp.maximum(array, -limit), limit).astype(held_as)


def setup_inputs(seed: int = 0) -> dict:
    arg_keys = jax.random.split(jax.random.key(seed), 7)
    return {
        "section_activations": noise(arg_keys[0], (ENC_F, CHANNEL_COUNT, FRAME_PIXELS), 1.0, 6.0, ((0, 8),)),
        "kernel_weight": noise(arg_keys[1], (TAPS, CHANNEL_COUNT, CHANNEL_COUNT), (TAPS * CHANNEL_COUNT) ** -0.5, 0.0625),
        "packed_output_gradient": noise(arg_keys[2], (FRAMES_OVERALL, CHANNEL_COUNT, FRAME_PIXELS), 1.0, 6.0, ((0, 8), (1, 4))),
        "clip_length": draw_clip_length(jax.random.fold_in(arg_keys[6], 71), 0),
        "clip_slab_index": draw_clip_slab_index(jax.random.fold_in(arg_keys[6], 71), 0),
        "packed_clip_order": jax.random.permutation(arg_keys[5], CLIP_COUNT).astype(jnp.int32),
    }


def slot_lookup(clip_lengths, slabs, order, slab_number, frame_list):
    clip_ids = jnp.arange(clip_lengths.shape[0], dtype=jnp.int32)
    same_slab = slabs[None, :] == slabs[:, None]
    earlier = clip_ids[None, :] < clip_ids[:, None]
    encoder_offset = lax.optimization_barrier(jnp.sum(jnp.where(same_slab & earlier, clip_lengths[None, :], 0), axis=1)).astype(jnp.int32)
    matches = order[None, :] == clip_ids[:, None]
    placing = lax.optimization_barrier(jnp.sum(jnp.where(matches, clip_ids[None, :], 0), axis=1)).astype(jnp.int32)
    prior_frames = placing[None, :] < placing[:, None]
    packed_start = lax.optimization_barrier(jnp.sum(jnp.where(prior_frames, clip_lengths[None, :], 0), axis=1)).astype(jnp.int32)
    slot_list = jnp.arange(frame_list, dtype=jnp.int32)[:, None]
    within_clip = (slabs[None, :] == slab_number) & (slot_list >= encoder_offset[None, :]) & (slot_list < (encoder_offset + clip_lengths)[None, :])
    filled_slots = jnp.any(within_clip, axis=1)
    frame_lag = lax.optimization_barrier(jnp.sum(jnp.where(within_clip, slot_list - encoder_offset[None, :], 0), axis=1)).astype(jnp.int32)
    incoming_sum = lax.optimization_barrier(jnp.sum(jnp.where(within_clip, packed_start[None, :] + slot_list - encoder_offset[None, :], 0), axis=1)).astype(jnp.int32)
    incoming_row = jnp.where(filled_slots, incoming_sum, -1).astype(jnp.int32)
    return (filled_slots, frame_lag, incoming_row)

def pixel_shift(values, row_step, col_step):
    pixels = PIXEL_ROWS * PIXEL_COLUMNS
    margin = PIXEL_COLUMNS + 1
    padded = jnp.pad(values, ((0, 0), (0, 0), (margin, margin)))
    offset = row_step * PIXEL_COLUMNS + col_step
    moved = padded[:, :, margin + offset:margin + offset + pixels]
    positions = jnp.arange(pixels, dtype=jnp.int32)
    pix_row = positions // PIXEL_COLUMNS + row_step
    pix_col = positions % PIXEL_COLUMNS + col_step
    keep = (pix_row >= 0) & (pix_row < PIXEL_ROWS) & (pix_col >= 0) & (pix_col < PIXEL_COLUMNS)
    return jnp.where(keep[None, None, :], moved, jnp.zeros((), values.dtype))

def tap_stack(grads, filled_slots, frame_lag, time_taps):
    stacked = []
    for time_tap in time_taps:
        delay = 2 - time_tap
        keep = filled_slots & (frame_lag >= delay)
        masked = jnp.where(keep[:, None, None], grads, jnp.zeros((), grads.dtype))
        if delay > 0:
            masked = jnp.concatenate([masked[delay:], jnp.zeros((delay,) + masked.shape[1:], masked.dtype)], axis=0)
        for row_tap in range(3):
            for col_tap in range(3):
                stacked.append(pixel_shift(masked, 1 - row_tap, 1 - col_tap))
    return jnp.stack(stacked, axis=1)

def reference(section_activations, kernel_weight, packed_output_gradient, clip_length, clip_slab_index, packed_clip_order):
    slab_inputs = section_activations.reshape(N_SLAB, SLAB_FRAME_SLOTS, CHANNEL_COUNT, FRAME_PIXELS)
    weight_wide = kernel_weight.astype(jnp.float32)
    gradient_scale = 1.0 / math.sqrt(FRAMES_OVERALL * FRAME_PIXELS)

    def per_slab(operands):
        slab_input, slab_number = operands
        filled_slots, frame_lag, incoming_row = slot_lookup(clip_length, clip_slab_index, packed_clip_order, slab_number, SLAB_FRAME_SLOTS)
        frame_rows = jnp.take(packed_output_gradient, jnp.maximum(incoming_row, 0).astype(jnp.int32), axis=0).astype(jnp.float32)
        out_grad = jnp.where(filled_slots[:, None, None], frame_rows, jnp.zeros((), jnp.float32))
        taps = tap_stack(out_grad, filled_slots, frame_lag, (0, 1, 2))
        input_part = jnp.einsum('tio,gtoq->giq', weight_wide, taps, precision=lax.Precision.HIGHEST)
        weight_part = jnp.einsum('giq,gtoq->tio', slab_input.astype(jnp.float32), taps, precision=lax.Precision.HIGHEST)
        return (input_part.astype(jnp.bfloat16), (weight_part * gradient_scale).astype(jnp.bfloat16))
    grads, weights = lax.map(per_slab, (slab_inputs, jnp.arange(N_SLAB, dtype=jnp.int32)))
    input_grad = grads.reshape(ENC_F, CHANNEL_COUNT, FRAME_PIXELS)
    weight_grad = lax.optimization_barrier(jnp.sum(weights.astype(jnp.float32), axis=0)).astype(jnp.bfloat16)
    return (input_grad, weight_grad)
```

```python
import functools
import math

import jax
import jax.numpy as jnp
from jax import lax
from jax.experimental import pallas as pl
from jax.experimental.pallas import tpu as pltpu
from jax.sharding import PartitionSpec as P

PIXEL_ROWS = 16
PIXEL_COLUMNS = 16
PIXELS = PIXEL_ROWS * PIXEL_COLUMNS
VMEM_BYTES = 44 * 1024 * 1024


def clip_places(clip_lengths, slabs, order):
    clip_ids = jnp.arange(clip_lengths.shape[0], dtype=jnp.int32)
    same_slab = slabs[None, :] == slabs[:, None]
    earlier = clip_ids[None, :] < clip_ids[:, None]
    encoder_offset = jnp.sum(jnp.where(same_slab & earlier, clip_lengths[None, :], 0), axis=1)
    matches = order[None, :] == clip_ids[:, None]
    placing = jnp.sum(jnp.where(matches, clip_ids[None, :], 0), axis=1)
    prior_frames = placing[None, :] < placing[:, None]
    packed_start = jnp.sum(jnp.where(prior_frames, clip_lengths[None, :], 0), axis=1)
    return encoder_offset, packed_start


def slot_lookup(clip_lengths, slabs, encoder_offset, packed_start, slab_number, slots):
    slot_list = jnp.arange(slots, dtype=jnp.int32)[:, None]
    lag = slot_list - encoder_offset[None, :]
    inside = (slabs[None, :] == slab_number) & (lag >= 0) & (lag < clip_lengths[None, :])
    age = jnp.sum(jnp.where(inside, lag + 1, 0), axis=1) - 1
    row = jnp.sum(jnp.where(inside, packed_start[None, :] + lag + 1, 0), axis=1) - 1
    return age, row


def row_ages(clip_lengths, packed_start, rows):
    lag = rows[:, None] - packed_start[None, :]
    inside = (lag >= 0) & (lag < clip_lengths[None, :])
    return jnp.sum(jnp.where(inside, lag + 1, 0), axis=1) - 1


def pixel_taps(frame):
    frame = frame.astype(jnp.float32)
    pixel = lax.broadcasted_iota(jnp.int32, frame.shape, 1)
    row, column = pixel // PIXEL_COLUMNS, pixel % PIXEL_COLUMNS
    taps = []
    for row_tap in range(3):
        for col_tap in range(3):
            row_step, col_step = 1 - row_tap, 1 - col_tap
            offset = row_step * PIXEL_COLUMNS + col_step
            moved = pltpu.roll(frame, (-offset) % PIXELS, 1) if offset else frame
            keep = None
            for place, step, extent in ((row, row_step, PIXEL_ROWS), (column, col_step, PIXEL_COLUMNS)):
                if step:
                    good = (place < extent - 1) if step > 0 else (place > 0)
                    keep = good if keep is None else keep & good
            if keep is not None:
                moved = jnp.where(keep, moved, 0.0)
            taps.append(moved.astype(jnp.bfloat16))
    return taps


def input_kernel(heads, ages, places, weight, *rest):
    windows, (out, taps) = rest[:heads], rest[heads:]
    frames, channels = out.shape[1], weight.shape[1]
    group = channels // heads
    for r in range(frames + 2):
        for k in range(heads):
            for t, tap in enumerate(pixel_taps(windows[k][r])):
                start = pl.multiple_of(t * channels + places[k] * group, 16)
                taps[r, pl.ds(start, group), :] = tap
        f = r - 2
        if f < 0:
            continue
        total = None
        for d in range(3):
            kernel = jnp.concatenate([weight[9 * (2 - d) + t] for t in range(9)], axis=1)
            term = jnp.dot(kernel, taps[f + d], preferred_element_type=jnp.float32)
            if d == 0:
                total = term
            else:
                total = total + jnp.where(ages[f + d] >= d, term, 0.0)
        for g in range(heads):
            out[g, f] = total[g * group : (g + 1) * group, :].astype(jnp.bfloat16)


def input_part(windows, weight, ages, places, channels):
    heads = len(windows)
    frames = windows[0].shape[0] - 2
    group = channels // heads
    smem = pl.BlockSpec(memory_space=pltpu.SMEM)
    vmem = pl.BlockSpec(memory_space=pltpu.VMEM)
    return pl.pallas_call(
        functools.partial(input_kernel, heads),
        out_shape=jax.ShapeDtypeStruct((heads, frames, group, PIXELS), jnp.bfloat16),
        in_specs=[smem, smem, vmem] + [vmem] * heads,
        out_specs=vmem,
        scratch_shapes=[
            pltpu.VMEM((frames + 2, 9 * channels, PIXELS), jnp.bfloat16),
        ],
        compiler_params=pltpu.CompilerParams(vmem_limit_bytes=VMEM_BYTES),
        cost_estimate=pl.CostEstimate(
            flops=2 * frames * 27 * channels * channels * PIXELS,
            bytes_accessed=2 * 27 * channels * channels,
            transcendentals=0,
        ),
        name="input_grad_part",
    )(ages, places, weight, *windows)


def fetch_rows(sources, rows, pieces, target, sems, start):
    def slot(j, carry):
        if start:
            for p, piece in enumerate(pieces):

                @pl.when(sources[j] == p)
                def _():
                    pltpu.make_async_copy(piece.at[rows[j]], target.at[j], sems.at[j]).start()

        else:

            @pl.when(sources[j] >= 0)
            def _():
                pltpu.make_async_copy(pieces[0].at[0], target.at[j], sems.at[j]).wait()

        return carry

    lax.fori_loop(0, target.shape[0], slot, 0)


def weight_kernel(count, chunk, scale, ages, sources, rows, parity, x, *rest):
    pieces, (mine, theirs, grads, taps, total, sems) = rest[:count], rest[count:]
    slots, group = grads.shape[0], grads.shape[1]
    channels = x.shape[1]
    fetch_rows(sources, rows, pieces, grads, sems, True)
    total[...] = jnp.zeros_like(total)
    fetch_rows(sources, rows, pieces, grads, sems, False)

    def blank(j, carry):
        @pl.when(sources[j] < 0)
        def _():
            grads[j] = jnp.zeros(grads.shape[1:], grads.dtype)

        return carry

    lax.fori_loop(0, slots, blank, 0)

    def step(c, carry):
        first = c * chunk

        @pl.when(ages[first] >= 0)
        def _():
            for f in range(chunk):
                for t, tap in enumerate(pixel_taps(grads[first + f])):
                    taps[t * group : (t + 1) * group, f * PIXELS : (f + 1) * PIXELS] = tap
            for d in range(3):
                parts = []
                for f in range(chunk):
                    slot = first + f
                    seen = x[jnp.maximum(slot - d, 0)]
                    parts.append(jnp.where(ages[slot] >= d, seen, jnp.zeros_like(seen)))
                seen = jnp.concatenate(parts, axis=1)
                total[d] += lax.dot_general(
                    seen, taps[...], (((1,), (1,)), ((), ())), preferred_element_type=jnp.float32
                )

        return carry

    lax.fori_loop(0, slots // chunk, step, 0)
    block = channels // count
    for j in range(count // 2):
        for target, side in ((mine, parity[0]), (theirs, 1 - parity[0])):
            start = pl.multiple_of((2 * j + side) * block, 8)
            for d in range(3):
                terms = total[d, pl.ds(start, block), :] * scale
                target[j, 2 - d] = terms.astype(jnp.bfloat16)


def weight_part(pieces, x, ages, sources, rows, parity, scale):
    count = len(pieces)
    slots, channels = x.shape[0], x.shape[1]
    group = pieces[0].shape[1]
    chunk = 4 if slots % 4 == 0 else 1
    smem = pl.BlockSpec(memory_space=pltpu.SMEM)
    vmem = pl.BlockSpec(memory_space=pltpu.VMEM)
    anywhere = pl.BlockSpec(memory_space=pl.ANY)
    half = jax.ShapeDtypeStruct((count // 2, 3, channels // count, 9 * group), jnp.bfloat16)
    return pl.pallas_call(
        functools.partial(weight_kernel, count, chunk, scale),
        out_shape=(half, half),
        in_specs=[smem] * 4 + [vmem] + [anywhere] * count,
        out_specs=(vmem, vmem),
        scratch_shapes=[
            pltpu.VMEM((slots, group, PIXELS), jnp.bfloat16),
            pltpu.VMEM((9 * group, chunk * PIXELS), jnp.bfloat16),
            pltpu.VMEM((3, channels, 9 * group), jnp.float32),
            pltpu.SemaphoreType.DMA((slots,)),
        ],
        compiler_params=pltpu.CompilerParams(vmem_limit_bytes=VMEM_BYTES),
        cost_estimate=pl.CostEstimate(
            flops=2 * slots * 27 * channels * group * PIXELS,
            bytes_accessed=2 * slots * channels * PIXELS,
            transcendentals=0,
        ),
        name="weight_grad_part",
    )(ages, sources, rows, parity, x, *pieces)


def pick_kernel(count, sources, rows, *rest):
    pieces, (out, zero, sems) = rest[:count], rest[count:]
    zero[...] = jnp.zeros_like(zero)
    fetch_rows(sources, rows, pieces, out, sems, True)

    def blank(j, carry):
        @pl.when(sources[j] < 0)
        def _():
            pltpu.make_async_copy(zero, out.at[j], sems.at[j]).start()

        return carry

    def wait(j, carry):
        pltpu.make_async_copy(zero, out.at[j], sems.at[j]).wait()
        return carry

    lax.fori_loop(0, out.shape[0], blank, 0)
    lax.fori_loop(0, out.shape[0], wait, 0)


def pick_rows(pieces, sources, rows):
    slots = rows.shape[0]
    smem = pl.BlockSpec(memory_space=pltpu.SMEM)
    anywhere = pl.BlockSpec(memory_space=pl.ANY)
    frame = pieces[0].shape[1:]
    return pl.pallas_call(
        functools.partial(pick_kernel, len(pieces)),
        out_shape=jax.ShapeDtypeStruct((slots,) + frame, jnp.bfloat16),
        in_specs=[smem] * 2 + [anywhere] * len(pieces),
        out_specs=anywhere,
        scratch_shapes=[pltpu.VMEM(frame, jnp.bfloat16), pltpu.SemaphoreType.DMA((slots,))],
        name="pick_rows",
    )(sources, rows, *pieces)


def partner(axis, flip):
    return [(i, i ^ flip) for i in range(lax.axis_size(axis))]


def spread(piece, count):
    pieces = [piece] + [None] * (count - 1)
    for k in range(2, count, 2):
        pieces[k] = lax.ppermute(piece, "slab", partner("slab", k))
    for k in range(0, count, 2):
        pieces[k + 1] = lax.ppermute(pieces[k], "slab", partner("slab", 1))
    return pieces


def shards(
    section_activations,
    kernel_weight,
    packed_output_gradient,
    clip_length,
    clip_slab_index,
    packed_clip_order,
):
    slots, channels = section_activations.shape[:2]
    rows, group = packed_output_gradient.shape[:2]
    count, heads = lax.axis_size("slab"), lax.axis_size("head")
    me, head = lax.axis_index("slab"), lax.axis_index("head")
    each = rows // heads

    after = lax.ppermute(
        packed_output_gradient[:2], "slab", [(i, (i - 1) % count) for i in range(count)]
    )
    longer = jnp.concatenate([packed_output_gradient, after], axis=0)
    windows = []
    for k in range(heads):
        window = lax.dynamic_slice_in_dim(longer, each * (head ^ k), each + 2, 0)
        windows.append(lax.ppermute(window, "head", partner("head", k)) if k else window)
    gradient_pieces = spread(packed_output_gradient, count)

    encoder_offset, packed_start = clip_places(clip_length, clip_slab_index, packed_clip_order)
    slot_age, slot_row = slot_lookup(
        clip_length, clip_slab_index, encoder_offset, packed_start, me, slots
    )
    source = jnp.where(slot_row >= 0, (slot_row // rows) ^ me, -1)
    inner = jnp.maximum(slot_row, 0) % rows
    window_rows = rows * me + each * head + jnp.arange(each + 2, dtype=jnp.int32)
    window_age = row_ages(clip_length, packed_start, window_rows)
    places = head ^ jnp.arange(heads, dtype=jnp.int32)

    parts = input_part(windows, kernel_weight, window_age, places, channels)
    arrived = []
    for k in range(heads):
        part = lax.dynamic_index_in_dim(parts, head ^ k, 0, keepdims=False)
        arrived.append(lax.ppermute(part, "head", partner("head", k)) if k else part)
    input_pieces = spread(jnp.concatenate(arrived, axis=0), count)

    scale = 1.0 / math.sqrt(rows * count * PIXELS)
    mine, theirs = weight_part(
        gradient_pieces,
        section_activations,
        slot_age,
        source,
        inner,
        (me % 2).reshape((1,)).astype(jnp.int32),
        scale,
    )
    other = lax.ppermute(theirs, "slab", partner("slab", 1))
    pair = mine.astype(jnp.float32) + other.astype(jnp.float32)
    rounded = pair.astype(jnp.bfloat16)
    chip = me // 2
    weight_grad = lax.dynamic_index_in_dim(pair, chip, 0, keepdims=False)
    for k in range(1, count // 2):
        term = lax.dynamic_index_in_dim(rounded, chip ^ k, 0, keepdims=False)
        term = lax.ppermute(term, "slab", partner("slab", 2 * k))
        weight_grad = weight_grad + term.astype(jnp.float32)
    block = channels // count
    weight_grad = weight_grad.astype(jnp.bfloat16).reshape(3, block, 9, group)
    weight_grad = weight_grad.transpose(0, 2, 1, 3).reshape(27, block, group)

    place = (inner // each) ^ head
    input_grad = pick_rows(input_pieces, source, place * each + inner % each)
    return (input_grad, weight_grad)


def solution(mesh):
    return jax.shard_map(
        shards,
        mesh=mesh,
        in_specs=(P("slab", None, None), P(), P("slab", "head", None), P(), P(), P()),
        out_specs=(P("slab", "head", None), P(None, "slab", "head")),
        check_vma=False,
    )
```

```python
import functools
import math

import jax
import jax.numpy as jnp
from jax import lax
from jax.experimental import pallas as pl
from jax.experimental.pallas import tpu as pltpu
from jax.sharding import PartitionSpec as P

PIXEL_ROWS = 16
PIXEL_COLUMNS = 16
PIXELS = PIXEL_ROWS * PIXEL_COLUMNS
VMEM_BYTES = 44 * 1024 * 1024


def clip_places(clip_lengths, slabs, order):
    clip_ids = jnp.arange(clip_lengths.shape[0], dtype=jnp.int32)
    same_slab = slabs[None, :] == slabs[:, None]
    earlier = clip_ids[None, :] < clip_ids[:, None]
    encoder_offset = jnp.sum(jnp.where(same_slab & earlier, clip_lengths[None, :], 0), axis=1)
    matches = order[None, :] == clip_ids[:, None]
    placing = jnp.sum(jnp.where(matches, clip_ids[None, :], 0), axis=1)
    prior_frames = placing[None, :] < placing[:, None]
    packed_start = jnp.sum(jnp.where(prior_frames, clip_lengths[None, :], 0), axis=1)
    return encoder_offset, packed_start


def slot_lookup(clip_lengths, slabs, encoder_offset, packed_start, slab_number, slots):
    slot_list = jnp.arange(slots, dtype=jnp.int32)[:, None]
    lag = slot_list - encoder_offset[None, :]
    inside = (slabs[None, :] == slab_number) & (lag >= 0) & (lag < clip_lengths[None, :])
    age = jnp.sum(jnp.where(inside, lag + 1, 0), axis=1) - 1
    row = jnp.sum(jnp.where(inside, packed_start[None, :] + lag + 1, 0), axis=1) - 1
    return age, row


def row_ages(clip_lengths, packed_start, rows):
    lag = rows[:, None] - packed_start[None, :]
    inside = (lag >= 0) & (lag < clip_lengths[None, :])
    return jnp.sum(jnp.where(inside, lag + 1, 0), axis=1) - 1


def pixel_taps(frame):
    frame = frame.astype(jnp.float32)
    pixel = lax.broadcasted_iota(jnp.int32, frame.shape, 1)
    row, column = pixel // PIXEL_COLUMNS, pixel % PIXEL_COLUMNS
    taps = []
    for row_tap in range(3):
        for col_tap in range(3):
            row_step, col_step = 1 - row_tap, 1 - col_tap
            offset = row_step * PIXEL_COLUMNS + col_step
            moved = pltpu.roll(frame, (-offset) % PIXELS, 1) if offset else frame
            keep = None
            for place, step, extent in ((row, row_step, PIXEL_ROWS), (column, col_step, PIXEL_COLUMNS)):
                if step:
                    good = (place < extent - 1) if step > 0 else (place > 0)
                    keep = good if keep is None else keep & good
            if keep is not None:
                moved = jnp.where(keep, moved, 0.0)
            taps.append(moved.astype(jnp.bfloat16))
    return taps


def input_kernel(heads, ages, weight, *rest):
    own, halo, out, taps = rest
    frames, channels = out.shape[1], weight.shape[1]
    group = channels // heads
    for r in range(frames + 2):
        for k in range(heads):
            frame = own[k, r] if r < frames else halo[k, r - frames]
            for t, tap in enumerate(pixel_taps(frame)):
                start = t * channels + k * group
                taps[r, start : start + group, :] = tap
        f = r - 2
        if f < 0:
            continue
        total = None
        for d in range(3):
            kernel = jnp.concatenate([weight[9 * (2 - d) + t] for t in range(9)], axis=1)
            term = jnp.dot(kernel, taps[f + d], preferred_element_type=jnp.float32)
            if d == 0:
                total = term
            else:
                total = total + jnp.where(ages[f + d] >= d, term, 0.0)
        for g in range(heads):
            out[g, f] = total[g * group : (g + 1) * group, :].astype(jnp.bfloat16)


def input_part(own, halo, weight, ages):
    heads, frames, group = own.shape[:3]
    channels = weight.shape[1]
    smem = pl.BlockSpec(memory_space=pltpu.SMEM)
    vmem = pl.BlockSpec(memory_space=pltpu.VMEM)
    return pl.pallas_call(
        functools.partial(input_kernel, heads),
        out_shape=jax.ShapeDtypeStruct((heads, frames, group, PIXELS), jnp.bfloat16),
        in_specs=[smem, vmem, vmem, vmem],
        out_specs=vmem,
        scratch_shapes=[
            pltpu.VMEM((frames + 2, 9 * channels, PIXELS), jnp.bfloat16),
        ],
        compiler_params=pltpu.CompilerParams(vmem_limit_bytes=VMEM_BYTES),
        cost_estimate=pl.CostEstimate(
            flops=2 * frames * 27 * channels * channels * PIXELS,
            bytes_accessed=2 * 27 * channels * channels,
            transcendentals=0,
        ),
        name="input_grad_part",
    )(ages, weight, own, halo)


def fetch_rows(sources, rows, pieces, target, sems, start, first=0):
    def slot(j, carry):
        if start:
            for p, piece in enumerate(pieces):

                @pl.when(sources[j] == p)
                def _():
                    row = piece.at[rows[j], first : first + target.shape[1]]
                    pltpu.make_async_copy(row, target.at[j], sems.at[j]).start()

        else:

            @pl.when(sources[j] >= 0)
            def _():
                row = pieces[0].at[0, first : first + target.shape[1]]
                pltpu.make_async_copy(row, target.at[j], sems.at[j]).wait()

        return carry

    lax.fori_loop(0, target.shape[0], slot, 0)


def blank_rows(sources, target):
    def slot(j, carry):
        @pl.when(sources[j] < 0)
        def _():
            target[j] = jnp.zeros(target.shape[1:], target.dtype)

        return carry

    lax.fori_loop(0, target.shape[0], slot, 0)


def weight_kernel(count, chunk, scale, half, ages, sources, rows, parity, x, *rest):
    pieces, (mine, theirs, grads, taps, total, sems) = rest[:2], rest[2:]
    slots, group = grads.shape[0], grads.shape[1]
    channels = x.shape[1]
    fetch_rows(sources, rows, pieces, grads, sems, True, half * group)
    total[...] = jnp.zeros_like(total)
    fetch_rows(sources, rows, pieces, grads, sems, False, half * group)
    blank_rows(sources, grads)

    def step(c, carry):
        first = c * chunk

        @pl.when(ages[first] >= 0)
        def _():
            for f in range(chunk):
                for t, tap in enumerate(pixel_taps(grads[first + f])):
                    taps[t * group : (t + 1) * group, f * PIXELS : (f + 1) * PIXELS] = tap
            for d in range(3):
                parts = []
                for f in range(chunk):
                    slot = first + f
                    seen = x[jnp.maximum(slot - d, 0)]
                    parts.append(jnp.where(ages[slot] >= d, seen, jnp.zeros_like(seen)))
                seen = jnp.concatenate(parts, axis=1)
                total[d] += lax.dot_general(
                    seen, taps[...], (((1,), (1,)), ((), ())), preferred_element_type=jnp.float32
                )

        return carry

    lax.fori_loop(0, slots // chunk, step, 0)
    block = channels // count
    for j in range(count // 2):
        for target, side in ((mine, parity[0]), (theirs, 1 - parity[0])):
            start = pl.multiple_of((2 * j + side) * block, 8)
            for d in range(3):
                terms = total[d, pl.ds(start, block), :] * scale
                target[j, 2 - d] = terms.astype(jnp.bfloat16)


def weight_part(half, pieces, x, ages, sources, rows, parity, scale, count):
    slots, channels = x.shape[0], x.shape[1]
    group = pieces[0].shape[1] // 2
    chunk = 4 if slots % 4 == 0 else 1
    smem = pl.BlockSpec(memory_space=pltpu.SMEM)
    vmem = pl.BlockSpec(memory_space=pltpu.VMEM)
    anywhere = pl.BlockSpec(memory_space=pl.ANY)
    blocks = jax.ShapeDtypeStruct((count // 2, 3, channels // count, 9 * group), jnp.bfloat16)
    return pl.pallas_call(
        functools.partial(weight_kernel, count, chunk, scale, half),
        out_shape=(blocks, blocks),
        in_specs=[smem] * 4 + [vmem] + [anywhere] * 2,
        out_specs=(vmem, vmem),
        scratch_shapes=[
            pltpu.VMEM((slots, group, PIXELS), jnp.bfloat16),
            pltpu.VMEM((9 * group, chunk * PIXELS), jnp.bfloat16),
            pltpu.VMEM((3, channels, 9 * group), jnp.float32),
            pltpu.SemaphoreType.DMA((slots,)),
        ],
        compiler_params=pltpu.CompilerParams(vmem_limit_bytes=VMEM_BYTES),
        cost_estimate=pl.CostEstimate(
            flops=2 * slots * 27 * channels * group * PIXELS,
            bytes_accessed=2 * slots * channels * PIXELS,
            transcendentals=0,
        ),
        name="weight_grad_part",
    )(ages, sources, rows, parity, x, *pieces)


def pick_kernel(count, sources, rows, *rest):
    pieces, (out, sems) = rest[:count], rest[count:]
    fetch_rows(sources, rows, pieces, out, sems, True)
    blank_rows(sources, out)
    fetch_rows(sources, rows, pieces, out, sems, False)


def pick_rows(pieces, sources, rows):
    slots = rows.shape[0]
    smem = pl.BlockSpec(memory_space=pltpu.SMEM)
    anywhere = pl.BlockSpec(memory_space=pl.ANY)
    frame = pieces[0].shape[1:]
    return pl.pallas_call(
        functools.partial(pick_kernel, len(pieces)),
        out_shape=jax.ShapeDtypeStruct((slots,) + frame, jnp.bfloat16),
        in_specs=[smem] * 2 + [anywhere] * len(pieces),
        out_specs=pl.BlockSpec(memory_space=pltpu.VMEM),
        scratch_shapes=[pltpu.SemaphoreType.DMA((slots,))],
        compiler_params=pltpu.CompilerParams(vmem_limit_bytes=VMEM_BYTES),
        name="pick_rows",
    )(sources, rows, *pieces)


def same_core(count):
    return [[2 * chip + core for chip in range(count // 2)] for core in range(2)]


def sibling(value, count):
    return lax.ppermute(value, "slab", [(i, i ^ 1) for i in range(count)])


def spread(piece, count):
    near = lax.all_gather(piece, "slab", axis=0, tiled=True, axis_index_groups=same_core(count))
    return [near, sibling(near, count)]


def shards(
    section_activations,
    kernel_weight,
    packed_output_gradient,
    clip_length,
    clip_slab_index,
    packed_clip_order,
):
    slots, channels = section_activations.shape[:2]
    rows, group = packed_output_gradient.shape[:2]
    count, heads = lax.axis_size("slab"), lax.axis_size("head")
    me, head = lax.axis_index("slab"), lax.axis_index("head")
    each = rows // heads

    after = lax.ppermute(
        packed_output_gradient[:2], "slab", [(i, (i - 1) % count) for i in range(count)]
    )
    frame = packed_output_gradient.shape[1:]
    own = packed_output_gradient.reshape((heads, each) + frame)
    own_all = lax.all_to_all(own, "head", 0, 0)
    halo = jnp.concatenate([own[1:, :2], after[None]], axis=0)
    halo_all = lax.all_to_all(halo, "head", 0, 0)
    gradient_pieces = spread(packed_output_gradient, count)

    encoder_offset, packed_start = clip_places(clip_length, clip_slab_index, packed_clip_order)
    slot_age, slot_row = slot_lookup(
        clip_length, clip_slab_index, encoder_offset, packed_start, me, slots
    )
    parity = (me % 2).reshape((1,)).astype(jnp.int32)
    shard, inner = slot_row // rows, slot_row % rows
    source = jnp.where(slot_row >= 0, (shard ^ me) % 2, -1)
    inner = (shard // 2) * rows + inner
    window_rows = rows * me + each * head + jnp.arange(each + 2, dtype=jnp.int32)
    window_age = row_ages(clip_length, packed_start, window_rows)

    parts = input_part(own_all, halo_all, kernel_weight, window_age)
    x, parts = lax.optimization_barrier((section_activations, parts))
    arrived = lax.all_to_all(parts, "head", 0, 0)

    scale = 1.0 / math.sqrt(rows * count * PIXELS)
    scattered = []
    for half in range(2):
        if half:
            x, arrived = lax.optimization_barrier((x, arrived))
            input_pieces = spread(arrived.reshape((rows,) + frame), count)
        mine, theirs = weight_part(
            half, gradient_pieces, x, slot_age, source, inner, parity, scale, count
        )
        pair = mine.astype(jnp.float32) + sibling(theirs, count).astype(jnp.float32)
        terms = lax.all_to_all(
            pair.astype(jnp.bfloat16), "slab", 0, 0, axis_index_groups=same_core(count)
        )
        summed = jnp.sum(terms.astype(jnp.float32), axis=0)
        scattered.append(summed.astype(jnp.bfloat16))
    block = channels // count
    weight_grad = jnp.concatenate(
        [part.reshape(3, block, 9, group // 2) for part in scattered], axis=3
    )
    weight_grad = weight_grad.transpose(0, 2, 1, 3).reshape(27, block, group)

    input_grad = pick_rows(input_pieces, source, inner)
    return (input_grad, weight_grad)


def solution(mesh):
    return jax.shard_map(
        shards,
        mesh=mesh,
        in_specs=(P("slab", None, None), P(), P("slab", "head", None), P(), P(), P()),
        out_specs=(P("slab", "head", None), P(None, "slab", "head")),
        check_vma=False,
    )
```

```python
import functools
import math

import jax
import jax.numpy as jnp
import numpy as np
from jax import lax
from jax.experimental import pallas as pl
from jax.experimental.pallas import tpu as pltpu
from jax.sharding import PartitionSpec as P

PIXEL_ROWS = 16
PIXEL_COLUMNS = 16
PIXELS = PIXEL_ROWS * PIXEL_COLUMNS
VMEM_BYTES = 44 * 1024 * 1024


def clip_places(clip_lengths, slabs, order):
    clip_ids = jnp.arange(clip_lengths.shape[0], dtype=jnp.int32)
    same_slab = slabs[None, :] == slabs[:, None]
    earlier = clip_ids[None, :] < clip_ids[:, None]
    encoder_offset = jnp.sum(jnp.where(same_slab & earlier, clip_lengths[None, :], 0), axis=1)
    matches = order[None, :] == clip_ids[:, None]
    placing = jnp.sum(jnp.where(matches, clip_ids[None, :], 0), axis=1)
    prior_frames = placing[None, :] < placing[:, None]
    packed_start = jnp.sum(jnp.where(prior_frames, clip_lengths[None, :], 0), axis=1)
    return encoder_offset, packed_start


def slot_lookup(clip_lengths, slabs, encoder_offset, packed_start, slab_number, slots):
    slot_list = jnp.arange(slots, dtype=jnp.int32)[:, None]
    lag = slot_list - encoder_offset[None, :]
    inside = (slabs[None, :] == slab_number) & (lag >= 0) & (lag < clip_lengths[None, :])
    age = jnp.sum(jnp.where(inside, lag + 1, 0), axis=1) - 1
    row = jnp.sum(jnp.where(inside, packed_start[None, :] + lag + 1, 0), axis=1) - 1
    return age, row


def row_ages(clip_lengths, packed_start, rows):
    lag = rows[:, None] - packed_start[None, :]
    inside = (lag >= 0) & (lag < clip_lengths[None, :])
    return jnp.sum(jnp.where(inside, lag + 1, 0), axis=1) - 1


def tap_offsets():
    return [(1 - row_tap, 1 - col_tap) for row_tap in range(3) for col_tap in range(3)]


def tap_masks():
    row, column = np.divmod(np.arange(PIXELS), PIXEL_COLUMNS)
    masks = []
    for row_step, col_step in tap_offsets():
        good = (0 <= row + row_step) & (row + row_step < PIXEL_ROWS)
        good &= (0 <= column + col_step) & (column + col_step < PIXEL_COLUMNS)
        masks.append(np.broadcast_to(good, (16, PIXELS)))
    return jnp.asarray(np.stack(masks), jnp.bfloat16)


def pixel_taps(frame, masks):
    taps = []
    for t, (row_step, col_step) in enumerate(tap_offsets()):
        offset = row_step * PIXEL_COLUMNS + col_step
        if offset:
            moved = pltpu.roll(frame, (-offset) % PIXELS, 1).reshape(-1, 16, PIXELS)
            taps.append((moved * masks[t][None]).reshape(frame.shape))
        else:
            taps.append(frame)
    return taps


def input_kernel(ages, masks, weight, windows, out, taps, kernels, sems):
    heads, frames, group = out.shape[:3]
    channels = heads * group

    def fetch(kt):
        return pltpu.make_async_copy(weight.at[pl.ds(9 * kt, 9)], kernels.at[kt], sems.at[kt])

    for kt in range(3):
        fetch(kt).start()
    for r in range(frames + 2):
        for g in range(heads):
            for t, tap in enumerate(pixel_taps(windows[g, r], masks)):
                start = t * channels + g * group
                taps[r, start : start + group, :] = tap
        f = r - 2
        if f < 0:
            continue
        if f == 0:
            for kt in range(3):
                fetch(kt).wait()
        total = None
        for d in range(3):
            kernel = jnp.concatenate([kernels[2 - d, t] for t in range(9)], axis=1)
            term = jnp.dot(kernel, taps[f + d], preferred_element_type=jnp.float32)
            if d == 0:
                total = term
            else:
                total = total + jnp.where(ages[f + d] >= d, term, 0.0)
        for g in range(heads):
            out[g, f] = total[g * group : (g + 1) * group, :].astype(jnp.bfloat16)


def input_part(windows, weight, ages):
    heads, frames, group = windows.shape[:3]
    frames -= 2
    channels = weight.shape[1]
    smem = pl.BlockSpec(memory_space=pltpu.SMEM)
    vmem = pl.BlockSpec(memory_space=pltpu.VMEM)
    anywhere = pl.BlockSpec(memory_space=pl.ANY)
    return pl.pallas_call(
        input_kernel,
        out_shape=jax.ShapeDtypeStruct((heads, frames, group, PIXELS), jnp.bfloat16),
        in_specs=[smem, vmem, anywhere, vmem],
        out_specs=vmem,
        scratch_shapes=[
            pltpu.VMEM((frames + 2, 9 * channels, PIXELS), jnp.bfloat16),
            pltpu.VMEM((3, 9, channels, channels), jnp.bfloat16),
            pltpu.SemaphoreType.DMA((3,)),
        ],
        compiler_params=pltpu.CompilerParams(vmem_limit_bytes=VMEM_BYTES),
        cost_estimate=pl.CostEstimate(
            flops=2 * frames * 27 * channels * channels * PIXELS,
            bytes_accessed=2 * 27 * channels * channels,
            transcendentals=0,
        ),
        name="input_grad_part",
    )(ages, tap_masks(), weight, windows)


def fetch_rows(sources, rows, pieces, target, sems, start):
    def slot(j, carry):
        if start:
            for p, piece in enumerate(pieces):

                @pl.when(sources[j] == p)
                def _():
                    pltpu.make_async_copy(piece.at[rows[j]], target.at[j], sems.at[j]).start()

        else:

            @pl.when(sources[j] >= 0)
            def _():
                pltpu.make_async_copy(pieces[0].at[0], target.at[j], sems.at[j]).wait()

        return carry

    lax.fori_loop(0, target.shape[0], slot, 0)


def blank_rows(sources, target):
    def slot(j, carry):
        @pl.when(sources[j] < 0)
        def _():
            target[j] = jnp.zeros(target.shape[1:], target.dtype)

        return carry

    lax.fori_loop(0, target.shape[0], slot, 0)


def weight_kernel(chunk, scale, ages, sources, rows, parity, steps, masks, x, near, far, *rest):
    mine, theirs, seen, grads, even, odd, total, sems, seen_sem = rest
    slots, group = grads.shape[0], grads.shape[1]
    channels = x.shape[1]
    fetch_seen = pltpu.make_async_copy(x, seen, seen_sem)
    fetch_seen.start()
    fetch_rows(sources, rows, (near, far), grads, sems, True)
    total[...] = jnp.zeros_like(total)
    blank_rows(sources, grads)
    fetch_rows(sources, rows, (near, far), grads, sems, False)
    fetch_seen.wait()

    def build(first, taps):
        for f in range(chunk):
            frame = grads[jnp.minimum(first + f, slots - 1)]
            for t, tap in enumerate(pixel_taps(frame, masks)):
                taps[t * group : (t + 1) * group, f * PIXELS : (f + 1) * PIXELS] = tap

    def multiply(first, taps):
        parts = []
        for d in range(3):
            row = []
            for f in range(chunk):
                slot = first + f
                frame = seen[jnp.clip(slot - d, 0, slots - 1)]
                row.append(jnp.where(ages[slot] >= d, frame, jnp.zeros_like(frame)))
            parts.append(jnp.concatenate(row, axis=1))
        for d in range(3):
            total[d] += lax.dot_general(
                parts[d], taps[...], (((1,), (1,)), ((), ())), preferred_element_type=jnp.float32
            )

    build(0, even)

    def step(p, carry):
        first = 2 * p * chunk
        build(first + chunk, odd)
        multiply(first, even)
        build(first + 2 * chunk, even)
        multiply(first + chunk, odd)
        return carry

    lax.fori_loop(0, steps[0], step, 0)
    half, block = mine.shape[0], mine.shape[2]
    for j in range(half):
        for target, side in ((mine, parity[0]), (theirs, 1 - parity[0])):
            start = pl.multiple_of((2 * j + side) * block, 8)
            for d in range(3):
                terms = total[d, pl.ds(start, block), :] * scale
                target[j, 2 - d] = terms.astype(jnp.bfloat16)


def weight_part(near, far, x, ages, sources, rows, parity, scale, count):
    slots, channels = x.shape[0], x.shape[1]
    group = near.shape[1]
    chunk = 2
    filled = jnp.sum((ages >= 0).astype(jnp.int32))
    steps = ((filled + 2 * chunk - 1) // (2 * chunk)).reshape((1,))
    ages = jnp.concatenate([ages, jnp.full((2 * chunk,), -1, jnp.int32)])
    smem = pl.BlockSpec(memory_space=pltpu.SMEM)
    vmem = pl.BlockSpec(memory_space=pltpu.VMEM)
    anywhere = pl.BlockSpec(memory_space=pl.ANY)
    blocks = jax.ShapeDtypeStruct((count // 2, 3, channels // count, 9 * group), jnp.bfloat16)
    tap_buffer = pltpu.VMEM((9 * group, chunk * PIXELS), jnp.bfloat16)
    return pl.pallas_call(
        functools.partial(weight_kernel, chunk, scale),
        out_shape=(blocks, blocks),
        in_specs=[smem] * 5 + [vmem] + [anywhere] * 3,
        out_specs=(vmem, vmem),
        scratch_shapes=[
            pltpu.VMEM(x.shape, jnp.bfloat16),
            pltpu.VMEM((slots, group, PIXELS), jnp.bfloat16),
            tap_buffer,
            tap_buffer,
            pltpu.VMEM((3, channels, 9 * group), jnp.float32),
            pltpu.SemaphoreType.DMA((slots,)),
            pltpu.SemaphoreType.DMA,
        ],
        compiler_params=pltpu.CompilerParams(vmem_limit_bytes=VMEM_BYTES),
        cost_estimate=pl.CostEstimate(
            flops=2 * slots * 27 * channels * group * PIXELS,
            bytes_accessed=2 * slots * channels * PIXELS,
            transcendentals=0,
        ),
        name="weight_grad_part",
    )(ages, sources, rows, parity, steps, tap_masks(), x, near, far)


def pick_kernel(count, sources, rows, *rest):
    pieces, (out, sems) = rest[:count], rest[count:]
    fetch_rows(sources, rows, pieces, out, sems, True)
    blank_rows(sources, out)
    fetch_rows(sources, rows, pieces, out, sems, False)


def pick_rows(pieces, sources, rows):
    slots = rows.shape[0]
    smem = pl.BlockSpec(memory_space=pltpu.SMEM)
    anywhere = pl.BlockSpec(memory_space=pl.ANY)
    frame = pieces[0].shape[1:]
    return pl.pallas_call(
        functools.partial(pick_kernel, len(pieces)),
        out_shape=jax.ShapeDtypeStruct((slots,) + frame, jnp.bfloat16),
        in_specs=[smem] * 2 + [anywhere] * len(pieces),
        out_specs=pl.BlockSpec(memory_space=pltpu.VMEM),
        scratch_shapes=[pltpu.SemaphoreType.DMA((slots,))],
        compiler_params=pltpu.CompilerParams(vmem_limit_bytes=VMEM_BYTES),
        name="pick_rows",
    )(sources, rows, *pieces)


def swap(value, axis, flip):
    return lax.ppermute(value, axis, [(i, i ^ flip) for i in range(lax.axis_size(axis))])


def spread(piece, count):
    chips = [piece] + [swap(piece, "slab", k) for k in range(2, count, 2)]
    near = jnp.concatenate(chips, axis=0)
    return near, swap(near, "slab", 1)


def shards(
    section_activations,
    kernel_weight,
    packed_output_gradient,
    clip_length,
    clip_slab_index,
    packed_clip_order,
):
    slots, channels = section_activations.shape[:2]
    rows, group = packed_output_gradient.shape[:2]
    count, heads = lax.axis_size("slab"), lax.axis_size("head")
    me, head = lax.axis_index("slab"), lax.axis_index("head")
    each, frame = rows // heads, packed_output_gradient.shape[1:]

    after = lax.ppermute(
        packed_output_gradient[:2], "slab", [(i, (i - 1) % count) for i in range(count)]
    )
    piece, after = lax.optimization_barrier((packed_output_gradient, after))
    longer = jnp.concatenate([piece, after], axis=0)
    windows = jnp.stack([longer[each * h : each * h + each + 2] for h in range(heads)])
    windows = lax.all_to_all(windows, "head", 0, 0)
    near, far = spread(piece, count)

    encoder_offset, packed_start = clip_places(clip_length, clip_slab_index, packed_clip_order)
    slot_age, slot_row = slot_lookup(
        clip_length, clip_slab_index, encoder_offset, packed_start, me, slots
    )
    parity = (me % 2).reshape((1,)).astype(jnp.int32)
    shard, inner = jnp.maximum(slot_row, 0) // rows, jnp.maximum(slot_row, 0) % rows
    side, chip = (shard ^ me) % 2, (shard // 2) ^ (me // 2)
    source = jnp.where(slot_row >= 0, side, -1)
    window_rows = rows * me + each * head + jnp.arange(each + 2, dtype=jnp.int32)
    window_age = row_ages(clip_length, packed_start, window_rows)

    parts = input_part(windows, kernel_weight, window_age)
    x, parts = lax.optimization_barrier((section_activations, parts))
    arrived = []
    for k in range(heads):
        part = lax.dynamic_index_in_dim(parts, head ^ k, 0, keepdims=False)
        arrived.append(swap(part, "head", k) if k else part)
    stages = 2
    width = heads // stages
    input_pieces = []
    for stage in range(stages):
        piece = jnp.concatenate(arrived[stage * width : (stage + 1) * width], axis=0)
        if stage == 0:
            x, piece = lax.optimization_barrier((x, piece))
        input_pieces += spread(piece, count)

    scale = 1.0 / math.sqrt(rows * count * PIXELS)
    mine, theirs = weight_part(
        near, far, x, slot_age, source, chip * rows + inner, parity, scale, count
    )
    pair = mine.astype(jnp.float32) + swap(theirs, "slab", 1).astype(jnp.float32)
    rounded = pair.astype(jnp.bfloat16)
    my_chip = me // 2
    weight_grad = lax.dynamic_index_in_dim(pair, my_chip, 0, keepdims=False)
    for k in range(1, count // 2):
        term = lax.dynamic_index_in_dim(rounded, my_chip ^ k, 0, keepdims=False)
        weight_grad = weight_grad + swap(term, "slab", 2 * k).astype(jnp.float32)
    block = channels // count
    weight_grad = weight_grad.astype(jnp.bfloat16).reshape(3, block, 9, group)
    weight_grad = weight_grad.transpose(0, 2, 1, 3).reshape(27, block, group)

    place = (inner // each) ^ head
    stage, place = place // width, place % width
    input_source = jnp.where(slot_row >= 0, 2 * stage + side, -1)
    input_row = (chip * width + place) * each + inner % each
    input_grad = pick_rows(input_pieces, input_source, input_row)
    return (input_grad, weight_grad)


def solution(mesh):
    return jax.shard_map(
        shards,
        mesh=mesh,
        in_specs=(P("slab", None, None), P(), P("slab", "head", None), P(), P(), P()),
        out_specs=(P("slab", "head", None), P(None, "slab", "head")),
        check_vma=False,
    )
```

```python
import functools
import math

import jax
import jax.numpy as jnp
import numpy as np
from jax import lax
from jax.experimental import pallas as pl
from jax.experimental.pallas import tpu as pltpu
from jax.sharding import PartitionSpec as P

PIXEL_ROWS = 16
PIXEL_COLUMNS = 16
PIXELS = PIXEL_ROWS * PIXEL_COLUMNS
VMEM_BYTES = 58 * 1024 * 1024


def clip_places(clip_lengths, slabs, order):
    clip_ids = jnp.arange(clip_lengths.shape[0], dtype=jnp.int32)
    same_slab = slabs[None, :] == slabs[:, None]
    earlier = clip_ids[None, :] < clip_ids[:, None]
    encoder_offset = jnp.sum(jnp.where(same_slab & earlier, clip_lengths[None, :], 0), axis=1)
    matches = order[None, :] == clip_ids[:, None]
    placing = jnp.sum(jnp.where(matches, clip_ids[None, :], 0), axis=1)
    prior_frames = placing[None, :] < placing[:, None]
    packed_start = jnp.sum(jnp.where(prior_frames, clip_lengths[None, :], 0), axis=1)
    return encoder_offset, packed_start


def slot_lookup(clip_lengths, slabs, encoder_offset, packed_start, slab_number, slots):
    slot_list = jnp.arange(slots, dtype=jnp.int32)[:, None]
    lag = slot_list - encoder_offset[None, :]
    inside = (slabs[None, :] == slab_number) & (lag >= 0) & (lag < clip_lengths[None, :])
    age = jnp.sum(jnp.where(inside, lag + 1, 0), axis=1) - 1
    row = jnp.sum(jnp.where(inside, packed_start[None, :] + lag + 1, 0), axis=1) - 1
    return age, row


def row_ages(clip_lengths, packed_start, rows):
    lag = rows[:, None] - packed_start[None, :]
    inside = (lag >= 0) & (lag < clip_lengths[None, :])
    return jnp.sum(jnp.where(inside, lag + 1, 0), axis=1) - 1


def tap_offsets():
    return [(1 - row_tap, 1 - col_tap) for row_tap in range(3) for col_tap in range(3)]


def tap_masks():
    row, column = np.divmod(np.arange(PIXELS), PIXEL_COLUMNS)
    masks = []
    for row_step, col_step in tap_offsets():
        good = (0 <= row + row_step) & (row + row_step < PIXEL_ROWS)
        good &= (0 <= column + col_step) & (column + col_step < PIXEL_COLUMNS)
        masks.append(np.broadcast_to(good, (16, PIXELS)))
    return jnp.asarray(np.stack(masks), jnp.bfloat16)


def pixel_taps(frame, masks):
    taps = []
    for t, (row_step, col_step) in enumerate(tap_offsets()):
        offset = row_step * PIXEL_COLUMNS + col_step
        if offset:
            moved = pltpu.roll(frame, (-offset) % PIXELS, 1).reshape(-1, 16, PIXELS)
            taps.append((moved * masks[t][None]).reshape(frame.shape))
        else:
            taps.append(frame)
    return taps


def input_kernel(ages, masks, weight, windows, out, taps, kernels, sems):
    heads, frames, group = out.shape[:3]
    channels = heads * group

    def fetch(kt):
        return pltpu.make_async_copy(weight.at[pl.ds(9 * kt, 9)], kernels.at[kt], sems.at[kt])

    for kt in range(3):
        fetch(kt).start()
    for r in range(frames + 2):
        for g in range(heads):
            for t, tap in enumerate(pixel_taps(windows[g, r], masks)):
                start = t * channels + g * group
                taps[r, start : start + group, :] = tap
        f = r - 2
        if f < 0:
            continue
        if f == 0:
            for kt in range(3):
                fetch(kt).wait()
        total = None
        for d in range(3):
            kernel = jnp.concatenate([kernels[2 - d, t] for t in range(9)], axis=1)
            term = jnp.dot(kernel, taps[f + d], preferred_element_type=jnp.float32)
            if d == 0:
                total = term
            else:
                total = total + jnp.where(ages[f + d] >= d, term, 0.0)
        for g in range(heads):
            out[g, f] = total[g * group : (g + 1) * group, :].astype(jnp.bfloat16)


def input_part(windows, weight, ages):
    heads, frames, group = windows.shape[:3]
    frames -= 2
    channels = weight.shape[1]
    smem = pl.BlockSpec(memory_space=pltpu.SMEM)
    vmem = pl.BlockSpec(memory_space=pltpu.VMEM)
    anywhere = pl.BlockSpec(memory_space=pl.ANY)
    return pl.pallas_call(
        input_kernel,
        out_shape=jax.ShapeDtypeStruct((heads, frames, group, PIXELS), jnp.bfloat16),
        in_specs=[smem, vmem, anywhere, vmem],
        out_specs=vmem,
        scratch_shapes=[
            pltpu.VMEM((frames + 2, 9 * channels, PIXELS), jnp.bfloat16),
            pltpu.VMEM((3, 9, channels, channels), jnp.bfloat16),
            pltpu.SemaphoreType.DMA((3,)),
        ],
        compiler_params=pltpu.CompilerParams(vmem_limit_bytes=VMEM_BYTES),
        cost_estimate=pl.CostEstimate(
            flops=2 * frames * 27 * channels * channels * PIXELS,
            bytes_accessed=2 * 27 * channels * channels,
            transcendentals=0,
        ),
        name="input_grad_part",
    )(ages, tap_masks(), weight, windows)


def fetch_rows(sources, rows, pieces, target, sems, start):
    def slot(j, carry):
        if start:
            for p, piece in enumerate(pieces):

                @pl.when(sources[j] == p)
                def _():
                    pltpu.make_async_copy(piece.at[rows[j]], target.at[j], sems.at[j]).start()

        else:

            @pl.when(sources[j] >= 0)
            def _():
                pltpu.make_async_copy(pieces[0].at[0], target.at[j], sems.at[j]).wait()

        return carry

    lax.fori_loop(0, target.shape[0], slot, 0)


def blank_rows(sources, target):
    def slot(j, carry):
        @pl.when(sources[j] < 0)
        def _():
            target[j] = jnp.zeros(target.shape[1:], target.dtype)

        return carry

    lax.fori_loop(0, target.shape[0], slot, 0)


def weight_kernel(chunk, scale, ages, sources, rows, parity, steps, masks, x, near, far, *rest):
    mine, theirs, seen, grads, even, odd, total, sems, seen_sem = rest
    slots, group = grads.shape[0], grads.shape[1]
    channels = x.shape[1]
    fetch_seen = pltpu.make_async_copy(x, seen, seen_sem)
    fetch_seen.start()
    fetch_rows(sources, rows, (near, far), grads, sems, True)
    total[...] = jnp.zeros_like(total)
    blank_rows(sources, grads)
    fetch_rows(sources, rows, (near, far), grads, sems, False)
    fetch_seen.wait()

    def build(first, taps):
        for f in range(chunk):
            frame = grads[jnp.minimum(first + f, slots - 1)]
            for t, tap in enumerate(pixel_taps(frame, masks)):
                taps[t * group : (t + 1) * group, f * PIXELS : (f + 1) * PIXELS] = tap

    def multiply(first, taps):
        parts = []
        for d in range(3):
            row = []
            for f in range(chunk):
                slot = first + f
                frame = seen[jnp.clip(slot - d, 0, slots - 1)]
                row.append(jnp.where(ages[slot] >= d, frame, jnp.zeros_like(frame)))
            parts.append(jnp.concatenate(row, axis=1))
        total[...] += lax.dot_general(
            jnp.concatenate(parts, axis=0),
            taps[...],
            (((1,), (1,)), ((), ())),
            preferred_element_type=jnp.float32,
        )

    build(0, even)

    def step(p, carry):
        first = 2 * p * chunk
        build(first + chunk, odd)
        multiply(first, even)
        build(first + 2 * chunk, even)
        multiply(first + chunk, odd)
        return carry

    lax.fori_loop(0, steps[0], step, 0)
    half, block = mine.shape[0], mine.shape[2]
    for j in range(half):
        for target, side in ((mine, parity[0]), (theirs, 1 - parity[0])):
            start = pl.multiple_of((2 * j + side) * block, 8)
            for d in range(3):
                terms = total[pl.ds(d * channels + start, block), :] * scale
                target[j, 2 - d] = terms.astype(jnp.bfloat16)


def weight_part(near, far, x, ages, sources, rows, parity, scale, count):
    slots, channels = x.shape[0], x.shape[1]
    group = near.shape[1]
    chunk = 2
    filled = jnp.sum((ages >= 0).astype(jnp.int32))
    steps = ((filled + 2 * chunk - 1) // (2 * chunk)).reshape((1,))
    ages = jnp.concatenate([ages, jnp.full((2 * chunk,), -1, jnp.int32)])
    smem = pl.BlockSpec(memory_space=pltpu.SMEM)
    vmem = pl.BlockSpec(memory_space=pltpu.VMEM)
    anywhere = pl.BlockSpec(memory_space=pl.ANY)
    blocks = jax.ShapeDtypeStruct((count // 2, 3, channels // count, 9 * group), jnp.bfloat16)
    tap_buffer = pltpu.VMEM((9 * group, chunk * PIXELS), jnp.bfloat16)
    return pl.pallas_call(
        functools.partial(weight_kernel, chunk, scale),
        out_shape=(blocks, blocks),
        in_specs=[smem] * 5 + [vmem] + [anywhere] * 3,
        out_specs=(vmem, vmem),
        scratch_shapes=[
            pltpu.VMEM(x.shape, jnp.bfloat16),
            pltpu.VMEM((slots, group, PIXELS), jnp.bfloat16),
            tap_buffer,
            tap_buffer,
            pltpu.VMEM((3 * channels, 9 * group), jnp.float32),
            pltpu.SemaphoreType.DMA((slots,)),
            pltpu.SemaphoreType.DMA,
        ],
        compiler_params=pltpu.CompilerParams(vmem_limit_bytes=VMEM_BYTES),
        cost_estimate=pl.CostEstimate(
            flops=2 * slots * 27 * channels * group * PIXELS,
            bytes_accessed=2 * slots * channels * PIXELS,
            transcendentals=0,
        ),
        name="weight_grad_part",
    )(ages, sources, rows, parity, steps, tap_masks(), x, near, far)


def pick_kernel(count, sources, rows, *rest):
    pieces, (out, sems) = rest[:count], rest[count:]
    fetch_rows(sources, rows, pieces, out, sems, True)
    blank_rows(sources, out)
    fetch_rows(sources, rows, pieces, out, sems, False)


def pick_rows(pieces, sources, rows):
    slots = rows.shape[0]
    smem = pl.BlockSpec(memory_space=pltpu.SMEM)
    anywhere = pl.BlockSpec(memory_space=pl.ANY)
    frame = pieces[0].shape[1:]
    return pl.pallas_call(
        functools.partial(pick_kernel, len(pieces)),
        out_shape=jax.ShapeDtypeStruct((slots,) + frame, jnp.bfloat16),
        in_specs=[smem] * 2 + [anywhere] * len(pieces),
        out_specs=pl.BlockSpec(memory_space=pltpu.VMEM),
        scratch_shapes=[pltpu.SemaphoreType.DMA((slots,))],
        compiler_params=pltpu.CompilerParams(vmem_limit_bytes=VMEM_BYTES),
        name="pick_rows",
    )(sources, rows, *pieces)


def swap(value, axis, flip):
    return lax.ppermute(value, axis, [(i, i ^ flip) for i in range(lax.axis_size(axis))])


def to_chips(piece, count):
    return [piece] + [swap(piece, "slab", k) for k in range(2, count, 2)]


def with_sibling(chips):
    near = jnp.concatenate(chips, axis=0)
    return near, swap(near, "slab", 1)


def shards(
    section_activations,
    kernel_weight,
    packed_output_gradient,
    clip_length,
    clip_slab_index,
    packed_clip_order,
):
    slots, channels = section_activations.shape[:2]
    rows, group = packed_output_gradient.shape[:2]
    count, heads = lax.axis_size("slab"), lax.axis_size("head")
    me, head = lax.axis_index("slab"), lax.axis_index("head")
    each, frame = rows // heads, packed_output_gradient.shape[1:]

    after = lax.ppermute(
        packed_output_gradient[:2], "slab", [(i, (i - 1) % count) for i in range(count)]
    )
    longer = jnp.concatenate([packed_output_gradient, after], axis=0)
    windows = jnp.stack([longer[each * h : each * h + each + 2] for h in range(heads)])
    piece, windows = lax.optimization_barrier((packed_output_gradient, windows))
    windows = lax.all_to_all(windows, "head", 0, 0)
    gradient_chips = to_chips(piece, count)

    encoder_offset, packed_start = clip_places(clip_length, clip_slab_index, packed_clip_order)
    slot_age, slot_row = slot_lookup(
        clip_length, clip_slab_index, encoder_offset, packed_start, me, slots
    )
    parity = (me % 2).reshape((1,)).astype(jnp.int32)
    shard, inner = jnp.maximum(slot_row, 0) // rows, jnp.maximum(slot_row, 0) % rows
    side, chip = (shard ^ me) % 2, (shard // 2) ^ (me // 2)
    source = jnp.where(slot_row >= 0, side, -1)
    window_rows = rows * me + each * head + jnp.arange(each + 2, dtype=jnp.int32)
    window_age = row_ages(clip_length, packed_start, window_rows)

    parts = input_part(windows, kernel_weight, window_age)
    parts, gradient_chips = lax.optimization_barrier((parts, gradient_chips))
    near, far = with_sibling(gradient_chips)
    sent = [lax.dynamic_index_in_dim(parts, head ^ k, 0, keepdims=False) for k in range(heads)]
    arrived = [sent[0], swap(sent[1], "head", 1)]
    arrived, sent = lax.optimization_barrier((arrived, sent))
    for k in range(2, heads):
        arrived.append(swap(sent[k], "head", k))
    width = heads // 2
    chips = [to_chips(jnp.concatenate(arrived[:width], axis=0), count)]

    x, near, far, first = lax.optimization_barrier((section_activations, near, far, arrived[0]))
    scale = 1.0 / math.sqrt(rows * count * PIXELS)
    mine, theirs = weight_part(
        near, far, x, slot_age, source, chip * rows + inner, parity, scale, count
    )
    mine, theirs, chips, late = lax.optimization_barrier((mine, theirs, chips, arrived[width:]))
    chips.append(to_chips(jnp.concatenate(late, axis=0), count))
    other = swap(theirs, "slab", 1)
    input_pieces = [piece for stage in chips for piece in with_sibling(stage)]

    rounded = (mine.astype(jnp.float32) + other.astype(jnp.float32)).astype(jnp.bfloat16)
    my_chip = me // 2
    weight_grad = sum(
        lax.dynamic_index_in_dim(term, my_chip, 0, keepdims=False).astype(jnp.float32)
        for term in (mine, other)
    )
    for k in range(1, count // 2):
        term = lax.dynamic_index_in_dim(rounded, my_chip ^ k, 0, keepdims=False)
        weight_grad = weight_grad + swap(term, "slab", 2 * k).astype(jnp.float32)
    block = channels // count
    weight_grad = weight_grad.astype(jnp.bfloat16).reshape(3, block, 9, group)
    weight_grad = weight_grad.transpose(0, 2, 1, 3).reshape(27, block, group)

    place = (inner // each) ^ head
    stage, place = place // width, place % width
    input_source = jnp.where(slot_row >= 0, 2 * stage + side, -1)
    input_row = (chip * width + place) * each + inner % each
    input_grad = pick_rows(input_pieces, input_source, input_row)
    return (input_grad, weight_grad)


def solution(mesh):
    return jax.shard_map(
        shards,
        mesh=mesh,
        in_specs=(P("slab", None, None), P(), P("slab", "head", None), P(), P(), P()),
        out_specs=(P("slab", "head", None), P(None, "slab", "head")),
        check_vma=False,
    )
```

```python
import functools
import math

import jax
import jax.numpy as jnp
import numpy as np
from jax import lax
from jax.experimental import pallas as pl
from jax.experimental.pallas import tpu as pltpu
from jax.sharding import PartitionSpec as P

PIXEL_ROWS = 16
PIXEL_COLUMNS = 16
PIXELS = PIXEL_ROWS * PIXEL_COLUMNS
MIB = 1024 * 1024


def clip_places(clip_lengths, slabs, order):
    clip_ids = jnp.arange(clip_lengths.shape[0], dtype=jnp.int32)
    same_slab = slabs[None, :] == slabs[:, None]
    earlier = clip_ids[None, :] < clip_ids[:, None]
    encoder_offset = jnp.sum(jnp.where(same_slab & earlier, clip_lengths[None, :], 0), axis=1)
    matches = order[None, :] == clip_ids[:, None]
    placing = jnp.sum(jnp.where(matches, clip_ids[None, :], 0), axis=1)
    prior_frames = placing[None, :] < placing[:, None]
    packed_start = jnp.sum(jnp.where(prior_frames, clip_lengths[None, :], 0), axis=1)
    return encoder_offset, packed_start


def slot_lookup(clip_lengths, slabs, encoder_offset, packed_start, slab_number, slots):
    slot_list = jnp.arange(slots, dtype=jnp.int32)[:, None]
    lag = slot_list - encoder_offset[None, :]
    inside = (slabs[None, :] == slab_number) & (lag >= 0) & (lag < clip_lengths[None, :])
    age = jnp.sum(jnp.where(inside, lag + 1, 0), axis=1) - 1
    row = jnp.sum(jnp.where(inside, packed_start[None, :] + lag + 1, 0), axis=1) - 1
    return age, row


def row_ages(clip_lengths, packed_start, rows):
    lag = rows[:, None] - packed_start[None, :]
    inside = (lag >= 0) & (lag < clip_lengths[None, :])
    return jnp.sum(jnp.where(inside, lag + 1, 0), axis=1) - 1


def tap_offsets():
    return [(1 - row_tap, 1 - col_tap) for row_tap in range(3) for col_tap in range(3)]


def tap_masks():
    row, column = np.divmod(np.arange(PIXELS), PIXEL_COLUMNS)
    masks = []
    for row_step, col_step in tap_offsets():
        good = (0 <= row + row_step) & (row + row_step < PIXEL_ROWS)
        good &= (0 <= column + col_step) & (column + col_step < PIXEL_COLUMNS)
        masks.append(np.broadcast_to(good, (16, PIXELS)))
    return jnp.asarray(np.stack(masks), jnp.bfloat16)


def pixel_taps(frame, masks):
    taps = []
    for t, (row_step, col_step) in enumerate(tap_offsets()):
        offset = row_step * PIXEL_COLUMNS + col_step
        if offset:
            moved = pltpu.roll(frame, (-offset) % PIXELS, 1).reshape(-1, 16, PIXELS)
            taps.append((moved * masks[t][None]).reshape(frame.shape))
        else:
            taps.append(frame)
    return taps


def input_kernel(heads, ages, places, masks, weight, *rest):
    mains, halos = rest[:heads], rest[heads : 2 * heads]
    out, windows, taps, kernels, sems, window_sems = rest[2 * heads :]
    frames, group = out.shape[1:3]
    channels = heads * group

    def fetch(kt):
        return pltpu.make_async_copy(weight.at[pl.ds(9 * kt, 9)], kernels.at[kt], sems.at[kt])

    def arrange(k):
        place = windows.at[places[k]]
        return (
            pltpu.make_async_copy(mains[k], place.at[pl.ds(0, frames)], window_sems.at[0, k]),
            pltpu.make_async_copy(halos[k], place.at[pl.ds(frames, 2)], window_sems.at[1, k]),
        )

    for k in range(heads):
        for copy in arrange(k):
            copy.start()
    for kt in (2, 1, 0):
        fetch(kt).start()
    for k in range(heads):
        for copy in arrange(k):
            copy.wait()
    for r in range(frames + 2):
        for g in range(heads):
            for t, tap in enumerate(pixel_taps(windows[g, r], masks)):
                start = t * channels + g * group
                taps[r, start : start + group, :] = tap
        f = r - 2
        if f < 0:
            continue
        total = None
        for d in range(3):
            if f == 0:
                fetch(2 - d).wait()
            kernel = jnp.concatenate([kernels[2 - d, t] for t in range(9)], axis=1)
            term = jnp.dot(kernel, taps[f + d], preferred_element_type=jnp.float32)
            if d == 0:
                total = term
            else:
                total = total + jnp.where(ages[f + d] >= d, term, 0.0)
        for g in range(heads):
            out[g, f] = total[g * group : (g + 1) * group, :].astype(jnp.bfloat16)


def input_part(mains, halos, weight, ages, places):
    heads = len(mains)
    frames, group = mains[0].shape[:2]
    channels = weight.shape[1]
    smem = pl.BlockSpec(memory_space=pltpu.SMEM)
    vmem = pl.BlockSpec(memory_space=pltpu.VMEM)
    anywhere = pl.BlockSpec(memory_space=pl.ANY)
    return pl.pallas_call(
        functools.partial(input_kernel, heads),
        out_shape=jax.ShapeDtypeStruct((heads, frames, group, PIXELS), jnp.bfloat16),
        in_specs=[smem, smem, vmem] + [anywhere] * (1 + 2 * heads),
        out_specs=vmem,
        scratch_shapes=[
            pltpu.VMEM((heads, frames + 2, group, PIXELS), jnp.bfloat16),
            pltpu.VMEM((frames + 2, 9 * channels, PIXELS), jnp.bfloat16),
            pltpu.VMEM((3, 9, channels, channels), jnp.bfloat16),
            pltpu.SemaphoreType.DMA((3,)),
            pltpu.SemaphoreType.DMA((2, heads)),
        ],
        compiler_params=pltpu.CompilerParams(vmem_limit_bytes=57 * MIB),
        cost_estimate=pl.CostEstimate(
            flops=2 * frames * 27 * channels * channels * PIXELS,
            bytes_accessed=2 * 27 * channels * channels,
            transcendentals=0,
        ),
        name="input_grad_part",
    )(ages, places, tap_masks(), weight, *mains, *halos)


def fetch_rows(sources, rows, pieces, target, sems, start, first=0):
    def slot(j, carry):
        if start:
            for p, piece in enumerate(pieces):

                @pl.when(sources[j] == p)
                def _():
                    row = piece.at[rows[j], pl.ds(first, target.shape[1])]
                    pltpu.make_async_copy(row, target.at[j], sems.at[j]).start()

        else:

            @pl.when(sources[j] >= 0)
            def _():
                row = pieces[0].at[0, pl.ds(first, target.shape[1])]
                pltpu.make_async_copy(row, target.at[j], sems.at[j]).wait()

        return carry

    lax.fori_loop(0, target.shape[0], slot, 0)


def blank_rows(sources, target):
    def slot(j, carry):
        @pl.when(sources[j] < 0)
        def _():
            target[j] = jnp.zeros(target.shape[1:], target.dtype)

        return carry

    lax.fori_loop(0, target.shape[0], slot, 0)


def weight_kernel(chunk, scale, half, ages, sources, rows, parity, steps, masks, x, *rest):
    gathered, mine, theirs, seen, grads, even, odd, total, sems, seen_sems = rest
    slots, group = grads.shape[0], grads.shape[1]
    channels = x.shape[1]
    span = 2 * chunk

    def fetch_seen(p):
        part = pl.ds(p * span, span)
        return pltpu.make_async_copy(x.at[part], seen.at[part], seen_sems.at[p])

    fetch_rows(sources, rows, (gathered,), grads, sems, True, half * group)
    for p in range(slots // span):
        fetch_seen(p).start()
    total[...] = jnp.zeros_like(total)
    blank_rows(sources, grads)
    fetch_rows(sources, rows, (gathered,), grads, sems, False, half * group)

    def build(first, taps):
        for f in range(chunk):
            frame = grads[jnp.minimum(first + f, slots - 1)]
            for t, tap in enumerate(pixel_taps(frame, masks)):
                taps[t * group : (t + 1) * group, f * PIXELS : (f + 1) * PIXELS] = tap

    def multiply(first, taps):
        parts = []
        for d in range(3):
            row = []
            for f in range(chunk):
                slot = first + f
                frame = seen[jnp.clip(slot - d, 0, slots - 1)]
                row.append(jnp.where(ages[slot] >= d, frame, jnp.zeros_like(frame)))
            parts.append(jnp.concatenate(row, axis=1))
        total[...] += lax.dot_general(
            jnp.concatenate(parts, axis=0),
            taps[...],
            (((1,), (1,)), ((), ())),
            preferred_element_type=jnp.float32,
        )

    build(0, even)

    def step(p, carry):
        first = 2 * p * chunk
        fetch_seen(p).wait()
        build(first + chunk, odd)
        multiply(first, even)
        build(first + 2 * chunk, even)
        multiply(first + chunk, odd)
        return carry

    def finish(p, carry):
        fetch_seen(p).wait()
        return carry

    lax.fori_loop(0, steps[0], step, 0)
    lax.fori_loop(steps[0], slots // span, finish, 0)
    chips, block = mine.shape[0], mine.shape[2]
    for j in range(chips):
        for target, side in ((mine, parity[0]), (theirs, 1 - parity[0])):
            start = pl.multiple_of((2 * j + side) * block, 8)
            for d in range(3):
                terms = total[pl.ds(d * channels + start, block), :] * scale
                target[j, 2 - d] = terms.astype(jnp.bfloat16)


def weight_part(half, halves, gathered, x, ages, sources, rows, parity, scale, count):
    slots, channels = x.shape[0], x.shape[1]
    group = gathered.shape[1] // halves
    chunk = 2
    assert slots % (2 * chunk) == 0
    filled = jnp.sum((ages >= 0).astype(jnp.int32))
    steps = ((filled + 2 * chunk - 1) // (2 * chunk)).reshape((1,))
    ages = jnp.concatenate([ages, jnp.full((2 * chunk,), -1, jnp.int32)])
    smem = pl.BlockSpec(memory_space=pltpu.SMEM)
    vmem = pl.BlockSpec(memory_space=pltpu.VMEM)
    anywhere = pl.BlockSpec(memory_space=pl.ANY)
    blocks = jax.ShapeDtypeStruct((count // 2, 3, channels // count, 9 * group), jnp.bfloat16)
    tap_buffer = pltpu.VMEM((9 * group, chunk * PIXELS), jnp.bfloat16)
    return pl.pallas_call(
        functools.partial(weight_kernel, chunk, scale, half),
        out_shape=(blocks, blocks),
        in_specs=[smem] * 5 + [vmem] + [anywhere] * 2,
        out_specs=(vmem, vmem),
        scratch_shapes=[
            pltpu.VMEM(x.shape, jnp.bfloat16),
            pltpu.VMEM((slots, group, PIXELS), jnp.bfloat16),
            tap_buffer,
            tap_buffer,
            pltpu.VMEM((3 * channels, 9 * group), jnp.float32),
            pltpu.SemaphoreType.DMA((slots,)),
            pltpu.SemaphoreType.DMA((slots // (2 * chunk),)),
        ],
        compiler_params=pltpu.CompilerParams(vmem_limit_bytes=59 * MIB),
        cost_estimate=pl.CostEstimate(
            flops=2 * slots * 27 * channels * group * PIXELS,
            bytes_accessed=2 * slots * channels * PIXELS,
            transcendentals=0,
        ),
        name="weight_grad_part",
    )(ages, sources, rows, parity, steps, tap_masks(), x, gathered)


def pick_kernel(count, sources, rows, *rest):
    pieces, (out, sems) = rest[:count], rest[count:]
    fetch_rows(sources, rows, pieces, out, sems, True)
    blank_rows(sources, out)
    fetch_rows(sources, rows, pieces, out, sems, False)


def pick_rows(pieces, sources, rows):
    slots = rows.shape[0]
    smem = pl.BlockSpec(memory_space=pltpu.SMEM)
    anywhere = pl.BlockSpec(memory_space=pl.ANY)
    frame = pieces[0].shape[1:]
    return pl.pallas_call(
        functools.partial(pick_kernel, len(pieces)),
        out_shape=jax.ShapeDtypeStruct((slots,) + frame, jnp.bfloat16),
        in_specs=[smem] * 2 + [anywhere] * len(pieces),
        out_specs=pl.BlockSpec(memory_space=pltpu.VMEM),
        scratch_shapes=[pltpu.SemaphoreType.DMA((slots,))],
        compiler_params=pltpu.CompilerParams(vmem_limit_bytes=16 * MIB),
        name="pick_rows",
    )(sources, rows, *pieces)


def swap(value, axis, flip):
    return lax.ppermute(value, axis, [(i, i ^ flip) for i in range(lax.axis_size(axis))])


def to_chips(piece, count):
    return [piece] + [swap(piece, "slab", k) for k in range(2, count, 2)]


def with_siblings(chips):
    return chips + [swap(piece, "slab", 1) for piece in chips]


def shards(
    section_activations,
    kernel_weight,
    packed_output_gradient,
    clip_length,
    clip_slab_index,
    packed_clip_order,
):
    slots, channels = section_activations.shape[:2]
    rows, group = packed_output_gradient.shape[:2]
    count, heads = lax.axis_size("slab"), lax.axis_size("head")
    me, head = lax.axis_index("slab"), lax.axis_index("head")
    each, frame = rows // heads, packed_output_gradient.shape[1:]

    gathered = lax.all_gather(packed_output_gradient, "slab", axis=0, tiled=True)
    own = packed_output_gradient.reshape((heads, each) + frame)
    after = lax.ppermute(
        packed_output_gradient[:2], "slab", [(i, (i - 1) % count) for i in range(count)]
    )
    mains = [lax.dynamic_index_in_dim(own, head ^ k, 0, keepdims=False) for k in range(heads)]
    mains = mains[:1] + [swap(mains[k], "head", k) for k in range(1, heads)]
    later = jnp.concatenate([own[1:, :2], after[None]], axis=0)
    halos = [lax.dynamic_index_in_dim(later, head ^ k, 0, keepdims=False) for k in range(heads)]
    halos = halos[:1] + [swap(halos[k], "head", k) for k in range(1, heads)]

    encoder_offset, packed_start = clip_places(clip_length, clip_slab_index, packed_clip_order)
    slot_age, slot_row = slot_lookup(
        clip_length, clip_slab_index, encoder_offset, packed_start, me, slots
    )
    parity = (me % 2).reshape((1,)).astype(jnp.int32)
    shard, inner = jnp.maximum(slot_row, 0) // rows, jnp.maximum(slot_row, 0) % rows
    side, chip = (shard ^ me) % 2, (shard // 2) ^ (me // 2)
    source = jnp.where(slot_row >= 0, 0, -1)
    places = head ^ jnp.arange(heads, dtype=jnp.int32)
    window_rows = rows * me + each * head + jnp.arange(each + 2, dtype=jnp.int32)
    window_age = row_ages(clip_length, packed_start, window_rows)

    parts = input_part(mains, halos, kernel_weight, window_age, places)
    sent = [lax.dynamic_index_in_dim(parts, head ^ k, 0, keepdims=False) for k in range(heads)]
    arrived = [sent[0], swap(sent[1], "head", 1)]
    arrived, sent = lax.optimization_barrier((arrived, sent))
    for k in range(2, heads):
        arrived.append(swap(sent[k], "head", k))
    width = heads // 2
    piece = jnp.concatenate(arrived[:width], axis=0)
    near = to_chips(piece, count)

    scale = 1.0 / math.sqrt(rows * count * PIXELS)
    halves = 2 if group % 32 == 0 else 1

    def weight_half(half, x):
        return weight_part(
            half, halves, gathered, x, slot_age, source, slot_row, parity, scale, count
        )

    x, piece = lax.optimization_barrier((section_activations, piece))
    mine, theirs = weight_half(0, x)
    mine, theirs, near, late = lax.optimization_barrier((mine, theirs, near, arrived[width:]))
    piece = jnp.concatenate(late, axis=0)
    far = to_chips(piece, count)
    other = swap(theirs, "slab", 1)
    input_pieces = with_siblings(near)
    mines, others = [mine], [other]
    if halves == 2:
        x, piece = lax.optimization_barrier((x, piece))
        mine, theirs = weight_half(1, x)
        mine, theirs, far, others = lax.optimization_barrier((mine, theirs, far, others))
        mines.append(mine)
        others.append(swap(theirs, "slab", 1))
    input_pieces += with_siblings(far)

    mine, other = jnp.stack(mines, axis=1), jnp.stack(others, axis=1)
    rounded = (mine.astype(jnp.float32) + other.astype(jnp.float32)).astype(jnp.bfloat16)
    my_chip = me // 2
    weight_grad = sum(
        lax.dynamic_index_in_dim(term, my_chip, 0, keepdims=False).astype(jnp.float32)
        for term in (mine, other)
    )
    for k in range(1, count // 2):
        term = lax.dynamic_index_in_dim(rounded, my_chip ^ k, 0, keepdims=False)
        weight_grad = weight_grad + swap(term, "slab", 2 * k).astype(jnp.float32)
    block = channels // count
    weight_grad = weight_grad.astype(jnp.bfloat16).reshape(halves, 3, block, 9, group // halves)
    weight_grad = weight_grad.transpose(1, 3, 2, 0, 4).reshape(27, block, group)

    place = (inner // each) ^ head
    stage, place = place // width, place % width
    input_source = jnp.where(slot_row >= 0, (2 * stage + side) * (count // 2) + chip, -1)
    input_row = place * each + inner % each
    input_grad = pick_rows(input_pieces, input_source, input_row)
    return (input_grad, weight_grad)


def solution(mesh):
    return jax.shard_map(
        shards,
        mesh=mesh,
        in_specs=(P("slab", None, None), P(), P("slab", "head", None), P(), P(), P()),
        out_specs=(P("slab", "head", None), P(None, "slab", "head")),
        check_vma=False,
    )
```

```python
import functools
import math

import jax
import jax.numpy as jnp
import numpy as np
from jax import lax
from jax.experimental import pallas as pl
from jax.experimental.pallas import tpu as pltpu
from jax.sharding import PartitionSpec as P

PIXEL_ROWS = 16
PIXEL_COLUMNS = 16
PIXELS = PIXEL_ROWS * PIXEL_COLUMNS
MIB = 1024 * 1024


def clip_places(clip_lengths, slabs, order):
    clip_ids = jnp.arange(clip_lengths.shape[0], dtype=jnp.int32)
    same_slab = slabs[None, :] == slabs[:, None]
    earlier = clip_ids[None, :] < clip_ids[:, None]
    encoder_offset = jnp.sum(jnp.where(same_slab & earlier, clip_lengths[None, :], 0), axis=1)
    matches = order[None, :] == clip_ids[:, None]
    placing = jnp.sum(jnp.where(matches, clip_ids[None, :], 0), axis=1)
    prior_frames = placing[None, :] < placing[:, None]
    packed_start = jnp.sum(jnp.where(prior_frames, clip_lengths[None, :], 0), axis=1)
    return encoder_offset, packed_start


def slot_lookup(clip_lengths, slabs, encoder_offset, packed_start, slab_number, slots):
    slot_list = jnp.arange(slots, dtype=jnp.int32)[:, None]
    lag = slot_list - encoder_offset[None, :]
    inside = (slabs[None, :] == slab_number) & (lag >= 0) & (lag < clip_lengths[None, :])
    age = jnp.sum(jnp.where(inside, lag + 1, 0), axis=1) - 1
    row = jnp.sum(jnp.where(inside, packed_start[None, :] + lag + 1, 0), axis=1) - 1
    return age, row


def row_ages(clip_lengths, packed_start, rows):
    lag = rows[:, None] - packed_start[None, :]
    inside = (lag >= 0) & (lag < clip_lengths[None, :])
    return jnp.sum(jnp.where(inside, lag + 1, 0), axis=1) - 1


def tap_offsets():
    return [(1 - row_tap, 1 - col_tap) for row_tap in range(3) for col_tap in range(3)]


def tap_masks():
    row, column = np.divmod(np.arange(PIXELS), PIXEL_COLUMNS)
    masks = []
    for row_step, col_step in tap_offsets():
        good = (0 <= row + row_step) & (row + row_step < PIXEL_ROWS)
        good &= (0 <= column + col_step) & (column + col_step < PIXEL_COLUMNS)
        masks.append(np.broadcast_to(good, (16, PIXELS)))
    return jnp.asarray(np.stack(masks), jnp.bfloat16)


def pixel_taps(frame, masks):
    taps = []
    for t, (row_step, col_step) in enumerate(tap_offsets()):
        offset = row_step * PIXEL_COLUMNS + col_step
        if offset:
            moved = pltpu.roll(frame, (-offset) % PIXELS, 1).reshape(-1, 16, PIXELS)
            taps.append((moved * masks[t][None]).reshape(frame.shape))
        else:
            taps.append(frame)
    return taps


def input_kernel(heads, ages, places, masks, kernels, *rest):
    pieces, (out, windows, taps, sems) = rest[:heads], rest[heads:]
    frames, group = out.shape[1:3]
    channels = heads * group
    copies = [
        pltpu.make_async_copy(pieces[k], windows.at[places[k]], sems.at[k]) for k in range(heads)
    ]
    for copy in copies:
        copy.start()
    for copy in copies:
        copy.wait()
    for r in range(frames + 2):
        for g in range(heads):
            for t, tap in enumerate(pixel_taps(windows[g, r], masks)):
                start = t * channels + g * group
                taps[r, start : start + group, :] = tap
        f = r - 2
        if f < 0:
            continue
        total = None
        for d in range(3):
            term = jnp.dot(kernels[2 - d], taps[f + d], preferred_element_type=jnp.float32)
            if d == 0:
                total = term
            else:
                total = total + jnp.where(ages[f + d] >= d, term, 0.0)
        for g in range(heads):
            out[g, f] = total[g * group : (g + 1) * group, :].astype(jnp.bfloat16)


def input_part(pieces, kernels, ages, places):
    heads = len(pieces)
    frames, group = pieces[0].shape[0] - 2, pieces[0].shape[1]
    channels = heads * group
    smem = pl.BlockSpec(memory_space=pltpu.SMEM)
    vmem = pl.BlockSpec(memory_space=pltpu.VMEM)
    anywhere = pl.BlockSpec(memory_space=pl.ANY)
    return pl.pallas_call(
        functools.partial(input_kernel, heads),
        out_shape=jax.ShapeDtypeStruct((heads, frames, group, PIXELS), jnp.bfloat16),
        in_specs=[smem, smem, vmem, vmem] + [anywhere] * heads,
        out_specs=vmem,
        scratch_shapes=[
            pltpu.VMEM((heads, frames + 2, group, PIXELS), jnp.bfloat16),
            pltpu.VMEM((frames + 2, 9 * channels, PIXELS), jnp.bfloat16),
            pltpu.SemaphoreType.DMA((heads,)),
        ],
        compiler_params=pltpu.CompilerParams(vmem_limit_bytes=32 * MIB),
        cost_estimate=pl.CostEstimate(
            flops=2 * frames * 27 * channels * channels * PIXELS,
            bytes_accessed=2 * 27 * channels * channels,
            transcendentals=0,
        ),
        name="input_grad_part",
    )(ages, places, tap_masks(), kernels, *pieces)


def arrange_kernel(weight, out, sems):
    channels = weight.shape[1]
    copies = []
    for tap in range(27):
        columns = pl.ds(tap % 9 * channels, channels)
        target = out.at[tap // 9, :, columns]
        copies.append(pltpu.make_async_copy(weight.at[tap], target, sems.at[tap]))
    for copy in copies:
        copy.start()
    for copy in copies:
        copy.wait()


def arrange_weight(weight):
    channels = weight.shape[1]
    anywhere = pl.BlockSpec(memory_space=pl.ANY)
    return pl.pallas_call(
        arrange_kernel,
        out_shape=jax.ShapeDtypeStruct((3, channels, 9 * channels), jnp.bfloat16),
        in_specs=[anywhere],
        out_specs=anywhere,
        scratch_shapes=[pltpu.SemaphoreType.DMA((27,))],
        name="arrange_weight",
    )(weight)


def fetch_rows(sources, rows, pieces, target, sems, start, first=0):
    def slot(j, carry):
        if start:
            for p, piece in enumerate(pieces):

                @pl.when(sources[j] == p)
                def _():
                    row = piece.at[rows[j], pl.ds(first, target.shape[1])]
                    pltpu.make_async_copy(row, target.at[j], sems.at[j]).start()

        else:

            @pl.when(sources[j] >= 0)
            def _():
                row = pieces[0].at[0, pl.ds(first, target.shape[1])]
                pltpu.make_async_copy(row, target.at[j], sems.at[j]).wait()

        return carry

    lax.fori_loop(0, target.shape[0], slot, 0)


def blank_rows(sources, target):
    def slot(j, carry):
        @pl.when(sources[j] < 0)
        def _():
            target[j] = jnp.zeros(target.shape[1:], target.dtype)

        return carry

    lax.fori_loop(0, target.shape[0], slot, 0)


def weight_kernel(chunk, scale, half, ages, sources, rows, parity, steps, masks, x, *rest):
    pieces, rest = rest[:-9], rest[-9:]
    mine, theirs, seen, grads, even, odd, total, sems, seen_sems = rest
    slots, group = grads.shape[0], grads.shape[1]
    channels = x.shape[1]
    span = 2 * chunk

    def fetch_seen(p):
        part = pl.ds(p * span, span)
        return pltpu.make_async_copy(x.at[part], seen.at[part], seen_sems.at[p])

    fetch_rows(sources, rows, pieces, grads, sems, True, half * group)
    for p in range(slots // span):
        fetch_seen(p).start()
    total[...] = jnp.zeros_like(total)
    blank_rows(sources, grads)
    fetch_rows(sources, rows, pieces, grads, sems, False, half * group)

    def build(first, taps):
        for f in range(chunk):
            frame = grads[jnp.minimum(first + f, slots - 1)]
            for t, tap in enumerate(pixel_taps(frame, masks)):
                taps[t * group : (t + 1) * group, f * PIXELS : (f + 1) * PIXELS] = tap

    def multiply(first, taps):
        parts = []
        for d in range(3):
            row = []
            for f in range(chunk):
                slot = first + f
                frame = seen[jnp.clip(slot - d, 0, slots - 1)]
                row.append(jnp.where(ages[slot] >= d, frame, jnp.zeros_like(frame)))
            parts.append(jnp.concatenate(row, axis=1))
        total[...] += lax.dot_general(
            jnp.concatenate(parts, axis=0),
            taps[...],
            (((1,), (1,)), ((), ())),
            preferred_element_type=jnp.float32,
        )

    build(0, even)

    def step(p, carry):
        first = 2 * p * chunk
        fetch_seen(p).wait()
        build(first + chunk, odd)
        multiply(first, even)
        build(first + 2 * chunk, even)
        multiply(first + chunk, odd)
        return carry

    def finish(p, carry):
        fetch_seen(p).wait()
        return carry

    lax.fori_loop(0, steps[0], step, 0)
    lax.fori_loop(steps[0], slots // span, finish, 0)
    chips, block = mine.shape[0], mine.shape[2]
    for j in range(chips):
        for target, side in ((mine, parity[0]), (theirs, 1 - parity[0])):
            start = pl.multiple_of((2 * j + side) * block, 8)
            for d in range(3):
                terms = total[pl.ds(d * channels + start, block), :] * scale
                target[j, 2 - d] = terms.astype(jnp.bfloat16)


def weight_part(half, halves, pieces, x, ages, sources, rows, parity, scale, count):
    slots, channels = x.shape[0], x.shape[1]
    group = pieces[0].shape[1] // halves
    chunk = 2
    assert slots % (2 * chunk) == 0
    filled = jnp.sum((ages >= 0).astype(jnp.int32))
    steps = ((filled + 2 * chunk - 1) // (2 * chunk)).reshape((1,))
    ages = jnp.concatenate([ages, jnp.full((2 * chunk,), -1, jnp.int32)])
    smem = pl.BlockSpec(memory_space=pltpu.SMEM)
    vmem = pl.BlockSpec(memory_space=pltpu.VMEM)
    anywhere = pl.BlockSpec(memory_space=pl.ANY)
    blocks = jax.ShapeDtypeStruct((count // 2, 3, channels // count, 9 * group), jnp.bfloat16)
    tap_buffer = pltpu.VMEM((9 * group, chunk * PIXELS), jnp.bfloat16)
    return pl.pallas_call(
        functools.partial(weight_kernel, chunk, scale, half),
        out_shape=(blocks, blocks),
        in_specs=[smem] * 5 + [vmem] + [anywhere] * (1 + len(pieces)),
        out_specs=(vmem, vmem),
        scratch_shapes=[
            pltpu.VMEM(x.shape, jnp.bfloat16),
            pltpu.VMEM((slots, group, PIXELS), jnp.bfloat16),
            tap_buffer,
            tap_buffer,
            pltpu.VMEM((3 * channels, 9 * group), jnp.float32),
            pltpu.SemaphoreType.DMA((slots,)),
            pltpu.SemaphoreType.DMA((slots // (2 * chunk),)),
        ],
        compiler_params=pltpu.CompilerParams(vmem_limit_bytes=32 * MIB),
        cost_estimate=pl.CostEstimate(
            flops=2 * slots * 27 * channels * group * PIXELS,
            bytes_accessed=2 * slots * channels * PIXELS,
            transcendentals=0,
        ),
        name="weight_grad_part",
    )(ages, sources, rows, parity, steps, tap_masks(), x, *pieces)


def pick_kernel(count, *rest):
    tables, pieces = rest[:4], rest[4 : 4 + count]
    outs, sems = rest[4 + count : 6 + count], rest[6 + count]
    for start in (True, False):
        for i, out in enumerate(outs):
            sources, rows = tables[2 * i : 2 * i + 2]
            fetch_rows(sources, rows, pieces, out, sems.at[i], start)
            if start:
                blank_rows(sources, out)


def pick_rows(pieces, *tables):
    slots = tables[0].shape[0]
    smem = pl.BlockSpec(memory_space=pltpu.SMEM)
    vmem = pl.BlockSpec(memory_space=pltpu.VMEM)
    anywhere = pl.BlockSpec(memory_space=pl.ANY)
    frames = jax.ShapeDtypeStruct((slots,) + pieces[0].shape[1:], jnp.bfloat16)
    return pl.pallas_call(
        functools.partial(pick_kernel, len(pieces)),
        out_shape=(frames, frames),
        in_specs=[smem] * 4 + [anywhere] * len(pieces),
        out_specs=(vmem, vmem),
        scratch_shapes=[pltpu.SemaphoreType.DMA((2, slots))],
        compiler_params=pltpu.CompilerParams(vmem_limit_bytes=16 * MIB),
        cost_estimate=pl.CostEstimate(
            flops=0, bytes_accessed=16 * frames.size, transcendentals=0
        ),
        name="pick_rows",
    )(*tables, *pieces)


def swap(value, axis, flip):
    return lax.ppermute(value, axis, [(i, i ^ flip) for i in range(lax.axis_size(axis))])


def to_chips(piece, count, late=None):
    late = piece if late is None else late
    return [piece] + [swap(late if k & (k - 1) else piece, "slab", k) for k in range(2, count, 2)]


def with_siblings(chips):
    return chips + [swap(piece, "slab", 1) for piece in chips]


def shards(
    section_activations,
    kernel_weight,
    packed_output_gradient,
    clip_length,
    clip_slab_index,
    packed_clip_order,
):
    slots, channels = section_activations.shape[:2]
    rows, group = packed_output_gradient.shape[:2]
    count, heads = lax.axis_size("slab"), lax.axis_size("head")
    me, head = lax.axis_index("slab"), lax.axis_index("head")
    each, frame = rows // heads, packed_output_gradient.shape[1:]

    after = lax.ppermute(
        packed_output_gradient[:2], "slab", [(i, (i - 1) % count) for i in range(count)]
    )
    longer = jnp.concatenate([packed_output_gradient, after], axis=0)
    windows = [
        lax.dynamic_slice_in_dim(longer, each * (head ^ k), each + 2, 0) for k in range(heads)
    ]
    piece, windows = lax.optimization_barrier((packed_output_gradient, windows))
    windows = windows[:1] + [swap(windows[k], "head", k) for k in range(1, heads)]
    late_piece, windows[1] = lax.optimization_barrier((piece, windows[1]))
    gradient_chips = to_chips(piece, count, late_piece)
    kernels = arrange_weight(kernel_weight)

    encoder_offset, packed_start = clip_places(clip_length, clip_slab_index, packed_clip_order)
    parity = (me % 2).reshape((1,)).astype(jnp.int32)
    tables = []
    for slab in (me, me ^ 1):
        age, row = slot_lookup(
            clip_length, clip_slab_index, encoder_offset, packed_start, slab, slots
        )
        shard, inner = jnp.maximum(row, 0) // rows, jnp.maximum(row, 0) % rows
        tables.append((age, row, (shard ^ me) % 2, (shard // 2) ^ (me // 2), inner))
    slot_age, slot_row, side, chip, inner = tables[0]
    source = jnp.where(slot_row >= 0, side * (count // 2) + chip, -1)
    places = head ^ jnp.arange(heads, dtype=jnp.int32)
    window_rows = rows * me + each * head + jnp.arange(each + 2, dtype=jnp.int32)
    window_age = row_ages(clip_length, packed_start, window_rows)

    parts = input_part(windows, kernels, window_age, places)
    parts, gradient_chips = lax.optimization_barrier((parts, gradient_chips))
    gradient_pieces = with_siblings(gradient_chips)
    sent = [lax.dynamic_index_in_dim(parts, head ^ k, 0, keepdims=False) for k in range(heads)]
    arrived = [sent[0], swap(sent[1], "head", 1)]
    arrived, sent = lax.optimization_barrier((arrived, sent))
    for k in range(2, heads):
        arrived.append(swap(sent[k], "head", k))
    width = heads // 2
    piece = jnp.concatenate(arrived[:width], axis=0)
    near = to_chips(piece, count)

    scale = 1.0 / math.sqrt(rows * count * PIXELS)
    halves = 2 if group % 32 == 0 else 1

    def weight_half(half, x):
        return weight_part(
            half, halves, gradient_pieces, x, slot_age, source, inner, parity, scale, count
        )

    x, piece = lax.optimization_barrier((section_activations, piece))
    mine, theirs = weight_half(0, x)
    mine, theirs, late = lax.optimization_barrier((mine, theirs, arrived[width:]))
    piece = jnp.concatenate(late, axis=0)
    far = to_chips(piece, count)
    mines, others = [mine], [swap(theirs, "slab", 1)]
    if halves == 2:
        x, piece = lax.optimization_barrier((x, piece))
        mine, theirs = weight_half(1, x)
        mine, theirs, near, far, others = lax.optimization_barrier(
            (mine, theirs, near, far, others)
        )
        mines.append(mine)
        others.append(swap(theirs, "slab", 1))

    mine, other = jnp.stack(mines, axis=1), jnp.stack(others, axis=1)
    rounded = (mine.astype(jnp.float32) + other.astype(jnp.float32)).astype(jnp.bfloat16)
    rounded, near, far = lax.optimization_barrier((rounded, near, far))
    my_chip = me // 2
    weight_grad = sum(
        lax.dynamic_index_in_dim(term, my_chip, 0, keepdims=False).astype(jnp.float32)
        for term in (mine, other)
    )
    for k in range(1, count // 2):
        term = lax.dynamic_index_in_dim(rounded, my_chip ^ k, 0, keepdims=False)
        weight_grad = weight_grad + swap(term, "slab", 2 * k).astype(jnp.float32)
    block = channels // count
    weight_grad = weight_grad.astype(jnp.bfloat16).reshape(halves, 3, block, 9, group // halves)
    weight_grad = weight_grad.transpose(1, 3, 2, 0, 4).reshape(27, block, group)

    picks = []
    for _, row, beside, chip, inner in tables:
        stage, place = ((inner // each) ^ head) // width, ((inner // each) ^ head) % width
        held = (row >= 0) & (beside == 0)
        picks.append(jnp.where(held, stage * (count // 2) + chip, -1))
        picks.append(place * each + inner % each)
    here, there = pick_rows(near + far, *picks)
    there = swap(there, "slab", 1)
    input_grad = jnp.where((side == 0)[:, None, None], here, there)
    return (input_grad, weight_grad)


def solution(mesh):
    return jax.shard_map(
        shards,
        mesh=mesh,
        in_specs=(P("slab", None, None), P(), P("slab", "head", None), P(), P(), P()),
        out_specs=(P("slab", "head", None), P(None, "slab", "head")),
        check_vma=False,
    )
```

```python
import functools
import math

import jax
import jax.numpy as jnp
import numpy as np
from jax import lax
from jax.experimental import pallas as pl
from jax.experimental.pallas import tpu as pltpu
from jax.sharding import PartitionSpec as P

PIXEL_ROWS = 16
PIXEL_COLUMNS = 16
PIXELS = PIXEL_ROWS * PIXEL_COLUMNS
MIB = 1024 * 1024


def clip_places(clip_lengths, slabs, order):
    clip_ids = jnp.arange(clip_lengths.shape[0], dtype=jnp.int32)
    same_slab = slabs[None, :] == slabs[:, None]
    earlier = clip_ids[None, :] < clip_ids[:, None]
    encoder_offset = jnp.sum(jnp.where(same_slab & earlier, clip_lengths[None, :], 0), axis=1)
    matches = order[None, :] == clip_ids[:, None]
    placing = jnp.sum(jnp.where(matches, clip_ids[None, :], 0), axis=1)
    prior_frames = placing[None, :] < placing[:, None]
    packed_start = jnp.sum(jnp.where(prior_frames, clip_lengths[None, :], 0), axis=1)
    return encoder_offset, packed_start


def slot_lookup(clip_lengths, slabs, encoder_offset, packed_start, slab_number, slots):
    slot_list = jnp.arange(slots, dtype=jnp.int32)[:, None]
    lag = slot_list - encoder_offset[None, :]
    inside = (slabs[None, :] == slab_number) & (lag >= 0) & (lag < clip_lengths[None, :])
    age = jnp.sum(jnp.where(inside, lag + 1, 0), axis=1) - 1
    row = jnp.sum(jnp.where(inside, packed_start[None, :] + lag + 1, 0), axis=1) - 1
    return age, row


def row_ages(clip_lengths, packed_start, rows):
    lag = rows[:, None] - packed_start[None, :]
    inside = (lag >= 0) & (lag < clip_lengths[None, :])
    return jnp.sum(jnp.where(inside, lag + 1, 0), axis=1) - 1


def row_slot(clip_lengths, slabs, encoder_offset, packed_start, rows):
    lag = rows[:, None] - packed_start[None, :]
    inside = (lag >= 0) & (lag < clip_lengths[None, :])
    slab = jnp.sum(jnp.where(inside, slabs[None, :], 0), axis=1)
    slot = jnp.sum(jnp.where(inside, encoder_offset[None, :] + lag, 0), axis=1)
    return slab, slot


def tap_offsets():
    return [(1 - row_tap, 1 - col_tap) for row_tap in range(3) for col_tap in range(3)]


def tap_masks():
    row, column = np.divmod(np.arange(PIXELS), PIXEL_COLUMNS)
    masks = []
    for row_step, col_step in tap_offsets():
        good = (0 <= row + row_step) & (row + row_step < PIXEL_ROWS)
        good &= (0 <= column + col_step) & (column + col_step < PIXEL_COLUMNS)
        masks.append(np.broadcast_to(good, (16, PIXELS)))
    return jnp.asarray(np.stack(masks), jnp.bfloat16)


def pixel_taps(frame, masks):
    taps = []
    for t, (row_step, col_step) in enumerate(tap_offsets()):
        offset = row_step * PIXEL_COLUMNS + col_step
        if offset:
            moved = pltpu.roll(frame, (-offset) % PIXELS, 1).reshape(-1, 16, PIXELS)
            taps.append((moved * masks[t][None]).reshape(frame.shape))
        else:
            taps.append(frame)
    return taps


def input_kernel(heads, ages, places, masks, weight, *rest):
    pieces, (out, windows, taps, sems) = rest[:heads], rest[heads:]
    frames, group = out.shape[1:3]
    channels = heads * group
    copies = [
        pltpu.make_async_copy(pieces[k], windows.at[places[k]], sems.at[k]) for k in range(heads)
    ]
    for copy in copies:
        copy.start()
    for copy in copies:
        copy.wait()
    for r in range(frames + 2):
        for g in range(heads):
            for t, tap in enumerate(pixel_taps(windows[g, r], masks)):
                start = t * channels + g * group
                taps[r, start : start + group, :] = tap
        f = r - 2
        if f < 0:
            continue
        total = None
        for d in range(3):
            kernel = jnp.concatenate([weight[9 * (2 - d) + t] for t in range(9)], axis=1)
            term = jnp.dot(kernel, taps[f + d], preferred_element_type=jnp.float32)
            if d == 0:
                total = term
            else:
                total = total + jnp.where(ages[f + d] >= d, term, 0.0)
        for g in range(heads):
            out[g, f] = total[g * group : (g + 1) * group, :].astype(jnp.bfloat16)


def input_part(pieces, weight, ages, places, masks):
    heads = len(pieces)
    frames, group = pieces[0].shape[0] - 2, pieces[0].shape[1]
    channels = heads * group
    smem = pl.BlockSpec(memory_space=pltpu.SMEM)
    vmem = pl.BlockSpec(memory_space=pltpu.VMEM)
    anywhere = pl.BlockSpec(memory_space=pl.ANY)
    return pl.pallas_call(
        functools.partial(input_kernel, heads),
        out_shape=jax.ShapeDtypeStruct((heads, frames, group, PIXELS), jnp.bfloat16),
        in_specs=[smem, smem, vmem, vmem] + [anywhere] * heads,
        out_specs=vmem,
        scratch_shapes=[
            pltpu.VMEM((heads, frames + 2, group, PIXELS), jnp.bfloat16),
            pltpu.VMEM((frames + 2, 9 * channels, PIXELS), jnp.bfloat16),
            pltpu.SemaphoreType.DMA((heads,)),
        ],
        compiler_params=pltpu.CompilerParams(vmem_limit_bytes=32 * MIB),
        cost_estimate=pl.CostEstimate(
            flops=2 * frames * 27 * channels * channels * PIXELS,
            bytes_accessed=2 * 27 * channels * channels,
            transcendentals=0,
        ),
        name="input_grad_part",
    )(ages, places, masks, weight, *pieces)


def early_kernel(masks, weight, out):
    out[...] = masks[...]


def ask_early(masks, weight):
    vmem = pl.BlockSpec(memory_space=pltpu.VMEM)
    return pl.pallas_call(
        early_kernel,
        out_shape=jax.ShapeDtypeStruct(masks.shape, masks.dtype),
        in_specs=[vmem, vmem],
        out_specs=vmem,
        compiler_params=pltpu.CompilerParams(vmem_limit_bytes=16 * MIB),
        name="ask_early",
    )(masks, weight)


def fetch_rows(sources, rows, pieces, target, sems, start, first=0):
    def slot(j, carry):
        if start:
            for p, piece in enumerate(pieces):

                @pl.when(sources[j] == p)
                def _():
                    row = piece.at[rows[j], pl.ds(first, target.shape[1])]
                    pltpu.make_async_copy(row, target.at[j], sems.at[j]).start()

        else:

            @pl.when(sources[j] >= 0)
            def _():
                row = pieces[0].at[0, pl.ds(first, target.shape[1])]
                pltpu.make_async_copy(row, target.at[j], sems.at[j]).wait()

        return carry

    lax.fori_loop(0, target.shape[0], slot, 0)


def blank_rows(sources, target):
    def slot(j, carry):
        @pl.when(sources[j] < 0)
        def _():
            target[j] = jnp.zeros(target.shape[1:], target.dtype)

        return carry

    lax.fori_loop(0, target.shape[0], slot, 0)


def weight_kernel(chunk, scale, half, ages, sources, rows, parity, steps, masks, x, *rest):
    pieces, rest = rest[:-9], rest[-9:]
    mine, theirs, seen, grads, even, odd, total, sems, seen_sems = rest
    slots, group = grads.shape[0], grads.shape[1]
    channels = x.shape[1]
    span = 2 * chunk

    def fetch_seen(p):
        part = pl.ds(p * span, span)
        return pltpu.make_async_copy(x.at[part], seen.at[part], seen_sems.at[p])

    fetch_rows(sources, rows, pieces, grads, sems, True, half * group)
    for p in range(slots // span):
        fetch_seen(p).start()
    total[...] = jnp.zeros_like(total)
    blank_rows(sources, grads)
    fetch_rows(sources, rows, pieces, grads, sems, False, half * group)

    def build(first, taps):
        for f in range(chunk):
            frame = grads[jnp.minimum(first + f, slots - 1)]
            for t, tap in enumerate(pixel_taps(frame, masks)):
                taps[t * group : (t + 1) * group, f * PIXELS : (f + 1) * PIXELS] = tap

    def multiply(first, taps):
        parts = []
        for d in range(3):
            row = []
            for f in range(chunk):
                slot = first + f
                frame = seen[jnp.clip(slot - d, 0, slots - 1)]
                row.append(jnp.where(ages[slot] >= d, frame, jnp.zeros_like(frame)))
            parts.append(jnp.concatenate(row, axis=1))
        total[...] += lax.dot_general(
            jnp.concatenate(parts, axis=0),
            taps[...],
            (((1,), (1,)), ((), ())),
            preferred_element_type=jnp.float32,
        )

    build(0, even)

    def step(p, carry):
        first = 2 * p * chunk
        fetch_seen(p).wait()
        build(first + chunk, odd)
        multiply(first, even)
        build(first + 2 * chunk, even)
        multiply(first + chunk, odd)
        return carry

    def finish(p, carry):
        fetch_seen(p).wait()
        return carry

    lax.fori_loop(0, steps[0], step, 0)
    lax.fori_loop(steps[0], slots // span, finish, 0)
    chips, block = mine.shape[0], mine.shape[2]
    for j in range(chips):
        for target, side in ((mine, parity[0]), (theirs, 1 - parity[0])):
            start = pl.multiple_of((2 * j + side) * block, 8)
            for d in range(3):
                terms = total[pl.ds(d * channels + start, block), :] * scale
                target[j, 2 - d] = terms.astype(jnp.bfloat16)


def weight_part(half, halves, pieces, x, ages, sources, rows, parity, scale, count):
    slots, channels = x.shape[0], x.shape[1]
    group = pieces[0].shape[1] // halves
    chunk = 2
    assert slots % (2 * chunk) == 0
    filled = jnp.sum((ages >= 0).astype(jnp.int32))
    steps = ((filled + 2 * chunk - 1) // (2 * chunk)).reshape((1,))
    ages = jnp.concatenate([ages, jnp.full((2 * chunk,), -1, jnp.int32)])
    smem = pl.BlockSpec(memory_space=pltpu.SMEM)
    vmem = pl.BlockSpec(memory_space=pltpu.VMEM)
    anywhere = pl.BlockSpec(memory_space=pl.ANY)
    blocks = jax.ShapeDtypeStruct((count // 2, 3, channels // count, 9 * group), jnp.bfloat16)
    tap_buffer = pltpu.VMEM((9 * group, chunk * PIXELS), jnp.bfloat16)
    return pl.pallas_call(
        functools.partial(weight_kernel, chunk, scale, half),
        out_shape=(blocks, blocks),
        in_specs=[smem] * 5 + [vmem] + [anywhere] * (1 + len(pieces)),
        out_specs=(vmem, vmem),
        scratch_shapes=[
            pltpu.VMEM(x.shape, jnp.bfloat16),
            pltpu.VMEM((slots, group, PIXELS), jnp.bfloat16),
            tap_buffer,
            tap_buffer,
            pltpu.VMEM((3 * channels, 9 * group), jnp.float32),
            pltpu.SemaphoreType.DMA((slots,)),
            pltpu.SemaphoreType.DMA((slots // (2 * chunk),)),
        ],
        compiler_params=pltpu.CompilerParams(vmem_limit_bytes=32 * MIB),
        cost_estimate=pl.CostEstimate(
            flops=2 * slots * 27 * channels * group * PIXELS,
            bytes_accessed=2 * slots * channels * PIXELS,
            transcendentals=0,
        ),
        name="weight_grad_part",
    )(ages, sources, rows, parity, steps, tap_masks(), x, *pieces)


def pick_kernel(targets, *rest):
    pieces, (here, there, sems) = rest[:-3], rest[-3:]
    slots, rows = here.shape[0], pieces[0].shape[0]
    for start in (True, False):
        for p, piece in enumerate(pieces):
            for r in range(rows):
                target = targets[p * rows + r]
                sem = sems.at[p * rows + r]

                @pl.when((target >= 0) & (target < slots))
                def _():
                    copy = pltpu.make_async_copy(piece.at[r], here.at[target], sem)
                    copy.start() if start else copy.wait()

                @pl.when(target >= slots)
                def _():
                    copy = pltpu.make_async_copy(piece.at[r], there.at[target - slots], sem)
                    copy.start() if start else copy.wait()


def pick_rows(pieces, targets, slots):
    smem = pl.BlockSpec(memory_space=pltpu.SMEM)
    vmem = pl.BlockSpec(memory_space=pltpu.VMEM)
    anywhere = pl.BlockSpec(memory_space=pl.ANY)
    frames = jax.ShapeDtypeStruct((slots,) + pieces[0].shape[1:], jnp.bfloat16)
    return pl.pallas_call(
        pick_kernel,
        out_shape=(frames, frames),
        in_specs=[smem] + [anywhere] * len(pieces),
        out_specs=(vmem, vmem),
        scratch_shapes=[pltpu.SemaphoreType.DMA((targets.shape[0],))],
        compiler_params=pltpu.CompilerParams(vmem_limit_bytes=16 * MIB),
        cost_estimate=pl.CostEstimate(
            flops=0, bytes_accessed=16 * frames.size, transcendentals=0
        ),
        name="pick_rows",
    )(targets, *pieces)


def swap(value, axis, flip):
    return lax.ppermute(value, axis, [(i, i ^ flip) for i in range(lax.axis_size(axis))])


def to_chips(piece, count, late=None):
    late = piece if late is None else late
    return [piece] + [swap(late if k & (k - 1) else piece, "slab", k) for k in range(2, count, 2)]


def with_siblings(chips):
    return chips + [swap(piece, "slab", 1) for piece in chips]


def shards(
    section_activations,
    kernel_weight,
    packed_output_gradient,
    clip_length,
    clip_slab_index,
    packed_clip_order,
):
    slots, channels = section_activations.shape[:2]
    rows, group = packed_output_gradient.shape[:2]
    count, heads = lax.axis_size("slab"), lax.axis_size("head")
    me, head = lax.axis_index("slab"), lax.axis_index("head")
    each, frame = rows // heads, packed_output_gradient.shape[1:]

    after = lax.ppermute(
        packed_output_gradient[:2], "slab", [(i, (i - 1) % count) for i in range(count)]
    )
    longer = jnp.concatenate([packed_output_gradient, after], axis=0)
    windows = [
        lax.dynamic_slice_in_dim(longer, each * (head ^ k), each + 2, 0) for k in range(heads)
    ]
    piece, windows = lax.optimization_barrier((packed_output_gradient, windows))
    windows = windows[:1] + [swap(windows[k], "head", k) for k in range(1, heads)]
    late_piece, windows[1] = lax.optimization_barrier((piece, windows[1]))
    gradient_chips = to_chips(piece, count, late_piece)
    masks, windows[1] = lax.optimization_barrier((tap_masks(), windows[1]))
    masks = ask_early(masks, kernel_weight)

    encoder_offset, packed_start = clip_places(clip_length, clip_slab_index, packed_clip_order)
    parity = (me % 2).reshape((1,)).astype(jnp.int32)
    slot_age, slot_row = slot_lookup(
        clip_length, clip_slab_index, encoder_offset, packed_start, me, slots
    )
    shard, inner = jnp.maximum(slot_row, 0) // rows, jnp.maximum(slot_row, 0) % rows
    side, chip = (shard ^ me) % 2, (shard // 2) ^ (me // 2)
    source = jnp.where(slot_row >= 0, side * (count // 2) + chip, -1)
    places = head ^ jnp.arange(heads, dtype=jnp.int32)
    window_rows = rows * me + each * head + jnp.arange(each + 2, dtype=jnp.int32)
    window_age = row_ages(clip_length, packed_start, window_rows)

    parts = input_part(windows, kernel_weight, window_age, places, masks)
    parts, gradient_chips = lax.optimization_barrier((parts, gradient_chips))
    gradient_pieces = with_siblings(gradient_chips)
    sent = [lax.dynamic_index_in_dim(parts, head ^ k, 0, keepdims=False) for k in range(heads)]
    arrived = [sent[0], swap(sent[1], "head", 1)]
    arrived, sent = lax.optimization_barrier((arrived, sent))
    for k in range(2, heads):
        arrived.append(swap(sent[k], "head", k))
    width = heads // 2
    piece = jnp.concatenate(arrived[:width], axis=0)
    near = to_chips(piece, count)

    scale = 1.0 / math.sqrt(rows * count * PIXELS)
    halves = 2 if group % 32 == 0 else 1

    def weight_half(half, x):
        return weight_part(
            half, halves, gradient_pieces, x, slot_age, source, inner, parity, scale, count
        )

    x, piece = lax.optimization_barrier((section_activations, piece))
    mine, theirs = weight_half(0, x)
    mine, theirs, near, late = lax.optimization_barrier((mine, theirs, near, arrived[width:]))
    piece = jnp.concatenate(late, axis=0)
    far = to_chips(piece, count)
    mines, others = [mine], [swap(theirs, "slab", 1)]
    if halves == 2:
        x, piece = lax.optimization_barrier((x, piece))
        mine, theirs = weight_half(1, x)
        mine, far, others = lax.optimization_barrier((mine, far, others))
        mines.append(mine)
        others.append(swap(theirs, "slab", 1))

    mine, other = jnp.stack(mines, axis=1), jnp.stack(others, axis=1)
    rounded = (mine.astype(jnp.float32) + other.astype(jnp.float32)).astype(jnp.bfloat16)
    my_chip = me // 2
    weight_grad = sum(
        lax.dynamic_index_in_dim(term, my_chip, 0, keepdims=False).astype(jnp.float32)
        for term in (mine, other)
    )
    terms = []
    for k in range(1, count // 2):
        term = lax.dynamic_index_in_dim(rounded, my_chip ^ k, 0, keepdims=False)
        terms.append(swap(term, "slab", 2 * k))
    terms[0], near, far = lax.optimization_barrier((terms[0], near, far))
    for term in terms:
        weight_grad = weight_grad + term.astype(jnp.float32)
    block = channels // count
    weight_grad = weight_grad.astype(jnp.bfloat16).reshape(halves, 3, block, 9, group // halves)
    weight_grad = weight_grad.transpose(1, 3, 2, 0, 4).reshape(27, block, group)

    shape = (2, count // 2, width, each)
    stage, chip, place, row = (lax.broadcasted_iota(jnp.int32, shape, d) for d in range(4))
    shard = 2 * (chip ^ my_chip) + me % 2
    packed_row = shard * rows + ((stage * width + place) ^ head) * each + row
    slab, slot = row_slot(
        clip_length, clip_slab_index, encoder_offset, packed_start, packed_row.reshape(-1)
    )
    targets = jnp.where(slab == me, slot, jnp.where(slab == me ^ 1, slots + slot, -1))
    here, there = pick_rows(near + far, targets, slots)
    there = swap(there, "slab", 1)
    frames = jnp.where((side == 0)[:, None, None], here, there)
    input_grad = jnp.where((slot_row >= 0)[:, None, None], frames, jnp.zeros_like(frames))
    return (input_grad, weight_grad)


def solution(mesh):
    return jax.shard_map(
        shards,
        mesh=mesh,
        in_specs=(P("slab", None, None), P(), P("slab", "head", None), P(), P(), P()),
        out_specs=(P("slab", "head", None), P(None, "slab", "head")),
        check_vma=False,
    )
```

```python
import functools
import math

import jax
import jax.numpy as jnp
import numpy as np
from jax import lax
from jax.experimental import pallas as pl
from jax.experimental.pallas import tpu as pltpu
from jax.sharding import PartitionSpec as P

PIXEL_ROWS = 16
PIXEL_COLUMNS = 16
PIXELS = PIXEL_ROWS * PIXEL_COLUMNS
MIB = 1024 * 1024


def clip_places(clip_lengths, slabs, order):
    clip_ids = jnp.arange(clip_lengths.shape[0], dtype=jnp.int32)
    same_slab = slabs[None, :] == slabs[:, None]
    earlier = clip_ids[None, :] < clip_ids[:, None]
    encoder_offset = jnp.sum(jnp.where(same_slab & earlier, clip_lengths[None, :], 0), axis=1)
    matches = order[None, :] == clip_ids[:, None]
    placing = jnp.sum(jnp.where(matches, clip_ids[None, :], 0), axis=1)
    prior_frames = placing[None, :] < placing[:, None]
    packed_start = jnp.sum(jnp.where(prior_frames, clip_lengths[None, :], 0), axis=1)
    return encoder_offset, packed_start


def slot_lookup(clip_lengths, slabs, encoder_offset, packed_start, slab_number, slots):
    slot_list = jnp.arange(slots, dtype=jnp.int32)[:, None]
    lag = slot_list - encoder_offset[None, :]
    inside = (slabs[None, :] == slab_number) & (lag >= 0) & (lag < clip_lengths[None, :])
    age = jnp.sum(jnp.where(inside, lag + 1, 0), axis=1) - 1
    row = jnp.sum(jnp.where(inside, packed_start[None, :] + lag + 1, 0), axis=1) - 1
    return age, row


def row_ages(clip_lengths, packed_start, rows):
    lag = rows[:, None] - packed_start[None, :]
    inside = (lag >= 0) & (lag < clip_lengths[None, :])
    return jnp.sum(jnp.where(inside, lag + 1, 0), axis=1) - 1


def row_slot(clip_lengths, slabs, encoder_offset, packed_start, rows):
    lag = rows[:, None] - packed_start[None, :]
    inside = (lag >= 0) & (lag < clip_lengths[None, :])
    slab = jnp.sum(jnp.where(inside, slabs[None, :], 0), axis=1)
    slot = jnp.sum(jnp.where(inside, encoder_offset[None, :] + lag, 0), axis=1)
    return slab, slot


def tap_offsets():
    return [(1 - row_tap, 1 - col_tap) for row_tap in range(3) for col_tap in range(3)]


def tap_masks():
    row, column = np.divmod(np.arange(PIXELS), PIXEL_COLUMNS)
    masks = []
    for row_step, col_step in tap_offsets():
        good = (0 <= row + row_step) & (row + row_step < PIXEL_ROWS)
        good &= (0 <= column + col_step) & (column + col_step < PIXEL_COLUMNS)
        masks.append(np.broadcast_to(good, (16, PIXELS)))
    return jnp.asarray(np.stack(masks), jnp.bfloat16)


def pixel_taps(frame, masks):
    taps = []
    for t, (row_step, col_step) in enumerate(tap_offsets()):
        offset = row_step * PIXEL_COLUMNS + col_step
        if offset:
            moved = pltpu.roll(frame, (-offset) % PIXELS, 1).reshape(-1, 16, PIXELS)
            taps.append((moved * masks[t][None]).reshape(frame.shape))
        else:
            taps.append(frame)
    return taps


def input_kernel(heads, ages, places, masks, weight, *rest):
    pieces, (out, windows, taps, sems) = rest[:heads], rest[heads:]
    frames, group = out.shape[1:3]
    channels = heads * group
    copies = [
        pltpu.make_async_copy(pieces[k], windows.at[places[k]], sems.at[k]) for k in range(heads)
    ]
    for copy in copies:
        copy.start()
    for copy in copies:
        copy.wait()
    for r in range(frames + 2):
        for g in range(heads):
            for t, tap in enumerate(pixel_taps(windows[g, r], masks)):
                start = t * channels + g * group
                taps[r, start : start + group, :] = tap
        f = r - 2
        if f < 0:
            continue
        total = None
        for d in range(3):
            kernel = jnp.concatenate([weight[9 * (2 - d) + t] for t in range(9)], axis=1)
            term = jnp.dot(kernel, taps[f + d], preferred_element_type=jnp.float32)
            if d == 0:
                total = term
            else:
                total = total + jnp.where(ages[f + d] >= d, term, 0.0)
        for g in range(heads):
            out[g, f] = total[g * group : (g + 1) * group, :].astype(jnp.bfloat16)


def input_part(pieces, weight, ages, places, masks):
    heads = len(pieces)
    frames, group = pieces[0].shape[0] - 2, pieces[0].shape[1]
    channels = heads * group
    smem = pl.BlockSpec(memory_space=pltpu.SMEM)
    vmem = pl.BlockSpec(memory_space=pltpu.VMEM)
    anywhere = pl.BlockSpec(memory_space=pl.ANY)
    return pl.pallas_call(
        functools.partial(input_kernel, heads),
        out_shape=jax.ShapeDtypeStruct((heads, frames, group, PIXELS), jnp.bfloat16),
        in_specs=[smem, smem, vmem, vmem] + [anywhere] * heads,
        out_specs=vmem,
        scratch_shapes=[
            pltpu.VMEM((heads, frames + 2, group, PIXELS), jnp.bfloat16),
            pltpu.VMEM((frames + 2, 9 * channels, PIXELS), jnp.bfloat16),
            pltpu.SemaphoreType.DMA((heads,)),
        ],
        compiler_params=pltpu.CompilerParams(vmem_limit_bytes=32 * MIB),
        cost_estimate=pl.CostEstimate(
            flops=2 * frames * 27 * channels * channels * PIXELS,
            bytes_accessed=2 * 27 * channels * channels,
            transcendentals=0,
        ),
        name="input_grad_part",
    )(ages, places, masks, weight, *pieces)


def early_kernel(masks, weight, out):
    out[...] = masks[...]


def ask_early(masks, weight):
    vmem = pl.BlockSpec(memory_space=pltpu.VMEM)
    return pl.pallas_call(
        early_kernel,
        out_shape=jax.ShapeDtypeStruct(masks.shape, masks.dtype),
        in_specs=[vmem, vmem],
        out_specs=vmem,
        compiler_params=pltpu.CompilerParams(vmem_limit_bytes=16 * MIB),
        name="ask_early",
    )(masks, weight)


def fetch_rows(sources, rows, pieces, target, sems, start, first=0):
    def slot(j, carry):
        if start:
            for p, piece in enumerate(pieces):

                @pl.when(sources[j] == p)
                def _():
                    row = piece.at[rows[j], pl.ds(first, target.shape[1])]
                    pltpu.make_async_copy(row, target.at[j], sems.at[j]).start()

        else:

            @pl.when(sources[j] >= 0)
            def _():
                row = pieces[0].at[0, pl.ds(first, target.shape[1])]
                pltpu.make_async_copy(row, target.at[j], sems.at[j]).wait()

        return carry

    lax.fori_loop(0, target.shape[0], slot, 0)


def blank_rows(sources, target):
    def slot(j, carry):
        @pl.when(sources[j] < 0)
        def _():
            target[j] = jnp.zeros(target.shape[1:], target.dtype)

        return carry

    lax.fori_loop(0, target.shape[0], slot, 0)


def weight_kernel(chunk, scale, half, ages, sources, rows, parity, steps, masks, x, *rest):
    pieces, rest = rest[:-9], rest[-9:]
    mine, theirs, seen, grads, even, odd, total, sems, seen_sems = rest
    slots, group = grads.shape[0], grads.shape[1]
    channels = x.shape[1]
    span = 2 * chunk

    def fetch_seen(p):
        part = pl.ds(p * span, span)
        return pltpu.make_async_copy(x.at[part], seen.at[part], seen_sems.at[p])

    fetch_rows(sources, rows, pieces, grads, sems, True, half * group)
    for p in range(slots // span):
        fetch_seen(p).start()
    total[...] = jnp.zeros_like(total)
    blank_rows(sources, grads)
    fetch_rows(sources, rows, pieces, grads, sems, False, half * group)

    def build(first, taps):
        for f in range(chunk):
            frame = grads[jnp.minimum(first + f, slots - 1)]
            for t, tap in enumerate(pixel_taps(frame, masks)):
                taps[t * group : (t + 1) * group, f * PIXELS : (f + 1) * PIXELS] = tap

    def multiply(first, taps):
        parts = []
        for d in range(3):
            row = []
            for f in range(chunk):
                slot = first + f
                frame = seen[jnp.clip(slot - d, 0, slots - 1)]
                row.append(jnp.where(ages[slot] >= d, frame, jnp.zeros_like(frame)))
            parts.append(jnp.concatenate(row, axis=1))
        total[...] += lax.dot_general(
            jnp.concatenate(parts, axis=0),
            taps[...],
            (((1,), (1,)), ((), ())),
            preferred_element_type=jnp.float32,
        )

    build(0, even)

    def step(p, carry):
        first = 2 * p * chunk
        fetch_seen(p).wait()
        build(first + chunk, odd)
        multiply(first, even)
        build(first + 2 * chunk, even)
        multiply(first + chunk, odd)
        return carry

    def finish(p, carry):
        fetch_seen(p).wait()
        return carry

    lax.fori_loop(0, steps[0], step, 0)
    lax.fori_loop(steps[0], slots // span, finish, 0)
    chips, block = mine.shape[0], mine.shape[2]
    for j in range(chips):
        for target, side in ((mine, parity[0]), (theirs, 1 - parity[0])):
            start = pl.multiple_of((2 * j + side) * block, 8)
            for d in range(3):
                terms = total[pl.ds(d * channels + start, block), :] * scale
                target[j, 2 - d] = terms.astype(jnp.bfloat16)


def weight_part(half, halves, pieces, x, ages, sources, rows, parity, scale, count):
    slots, channels = x.shape[0], x.shape[1]
    group = pieces[0].shape[1] // halves
    chunk = 2
    assert slots % (2 * chunk) == 0
    filled = jnp.sum((ages >= 0).astype(jnp.int32))
    steps = ((filled + 2 * chunk - 1) // (2 * chunk)).reshape((1,))
    ages = jnp.concatenate([ages, jnp.full((2 * chunk,), -1, jnp.int32)])
    smem = pl.BlockSpec(memory_space=pltpu.SMEM)
    vmem = pl.BlockSpec(memory_space=pltpu.VMEM)
    anywhere = pl.BlockSpec(memory_space=pl.ANY)
    blocks = jax.ShapeDtypeStruct((count // 2, 3, channels // count, 9 * group), jnp.bfloat16)
    tap_buffer = pltpu.VMEM((9 * group, chunk * PIXELS), jnp.bfloat16)
    return pl.pallas_call(
        functools.partial(weight_kernel, chunk, scale, half),
        out_shape=(blocks, blocks),
        in_specs=[smem] * 5 + [vmem] + [anywhere] * (1 + len(pieces)),
        out_specs=(vmem, vmem),
        scratch_shapes=[
            pltpu.VMEM(x.shape, jnp.bfloat16),
            pltpu.VMEM((slots, group, PIXELS), jnp.bfloat16),
            tap_buffer,
            tap_buffer,
            pltpu.VMEM((3 * channels, 9 * group), jnp.float32),
            pltpu.SemaphoreType.DMA((slots,)),
            pltpu.SemaphoreType.DMA((slots // (2 * chunk),)),
        ],
        compiler_params=pltpu.CompilerParams(vmem_limit_bytes=32 * MIB),
        cost_estimate=pl.CostEstimate(
            flops=2 * slots * 27 * channels * group * PIXELS,
            bytes_accessed=2 * slots * channels * PIXELS,
            transcendentals=0,
        ),
        name="weight_grad_part",
    )(ages, sources, rows, parity, steps, tap_masks(), x, *pieces)


def pick_kernel(targets, *rest):
    pieces, (here, there, sems) = rest[:-3], rest[-3:]
    slots, rows = here.shape[0], pieces[0].shape[0]
    for start in (True, False):
        for p, piece in enumerate(pieces):
            for r in range(rows):
                target = targets[p * rows + r]
                sem = sems.at[p * rows + r]

                @pl.when((target >= 0) & (target < slots))
                def _():
                    copy = pltpu.make_async_copy(piece.at[r], here.at[target], sem)
                    copy.start() if start else copy.wait()

                @pl.when(target >= slots)
                def _():
                    copy = pltpu.make_async_copy(piece.at[r], there.at[target - slots], sem)
                    copy.start() if start else copy.wait()


def pick_rows(pieces, targets, slots):
    smem = pl.BlockSpec(memory_space=pltpu.SMEM)
    vmem = pl.BlockSpec(memory_space=pltpu.VMEM)
    anywhere = pl.BlockSpec(memory_space=pl.ANY)
    frames = jax.ShapeDtypeStruct((slots,) + pieces[0].shape[1:], jnp.bfloat16)
    return pl.pallas_call(
        pick_kernel,
        out_shape=(frames, frames),
        in_specs=[smem] + [anywhere] * len(pieces),
        out_specs=(vmem, vmem),
        scratch_shapes=[pltpu.SemaphoreType.DMA((targets.shape[0],))],
        compiler_params=pltpu.CompilerParams(vmem_limit_bytes=60 * MIB),
        cost_estimate=pl.CostEstimate(
            flops=0, bytes_accessed=16 * frames.size, transcendentals=0
        ),
        name="pick_rows",
    )(targets, *pieces)


def swap(value, axis, flip):
    return lax.ppermute(value, axis, [(i, i ^ flip) for i in range(lax.axis_size(axis))])


def to_chips(piece, count, late=None):
    late = piece if late is None else late
    return [piece] + [swap(late if k & (k - 1) else piece, "slab", k) for k in range(2, count, 2)]


def with_siblings(chips):
    return chips + [swap(piece, "slab", 1) for piece in chips]


def shards(
    section_activations,
    kernel_weight,
    packed_output_gradient,
    clip_length,
    clip_slab_index,
    packed_clip_order,
):
    slots, channels = section_activations.shape[:2]
    rows, group = packed_output_gradient.shape[:2]
    count, heads = lax.axis_size("slab"), lax.axis_size("head")
    me, head = lax.axis_index("slab"), lax.axis_index("head")
    each, frame = rows // heads, packed_output_gradient.shape[1:]

    after = lax.ppermute(
        packed_output_gradient[:2], "slab", [(i, (i - 1) % count) for i in range(count)]
    )
    longer = jnp.concatenate([packed_output_gradient, after], axis=0)
    windows = [
        lax.dynamic_slice_in_dim(longer, each * (head ^ k), each + 2, 0) for k in range(heads)
    ]
    piece, windows = lax.optimization_barrier((packed_output_gradient, windows))
    windows = windows[:1] + [swap(windows[k], "head", k) for k in range(1, heads)]
    late_piece, windows[1] = lax.optimization_barrier((piece, windows[1]))
    gradient_chips = to_chips(piece, count, late_piece)
    masks, windows[1] = lax.optimization_barrier((tap_masks(), windows[1]))
    masks = ask_early(masks, kernel_weight)

    encoder_offset, packed_start = clip_places(clip_length, clip_slab_index, packed_clip_order)
    parity = (me % 2).reshape((1,)).astype(jnp.int32)
    slot_age, slot_row = slot_lookup(
        clip_length, clip_slab_index, encoder_offset, packed_start, me, slots
    )
    shard, inner = jnp.maximum(slot_row, 0) // rows, jnp.maximum(slot_row, 0) % rows
    side, chip = (shard ^ me) % 2, (shard // 2) ^ (me // 2)
    source = jnp.where(slot_row >= 0, side * (count // 2) + chip, -1)
    places = head ^ jnp.arange(heads, dtype=jnp.int32)
    window_rows = rows * me + each * head + jnp.arange(each + 2, dtype=jnp.int32)
    window_age = row_ages(clip_length, packed_start, window_rows)

    parts = input_part(windows, kernel_weight, window_age, places, masks)
    parts, gradient_chips[2:] = lax.optimization_barrier((parts, gradient_chips[2:]))
    gradient_pieces = with_siblings(gradient_chips)
    sent = [lax.dynamic_index_in_dim(parts, head ^ k, 0, keepdims=False) for k in range(heads)]
    arrived = sent[:1] + [swap(sent[k], "head", k) for k in range(1, heads)]

    scale = 1.0 / math.sqrt(rows * count * PIXELS)
    halves = 2 if group % 32 == 0 else 1

    def weight_half(half, x):
        return weight_part(
            half, halves, gradient_pieces, x, slot_age, source, inner, parity, scale, count
        )

    x, sent = lax.optimization_barrier((section_activations, sent))
    mine, theirs = weight_half(0, x)
    mine, theirs, arrived = lax.optimization_barrier((mine, theirs, arrived))
    piece = jnp.concatenate(arrived, axis=0)
    chips = to_chips(piece, count)
    mines, others = [mine], [swap(theirs, "slab", 1)]
    if halves == 2:
        x, piece = lax.optimization_barrier((x, piece))
        mine, theirs = weight_half(1, x)
        mine, chips, others = lax.optimization_barrier((mine, chips, others))
        mines.append(mine)
        others.append(swap(theirs, "slab", 1))

    mine, other = jnp.stack(mines, axis=1), jnp.stack(others, axis=1)
    rounded = (mine.astype(jnp.float32) + other.astype(jnp.float32)).astype(jnp.bfloat16)
    rounded, chips = lax.optimization_barrier((rounded, chips))
    my_chip = me // 2
    weight_grad = sum(
        lax.dynamic_index_in_dim(term, my_chip, 0, keepdims=False).astype(jnp.float32)
        for term in (mine, other)
    )
    terms = []
    for k in range(1, count // 2):
        term = lax.dynamic_index_in_dim(rounded, my_chip ^ k, 0, keepdims=False)
        terms.append(swap(term, "slab", 2 * k))
    for term in terms:
        weight_grad = weight_grad + term.astype(jnp.float32)
    block = channels // count
    weight_grad = weight_grad.astype(jnp.bfloat16).reshape(halves, 3, block, 9, group // halves)
    weight_grad = weight_grad.transpose(1, 3, 2, 0, 4).reshape(27, block, group)

    shape = (count // 2, heads, each)
    chip, place, row = (lax.broadcasted_iota(jnp.int32, shape, d) for d in range(3))
    packed_row = (2 * (chip ^ my_chip) + me % 2) * rows + (place ^ head) * each + row
    slab, slot = row_slot(
        clip_length, clip_slab_index, encoder_offset, packed_start, packed_row.reshape(-1)
    )
    targets = jnp.where(slab == me, slot, jnp.where(slab == me ^ 1, slots + slot, -1))
    here, there = pick_rows(chips, targets, slots)
    there = swap(there, "slab", 1)
    frames = jnp.where((side == 0)[:, None, None], here, there)
    input_grad = jnp.where((slot_row >= 0)[:, None, None], frames, jnp.zeros_like(frames))
    return (input_grad, weight_grad)


def solution(mesh):
    return jax.shard_map(
        shards,
        mesh=mesh,
        in_specs=(P("slab", None, None), P(), P("slab", "head", None), P(), P(), P()),
        out_specs=(P("slab", "head", None), P(None, "slab", "head")),
        check_vma=False,
    )
```

```python
import functools
import math

import jax
import jax.numpy as jnp
import numpy as np
from jax import lax
from jax.experimental import pallas as pl
from jax.experimental.pallas import tpu as pltpu
from jax.sharding import PartitionSpec as P

PIXEL_ROWS = 16
PIXEL_COLUMNS = 16
PIXELS = PIXEL_ROWS * PIXEL_COLUMNS
MIB = 1024 * 1024


def clip_places(clip_lengths, slabs, order):
    clip_ids = jnp.arange(clip_lengths.shape[0], dtype=jnp.int32)
    same_slab = slabs[None, :] == slabs[:, None]
    earlier = clip_ids[None, :] < clip_ids[:, None]
    encoder_offset = jnp.sum(jnp.where(same_slab & earlier, clip_lengths[None, :], 0), axis=1)
    matches = order[None, :] == clip_ids[:, None]
    placing = jnp.sum(jnp.where(matches, clip_ids[None, :], 0), axis=1)
    prior_frames = placing[None, :] < placing[:, None]
    packed_start = jnp.sum(jnp.where(prior_frames, clip_lengths[None, :], 0), axis=1)
    return encoder_offset, packed_start


def slot_lookup(clip_lengths, slabs, encoder_offset, packed_start, slab_number, slots):
    slot_list = jnp.arange(slots, dtype=jnp.int32)[:, None]
    lag = slot_list - encoder_offset[None, :]
    inside = (slabs[None, :] == slab_number) & (lag >= 0) & (lag < clip_lengths[None, :])
    age = jnp.sum(jnp.where(inside, lag + 1, 0), axis=1) - 1
    row = jnp.sum(jnp.where(inside, packed_start[None, :] + lag + 1, 0), axis=1) - 1
    return age, row


def row_ages(clip_lengths, packed_start, rows):
    lag = rows[:, None] - packed_start[None, :]
    inside = (lag >= 0) & (lag < clip_lengths[None, :])
    return jnp.sum(jnp.where(inside, lag + 1, 0), axis=1) - 1


def row_slot(clip_lengths, slabs, encoder_offset, packed_start, rows):
    lag = rows[:, None] - packed_start[None, :]
    inside = (lag >= 0) & (lag < clip_lengths[None, :])
    slab = jnp.sum(jnp.where(inside, slabs[None, :], 0), axis=1)
    slot = jnp.sum(jnp.where(inside, encoder_offset[None, :] + lag, 0), axis=1)
    return slab, slot


def tap_offsets():
    return [(1 - row_tap, 1 - col_tap) for row_tap in range(3) for col_tap in range(3)]


def tap_masks():
    row, column = np.divmod(np.arange(PIXELS), PIXEL_COLUMNS)
    masks = []
    for row_step, col_step in tap_offsets():
        good = (0 <= row + row_step) & (row + row_step < PIXEL_ROWS)
        good &= (0 <= column + col_step) & (column + col_step < PIXEL_COLUMNS)
        masks.append(np.broadcast_to(good, (16, PIXELS)))
    return jnp.asarray(np.stack(masks), jnp.bfloat16)


def pixel_taps(frame, masks):
    taps = []
    for t, (row_step, col_step) in enumerate(tap_offsets()):
        offset = row_step * PIXEL_COLUMNS + col_step
        if offset:
            moved = pltpu.roll(frame, (-offset) % PIXELS, 1).reshape(-1, 16, PIXELS)
            taps.append((moved * masks[t][None]).reshape(frame.shape))
        else:
            taps.append(frame)
    return taps


def input_kernel(heads, ages, places, masks, weight, *rest):
    pieces, (out, windows, taps, sems) = rest[:heads], rest[heads:]
    frames, group = out.shape[1:3]
    channels = heads * group
    copies = [
        pltpu.make_async_copy(pieces[k], windows.at[places[k]], sems.at[k]) for k in range(heads)
    ]
    for copy in copies:
        copy.start()
    for copy in copies:
        copy.wait()
    for r in range(frames + 2):
        for g in range(heads):
            for t, tap in enumerate(pixel_taps(windows[g, r], masks)):
                start = t * channels + g * group
                taps[r, start : start + group, :] = tap
        f = r - 2
        if f < 0:
            continue
        total = None
        for d in range(3):
            kernel = jnp.concatenate([weight[9 * (2 - d) + t] for t in range(9)], axis=1)
            term = jnp.dot(kernel, taps[f + d], preferred_element_type=jnp.float32)
            if d == 0:
                total = term
            else:
                total = total + jnp.where(ages[f + d] >= d, term, 0.0)
        for g in range(heads):
            out[g, f] = total[g * group : (g + 1) * group, :].astype(jnp.bfloat16)


def input_part(pieces, weight, ages, places, masks):
    heads = len(pieces)
    frames, group = pieces[0].shape[0] - 2, pieces[0].shape[1]
    channels = heads * group
    smem = pl.BlockSpec(memory_space=pltpu.SMEM)
    vmem = pl.BlockSpec(memory_space=pltpu.VMEM)
    anywhere = pl.BlockSpec(memory_space=pl.ANY)
    return pl.pallas_call(
        functools.partial(input_kernel, heads),
        out_shape=jax.ShapeDtypeStruct((heads, frames, group, PIXELS), jnp.bfloat16),
        in_specs=[smem, smem, vmem, vmem] + [anywhere] * heads,
        out_specs=vmem,
        scratch_shapes=[
            pltpu.VMEM((heads, frames + 2, group, PIXELS), jnp.bfloat16),
            pltpu.VMEM((frames + 2, 9 * channels, PIXELS), jnp.bfloat16),
            pltpu.SemaphoreType.DMA((heads,)),
        ],
        compiler_params=pltpu.CompilerParams(vmem_limit_bytes=32 * MIB),
        cost_estimate=pl.CostEstimate(
            flops=2 * frames * 27 * channels * channels * PIXELS,
            bytes_accessed=2 * 27 * channels * channels,
            transcendentals=0,
        ),
        name="input_grad_part",
    )(ages, places, masks, weight, *pieces)


def early_kernel(masks, weight, out):
    out[...] = masks[...]


def ask_early(masks, weight):
    vmem = pl.BlockSpec(memory_space=pltpu.VMEM)
    return pl.pallas_call(
        early_kernel,
        out_shape=jax.ShapeDtypeStruct(masks.shape, masks.dtype),
        in_specs=[vmem, vmem],
        out_specs=vmem,
        compiler_params=pltpu.CompilerParams(vmem_limit_bytes=16 * MIB),
        name="ask_early",
    )(masks, weight)


def fetch_rows(sources, rows, pieces, target, sems, start, first=0):
    def slot(j, carry):
        if start:
            for p, piece in enumerate(pieces):

                @pl.when(sources[j] == p)
                def _():
                    row = piece.at[rows[j], pl.ds(first, target.shape[1])]
                    pltpu.make_async_copy(row, target.at[j], sems.at[j]).start()

        else:

            @pl.when(sources[j] >= 0)
            def _():
                row = pieces[0].at[0, pl.ds(first, target.shape[1])]
                pltpu.make_async_copy(row, target.at[j], sems.at[j]).wait()

        return carry

    lax.fori_loop(0, target.shape[0], slot, 0)


def blank_rows(sources, target):
    def slot(j, carry):
        @pl.when(sources[j] < 0)
        def _():
            target[j] = jnp.zeros(target.shape[1:], target.dtype)

        return carry

    lax.fori_loop(0, target.shape[0], slot, 0)


def weight_kernel(chunk, scale, half, ages, sources, rows, parity, steps, masks, x, *rest):
    pieces, rest = rest[:-9], rest[-9:]
    mine, theirs, seen, grads, even, odd, total, sems, seen_sems = rest
    slots, group = grads.shape[0], grads.shape[1]
    channels = x.shape[1]
    span = 2 * chunk

    def fetch_seen(p):
        part = pl.ds(p * span, span)
        return pltpu.make_async_copy(x.at[part], seen.at[part], seen_sems.at[p])

    fetch_rows(sources, rows, pieces, grads, sems, True, half * group)
    for p in range(slots // span):
        fetch_seen(p).start()
    total[...] = jnp.zeros_like(total)
    blank_rows(sources, grads)
    fetch_rows(sources, rows, pieces, grads, sems, False, half * group)

    def build(first, taps):
        for f in range(chunk):
            frame = grads[jnp.minimum(first + f, slots - 1)]
            for t, tap in enumerate(pixel_taps(frame, masks)):
                taps[t * group : (t + 1) * group, f * PIXELS : (f + 1) * PIXELS] = tap

    def multiply(first, taps):
        parts = []
        for d in range(3):
            row = []
            for f in range(chunk):
                slot = first + f
                frame = seen[jnp.clip(slot - d, 0, slots - 1)]
                row.append(jnp.where(ages[slot] >= d, frame, jnp.zeros_like(frame)))
            parts.append(jnp.concatenate(row, axis=1))
        total[...] += lax.dot_general(
            jnp.concatenate(parts, axis=0),
            taps[...],
            (((1,), (1,)), ((), ())),
            preferred_element_type=jnp.float32,
        )

    build(0, even)

    def step(p, carry):
        first = 2 * p * chunk
        fetch_seen(p).wait()
        build(first + chunk, odd)
        multiply(first, even)
        build(first + 2 * chunk, even)
        multiply(first + chunk, odd)
        return carry

    def finish(p, carry):
        fetch_seen(p).wait()
        return carry

    lax.fori_loop(0, steps[0], step, 0)
    lax.fori_loop(steps[0], slots // span, finish, 0)
    chips, block = mine.shape[0], mine.shape[2]
    for j in range(chips):
        for target, side in ((mine, parity[0]), (theirs, 1 - parity[0])):
            start = pl.multiple_of((2 * j + side) * block, 8)
            for d in range(3):
                terms = total[pl.ds(d * channels + start, block), :] * scale
                target[j, 2 - d] = terms.astype(jnp.bfloat16)


def weight_part(half, halves, pieces, x, ages, sources, rows, parity, scale, count):
    slots, channels = x.shape[0], x.shape[1]
    group = pieces[0].shape[1] // halves
    chunk = 2
    assert slots % (2 * chunk) == 0
    filled = jnp.sum((ages >= 0).astype(jnp.int32))
    steps = ((filled + 2 * chunk - 1) // (2 * chunk)).reshape((1,))
    ages = jnp.concatenate([ages, jnp.full((2 * chunk,), -1, jnp.int32)])
    smem = pl.BlockSpec(memory_space=pltpu.SMEM)
    vmem = pl.BlockSpec(memory_space=pltpu.VMEM)
    anywhere = pl.BlockSpec(memory_space=pl.ANY)
    blocks = jax.ShapeDtypeStruct((count // 2, 3, channels // count, 9 * group), jnp.bfloat16)
    tap_buffer = pltpu.VMEM((9 * group, chunk * PIXELS), jnp.bfloat16)
    return pl.pallas_call(
        functools.partial(weight_kernel, chunk, scale, half),
        out_shape=(blocks, blocks),
        in_specs=[smem] * 5 + [vmem] + [anywhere] * (1 + len(pieces)),
        out_specs=(vmem, vmem),
        scratch_shapes=[
            pltpu.VMEM(x.shape, jnp.bfloat16),
            pltpu.VMEM((slots, group, PIXELS), jnp.bfloat16),
            tap_buffer,
            tap_buffer,
            pltpu.VMEM((3 * channels, 9 * group), jnp.float32),
            pltpu.SemaphoreType.DMA((slots,)),
            pltpu.SemaphoreType.DMA((slots // (2 * chunk),)),
        ],
        compiler_params=pltpu.CompilerParams(vmem_limit_bytes=59 * MIB),
        cost_estimate=pl.CostEstimate(
            flops=2 * slots * 27 * channels * group * PIXELS,
            bytes_accessed=2 * slots * channels * PIXELS,
            transcendentals=0,
        ),
        name="weight_grad_part",
    )(ages, sources, rows, parity, steps, tap_masks(), x, *pieces)


def pick_kernel(targets, *rest):
    pieces, (here, there, sems) = rest[:-3], rest[-3:]
    slots, rows = here.shape[0], pieces[0].shape[0]
    for start in (True, False):
        for p, piece in enumerate(pieces):
            for r in range(rows):
                target = targets[p * rows + r]
                sem = sems.at[p * rows + r]

                @pl.when((target >= 0) & (target < slots))
                def _():
                    copy = pltpu.make_async_copy(piece.at[r], here.at[target], sem)
                    copy.start() if start else copy.wait()

                @pl.when(target >= slots)
                def _():
                    copy = pltpu.make_async_copy(piece.at[r], there.at[target - slots], sem)
                    copy.start() if start else copy.wait()


def pick_rows(pieces, targets, slots):
    smem = pl.BlockSpec(memory_space=pltpu.SMEM)
    vmem = pl.BlockSpec(memory_space=pltpu.VMEM)
    anywhere = pl.BlockSpec(memory_space=pl.ANY)
    frames = jax.ShapeDtypeStruct((slots,) + pieces[0].shape[1:], jnp.bfloat16)
    return pl.pallas_call(
        pick_kernel,
        out_shape=(frames, frames),
        in_specs=[smem] + [anywhere] * len(pieces),
        out_specs=(vmem, vmem),
        scratch_shapes=[pltpu.SemaphoreType.DMA((targets.shape[0],))],
        compiler_params=pltpu.CompilerParams(vmem_limit_bytes=60 * MIB),
        cost_estimate=pl.CostEstimate(
            flops=0, bytes_accessed=16 * frames.size, transcendentals=0
        ),
        name="pick_rows",
    )(targets, *pieces)


def swap(value, axis, flip):
    return lax.ppermute(value, axis, [(i, i ^ flip) for i in range(lax.axis_size(axis))])


def to_chips(piece, count, late=None):
    late = piece if late is None else late
    return [piece] + [swap(late if k & (k - 1) else piece, "slab", k) for k in range(2, count, 2)]


def joined(parts):
    shape = (len(parts),) + parts[0].shape
    place = lax.broadcasted_iota(jnp.int32, shape, 0)
    whole = jnp.broadcast_to(parts[0][None], shape)
    for k, part in enumerate(parts[1:], 1):
        whole = jnp.where(place == k, part[None], whole)
    return whole.reshape((-1,) + shape[2:])


def with_siblings(chips):
    return chips + [swap(piece, "slab", 1) for piece in chips]


def shards(
    section_activations,
    kernel_weight,
    packed_output_gradient,
    clip_length,
    clip_slab_index,
    packed_clip_order,
):
    slots, channels = section_activations.shape[:2]
    rows, group = packed_output_gradient.shape[:2]
    count, heads = lax.axis_size("slab"), lax.axis_size("head")
    me, head = lax.axis_index("slab"), lax.axis_index("head")
    each, frame = rows // heads, packed_output_gradient.shape[1:]

    after = lax.ppermute(
        packed_output_gradient[:2], "slab", [(i, (i - 1) % count) for i in range(count)]
    )
    longer = jnp.concatenate([packed_output_gradient, after], axis=0)
    windows = [
        lax.dynamic_slice_in_dim(longer, each * (head ^ k), each + 2, 0) for k in range(heads)
    ]
    piece, windows = lax.optimization_barrier((packed_output_gradient, windows))
    windows = windows[:1] + [swap(windows[k], "head", k) for k in range(1, heads)]
    late_piece, windows[1] = lax.optimization_barrier((piece, windows[1]))
    gradient_chips = to_chips(piece, count, late_piece)
    masks, windows[1] = lax.optimization_barrier((tap_masks(), windows[1]))
    masks = ask_early(masks, kernel_weight)

    encoder_offset, packed_start = clip_places(clip_length, clip_slab_index, packed_clip_order)
    parity = (me % 2).reshape((1,)).astype(jnp.int32)
    slot_age, slot_row = slot_lookup(
        clip_length, clip_slab_index, encoder_offset, packed_start, me, slots
    )
    shard, inner = jnp.maximum(slot_row, 0) // rows, jnp.maximum(slot_row, 0) % rows
    side, chip = (shard ^ me) % 2, (shard // 2) ^ (me // 2)
    source = jnp.where(slot_row >= 0, side * (count // 2) + chip, -1)
    places = head ^ jnp.arange(heads, dtype=jnp.int32)
    window_rows = rows * me + each * head + jnp.arange(each + 2, dtype=jnp.int32)
    window_age = row_ages(clip_length, packed_start, window_rows)

    parts = input_part(windows, kernel_weight, window_age, places, masks)
    parts, gradient_chips[2:] = lax.optimization_barrier((parts, gradient_chips[2:]))
    gradient_pieces = with_siblings(gradient_chips)
    sent = [lax.dynamic_index_in_dim(parts, head ^ k, 0, keepdims=False) for k in range(heads)]
    arrived = sent[:1] + [swap(sent[k], "head", k) for k in range(1, heads)]

    scale = 1.0 / math.sqrt(rows * count * PIXELS)
    halves = 2 if group % 32 == 0 else 1

    def weight_half(half, x):
        return weight_part(
            half, halves, gradient_pieces, x, slot_age, source, inner, parity, scale, count
        )

    x, sent = lax.optimization_barrier((section_activations, sent))
    mine, theirs = weight_half(0, x)
    mine, theirs, arrived = lax.optimization_barrier((mine, theirs, arrived))
    chips = to_chips(joined(arrived), count)
    mines, others = [mine], [swap(theirs, "slab", 1)]
    if halves == 2:
        x, chips[0], others = lax.optimization_barrier((x, chips[0], others))
        mine, theirs = weight_half(1, x)
        mine, chips[:3], others = lax.optimization_barrier((mine, chips[:3], others))
        mines.append(mine)
        others.append(swap(theirs, "slab", 1))

    mine, other = jnp.stack(mines, axis=1), jnp.stack(others, axis=1)
    rounded = (mine.astype(jnp.float32) + other.astype(jnp.float32)).astype(jnp.bfloat16)
    my_chip = me // 2
    weight_grad = sum(
        lax.dynamic_index_in_dim(term, my_chip, 0, keepdims=False).astype(jnp.float32)
        for term in (mine, other)
    )
    terms = []
    for k in range(1, count // 2):
        term = lax.dynamic_index_in_dim(rounded, my_chip ^ k, 0, keepdims=False)
        terms.append(swap(term, "slab", 2 * k))
    terms, chips = lax.optimization_barrier((terms, chips))
    for term in terms:
        weight_grad = weight_grad + term.astype(jnp.float32)
    block = channels // count
    weight_grad = weight_grad.astype(jnp.bfloat16).reshape(halves, 3, block, 9, group // halves)
    weight_grad = weight_grad.transpose(1, 3, 2, 0, 4).reshape(27, block, group)

    shape = (count // 2, heads, each)
    chip, place, row = (lax.broadcasted_iota(jnp.int32, shape, d) for d in range(3))
    packed_row = (2 * (chip ^ my_chip) + me % 2) * rows + (place ^ head) * each + row
    slab, slot = row_slot(
        clip_length, clip_slab_index, encoder_offset, packed_start, packed_row.reshape(-1)
    )
    targets = jnp.where(slab == me, slot, jnp.where(slab == me ^ 1, slots + slot, -1))
    here, there = pick_rows(chips, targets, slots)
    there = swap(there, "slab", 1)
    frames = jnp.where((side == 0)[:, None, None], here, there)
    input_grad = jnp.where((slot_row >= 0)[:, None, None], frames, jnp.zeros_like(frames))
    return (input_grad, weight_grad)


def solution(mesh):
    return jax.shard_map(
        shards,
        mesh=mesh,
        in_specs=(P("slab", None, None), P(), P("slab", "head", None), P(), P(), P()),
        out_specs=(P("slab", "head", None), P(None, "slab", "head")),
        check_vma=False,
    )
```

```python
import functools
import math

import jax
import jax.numpy as jnp
import numpy as np
from jax import lax
from jax.experimental import pallas as pl
from jax.experimental.pallas import tpu as pltpu
from jax.sharding import PartitionSpec as P

PIXEL_ROWS = 16
PIXEL_COLUMNS = 16
PIXELS = PIXEL_ROWS * PIXEL_COLUMNS
MIB = 1024 * 1024


def clip_places(clip_lengths, slabs, order):
    clip_ids = jnp.arange(clip_lengths.shape[0], dtype=jnp.int32)
    same_slab = slabs[None, :] == slabs[:, None]
    earlier = clip_ids[None, :] < clip_ids[:, None]
    encoder_offset = jnp.sum(jnp.where(same_slab & earlier, clip_lengths[None, :], 0), axis=1)
    matches = order[None, :] == clip_ids[:, None]
    placing = jnp.sum(jnp.where(matches, clip_ids[None, :], 0), axis=1)
    prior_frames = placing[None, :] < placing[:, None]
    packed_start = jnp.sum(jnp.where(prior_frames, clip_lengths[None, :], 0), axis=1)
    return encoder_offset, packed_start


def slot_lookup(clip_lengths, slabs, encoder_offset, packed_start, slab_number, slots):
    slot_list = jnp.arange(slots, dtype=jnp.int32)[:, None]
    lag = slot_list - encoder_offset[None, :]
    inside = (slabs[None, :] == slab_number) & (lag >= 0) & (lag < clip_lengths[None, :])
    age = jnp.sum(jnp.where(inside, lag + 1, 0), axis=1) - 1
    row = jnp.sum(jnp.where(inside, packed_start[None, :] + lag + 1, 0), axis=1) - 1
    return age, row


def row_ages(clip_lengths, packed_start, rows):
    lag = rows[:, None] - packed_start[None, :]
    inside = (lag >= 0) & (lag < clip_lengths[None, :])
    return jnp.sum(jnp.where(inside, lag + 1, 0), axis=1) - 1


def row_slot(clip_lengths, slabs, encoder_offset, packed_start, rows):
    lag = rows[:, None] - packed_start[None, :]
    inside = (lag >= 0) & (lag < clip_lengths[None, :])
    slab = jnp.sum(jnp.where(inside, slabs[None, :], 0), axis=1)
    slot = jnp.sum(jnp.where(inside, encoder_offset[None, :] + lag, 0), axis=1)
    return slab, slot


def tap_offsets():
    return [(1 - row_tap, 1 - col_tap) for row_tap in range(3) for col_tap in range(3)]


def tap_masks():
    row, column = np.divmod(np.arange(PIXELS), PIXEL_COLUMNS)
    masks = []
    for row_step, col_step in tap_offsets():
        good = (0 <= row + row_step) & (row + row_step < PIXEL_ROWS)
        good &= (0 <= column + col_step) & (column + col_step < PIXEL_COLUMNS)
        masks.append(np.broadcast_to(good, (16, PIXELS)))
    return jnp.asarray(np.stack(masks), jnp.bfloat16)


def pixel_taps(frame, masks):
    taps = []
    for t, (row_step, col_step) in enumerate(tap_offsets()):
        offset = row_step * PIXEL_COLUMNS + col_step
        if offset:
            moved = pltpu.roll(frame, (-offset) % PIXELS, 1).reshape(-1, 16, PIXELS)
            taps.append((moved * masks[t][None]).reshape(frame.shape))
        else:
            taps.append(frame)
    return taps


def input_kernel(heads, ages, places, masks, weight, *rest):
    pieces, (out, windows, taps, sems) = rest[:heads], rest[heads:]
    frames, group = out.shape[1:3]
    channels = heads * group
    copies = [
        pltpu.make_async_copy(pieces[k], windows.at[places[k]], sems.at[k]) for k in range(heads)
    ]
    for copy in copies:
        copy.start()
    for copy in copies:
        copy.wait()
    for r in range(frames + 2):
        for g in range(heads):
            for t, tap in enumerate(pixel_taps(windows[g, r], masks)):
                start = t * channels + g * group
                taps[r, start : start + group, :] = tap
        f = r - 2
        if f < 0:
            continue
        total = None
        for d in range(3):
            kernel = jnp.concatenate([weight[9 * (2 - d) + t] for t in range(9)], axis=1)
            term = jnp.dot(kernel, taps[f + d], preferred_element_type=jnp.float32)
            if d == 0:
                total = term
            else:
                total = total + jnp.where(ages[f + d] >= d, term, 0.0)
        for g in range(heads):
            out[g, f] = total[g * group : (g + 1) * group, :].astype(jnp.bfloat16)


def input_part(pieces, weight, ages, places, masks):
    heads = len(pieces)
    frames, group = pieces[0].shape[0] - 2, pieces[0].shape[1]
    channels = heads * group
    smem = pl.BlockSpec(memory_space=pltpu.SMEM)
    vmem = pl.BlockSpec(memory_space=pltpu.VMEM)
    anywhere = pl.BlockSpec(memory_space=pl.ANY)
    return pl.pallas_call(
        functools.partial(input_kernel, heads),
        out_shape=jax.ShapeDtypeStruct((heads, frames, group, PIXELS), jnp.bfloat16),
        in_specs=[smem, smem, vmem, vmem] + [anywhere] * heads,
        out_specs=vmem,
        scratch_shapes=[
            pltpu.VMEM((heads, frames + 2, group, PIXELS), jnp.bfloat16),
            pltpu.VMEM((frames + 2, 9 * channels, PIXELS), jnp.bfloat16),
            pltpu.SemaphoreType.DMA((heads,)),
        ],
        compiler_params=pltpu.CompilerParams(vmem_limit_bytes=32 * MIB),
        cost_estimate=pl.CostEstimate(
            flops=2 * frames * 27 * channels * channels * PIXELS,
            bytes_accessed=2 * 27 * channels * channels,
            transcendentals=0,
        ),
        name="input_grad_part",
    )(ages, places, masks, weight, *pieces)


def early_kernel(masks, weight, out):
    out[...] = masks[...]


def ask_early(masks, weight):
    vmem = pl.BlockSpec(memory_space=pltpu.VMEM)
    return pl.pallas_call(
        early_kernel,
        out_shape=jax.ShapeDtypeStruct(masks.shape, masks.dtype),
        in_specs=[vmem, vmem],
        out_specs=vmem,
        compiler_params=pltpu.CompilerParams(vmem_limit_bytes=16 * MIB),
        name="ask_early",
    )(masks, weight)


def fetch_rows(sources, rows, pieces, target, sems, start, first=0):
    def slot(j, carry):
        if start:
            for p, piece in enumerate(pieces):

                @pl.when(sources[j] == p)
                def _():
                    row = piece.at[rows[j], pl.ds(first, target.shape[1])]
                    pltpu.make_async_copy(row, target.at[j], sems.at[j]).start()

        else:

            @pl.when(sources[j] >= 0)
            def _():
                row = pieces[0].at[0, pl.ds(first, target.shape[1])]
                pltpu.make_async_copy(row, target.at[j], sems.at[j]).wait()

        return carry

    lax.fori_loop(0, target.shape[0], slot, 0)


def blank_rows(sources, target):
    def slot(j, carry):
        @pl.when(sources[j] < 0)
        def _():
            target[j] = jnp.zeros(target.shape[1:], target.dtype)

        return carry

    lax.fori_loop(0, target.shape[0], slot, 0)


def weight_kernel(chunk, scale, half, ages, sources, rows, parity, steps, masks, x, *rest):
    pieces, rest = rest[:-9], rest[-9:]
    mine, theirs, seen, grads, even, odd, total, sems, seen_sems = rest
    slots, group = grads.shape[0], grads.shape[1]
    channels = x.shape[1]
    span = 2 * chunk

    def fetch_seen(p):
        part = pl.ds(p * span, span)
        return pltpu.make_async_copy(x.at[part], seen.at[part], seen_sems.at[p])

    fetch_rows(sources, rows, pieces, grads, sems, True, half * group)
    for p in range(slots // span):
        fetch_seen(p).start()
    total[...] = jnp.zeros_like(total)
    blank_rows(sources, grads)
    fetch_rows(sources, rows, pieces, grads, sems, False, half * group)

    def build(first, taps):
        for f in range(chunk):
            frame = grads[jnp.minimum(first + f, slots - 1)]
            for t, tap in enumerate(pixel_taps(frame, masks)):
                taps[t * group : (t + 1) * group, f * PIXELS : (f + 1) * PIXELS] = tap

    def multiply(first, taps):
        parts = []
        for d in range(3):
            row = []
            for f in range(chunk):
                slot = first + f
                frame = seen[jnp.clip(slot - d, 0, slots - 1)]
                row.append(jnp.where(ages[slot] >= d, frame, jnp.zeros_like(frame)))
            parts.append(jnp.concatenate(row, axis=1))
        total[...] += lax.dot_general(
            jnp.concatenate(parts, axis=0),
            taps[...],
            (((1,), (1,)), ((), ())),
            preferred_element_type=jnp.float32,
        )

    build(0, even)

    def step(p, carry):
        first = 2 * p * chunk
        fetch_seen(p).wait()
        build(first + chunk, odd)
        multiply(first, even)
        build(first + 2 * chunk, even)
        multiply(first + chunk, odd)
        return carry

    def finish(p, carry):
        fetch_seen(p).wait()
        return carry

    lax.fori_loop(0, steps[0], step, 0)
    lax.fori_loop(steps[0], slots // span, finish, 0)
    chips, block = mine.shape[0], mine.shape[2]
    for j in range(chips):
        for target, side in ((mine, parity[0]), (theirs, 1 - parity[0])):
            start = pl.multiple_of((2 * j + side) * block, 8)
            for d in range(3):
                terms = total[pl.ds(d * channels + start, block), :] * scale
                target[j, 2 - d] = terms.astype(jnp.bfloat16)


def weight_part(half, halves, pieces, x, ages, sources, rows, parity, scale, count):
    slots, channels = x.shape[0], x.shape[1]
    group = pieces[0].shape[1] // halves
    chunk = 2
    assert slots % (2 * chunk) == 0
    filled = jnp.sum((ages >= 0).astype(jnp.int32))
    steps = ((filled + 2 * chunk - 1) // (2 * chunk)).reshape((1,))
    ages = jnp.concatenate([ages, jnp.full((2 * chunk,), -1, jnp.int32)])
    smem = pl.BlockSpec(memory_space=pltpu.SMEM)
    vmem = pl.BlockSpec(memory_space=pltpu.VMEM)
    anywhere = pl.BlockSpec(memory_space=pl.ANY)
    blocks = jax.ShapeDtypeStruct((count // 2, 3, channels // count, 9 * group), jnp.bfloat16)
    tap_buffer = pltpu.VMEM((9 * group, chunk * PIXELS), jnp.bfloat16)
    return pl.pallas_call(
        functools.partial(weight_kernel, chunk, scale, half),
        out_shape=(blocks, blocks),
        in_specs=[smem] * 5 + [vmem] + [anywhere] * (1 + len(pieces)),
        out_specs=(vmem, vmem),
        scratch_shapes=[
            pltpu.VMEM(x.shape, jnp.bfloat16),
            pltpu.VMEM((slots, group, PIXELS), jnp.bfloat16),
            tap_buffer,
            tap_buffer,
            pltpu.VMEM((3 * channels, 9 * group), jnp.float32),
            pltpu.SemaphoreType.DMA((slots,)),
            pltpu.SemaphoreType.DMA((slots // (2 * chunk),)),
        ],
        compiler_params=pltpu.CompilerParams(vmem_limit_bytes=59 * MIB),
        cost_estimate=pl.CostEstimate(
            flops=2 * slots * 27 * channels * group * PIXELS,
            bytes_accessed=2 * slots * channels * PIXELS,
            transcendentals=0,
        ),
        name="weight_grad_part",
    )(ages, sources, rows, parity, steps, tap_masks(), x, *pieces)


def pick_kernel(targets, *rest):
    pieces, (here, there, sems) = rest[:-3], rest[-3:]
    slots = here.shape[0]
    places = [(piece, r) for piece in pieces for r in range(piece.shape[0])]
    for start in (True, False):
        for i, (piece, r) in enumerate(places):
            target = targets[i]

            @pl.when((target >= 0) & (target < slots))
            def _():
                copy = pltpu.make_async_copy(piece.at[r], here.at[target], sems.at[i])
                copy.start() if start else copy.wait()

            @pl.when(target >= slots)
            def _():
                copy = pltpu.make_async_copy(piece.at[r], there.at[target - slots], sems.at[i])
                copy.start() if start else copy.wait()


def pick_rows(pieces, targets, slots):
    smem = pl.BlockSpec(memory_space=pltpu.SMEM)
    vmem = pl.BlockSpec(memory_space=pltpu.VMEM)
    anywhere = pl.BlockSpec(memory_space=pl.ANY)
    frames = jax.ShapeDtypeStruct((slots,) + pieces[0].shape[1:], jnp.bfloat16)
    return pl.pallas_call(
        pick_kernel,
        out_shape=(frames, frames),
        in_specs=[smem] + [anywhere] * len(pieces),
        out_specs=(vmem, vmem),
        scratch_shapes=[pltpu.SemaphoreType.DMA((targets.shape[0],))],
        compiler_params=pltpu.CompilerParams(vmem_limit_bytes=60 * MIB),
        cost_estimate=pl.CostEstimate(
            flops=0, bytes_accessed=16 * frames.size, transcendentals=0
        ),
        name="pick_rows",
    )(targets, *pieces)


def swap(value, axis, flip):
    return lax.ppermute(value, axis, [(i, i ^ flip) for i in range(lax.axis_size(axis))])


def to_chips(piece, count):
    flips = (2, 4) if count == 8 else range(2, count, 2)
    return [piece] + [swap(piece, "slab", k) for k in flips]


def passed_on(chips, count):
    if count != 8:
        return []
    half = chips[0].shape[0] // 2
    return [swap(chips[1][:half], "slab", 4), swap(chips[2][half:], "slab", 2)]


def piece_row(chip, row, rows, count):
    if count != 8:
        return chip, row
    half = rows // 2
    second = (chip == 3) & (row >= half)
    return chip + second.astype(jnp.int32), row - jnp.where(second, half, 0)


def joined(parts):
    shape = (len(parts),) + parts[0].shape
    place = lax.broadcasted_iota(jnp.int32, shape, 0)
    whole = jnp.broadcast_to(parts[0][None], shape)
    for k, part in enumerate(parts[1:], 1):
        whole = jnp.where(place == k, part[None], whole)
    return whole.reshape((-1,) + shape[2:])


def with_siblings(chips):
    return chips + [swap(piece, "slab", 1) for piece in chips]


def shards(
    section_activations,
    kernel_weight,
    packed_output_gradient,
    clip_length,
    clip_slab_index,
    packed_clip_order,
):
    slots, channels = section_activations.shape[:2]
    rows, group = packed_output_gradient.shape[:2]
    count, heads = lax.axis_size("slab"), lax.axis_size("head")
    me, head = lax.axis_index("slab"), lax.axis_index("head")
    each, frame = rows // heads, packed_output_gradient.shape[1:]

    after = lax.ppermute(
        packed_output_gradient[:2], "slab", [(i, (i - 1) % count) for i in range(count)]
    )
    longer = jnp.concatenate([packed_output_gradient, after], axis=0)
    windows = [
        lax.dynamic_slice_in_dim(longer, each * (head ^ k), each + 2, 0) for k in range(heads)
    ]
    piece, windows = lax.optimization_barrier((packed_output_gradient, windows))
    windows = windows[:1] + [swap(windows[k], "head", k) for k in range(1, heads)]
    gradient_chips = to_chips(piece, count)
    gradient_late = passed_on(gradient_chips, count)
    masks, windows[1] = lax.optimization_barrier((tap_masks(), windows[1]))
    masks = ask_early(masks, kernel_weight)

    encoder_offset, packed_start = clip_places(clip_length, clip_slab_index, packed_clip_order)
    parity = (me % 2).reshape((1,)).astype(jnp.int32)
    slot_age, slot_row = slot_lookup(
        clip_length, clip_slab_index, encoder_offset, packed_start, me, slots
    )
    shard, inner = jnp.maximum(slot_row, 0) // rows, jnp.maximum(slot_row, 0) % rows
    side, chip = (shard ^ me) % 2, (shard // 2) ^ (me // 2)
    source, source_row = piece_row(chip, inner, rows, count)
    source = jnp.where(slot_row >= 0, side * (5 if count == 8 else count // 2) + source, -1)
    places = head ^ jnp.arange(heads, dtype=jnp.int32)
    window_rows = rows * me + each * head + jnp.arange(each + 2, dtype=jnp.int32)
    window_age = row_ages(clip_length, packed_start, window_rows)

    parts = input_part(windows, kernel_weight, window_age, places, masks)
    parts, gradient_late = lax.optimization_barrier((parts, gradient_late))
    beside = with_siblings(gradient_chips)[len(gradient_chips) :]
    gradient_pieces = gradient_chips + gradient_late + beside
    gradient_pieces += with_siblings(gradient_late)[len(gradient_late) :]
    sent = [lax.dynamic_index_in_dim(parts, head ^ k, 0, keepdims=False) for k in range(heads)]
    arrived = sent[:1] + [swap(sent[k], "head", k) for k in range(1, heads)]

    scale = 1.0 / math.sqrt(rows * count * PIXELS)
    halves = 2 if group % 32 == 0 else 1

    def weight_half(half, x):
        return weight_part(
            half, halves, gradient_pieces, x, slot_age, source, source_row, parity, scale, count
        )

    x, sent = lax.optimization_barrier((section_activations, sent))
    mine, theirs = weight_half(0, x)
    mine, theirs, arrived = lax.optimization_barrier((mine, theirs, arrived))
    chips = to_chips(joined(arrived), count)
    mines, others = [mine], [swap(theirs, "slab", 1)]
    if halves == 2:
        x, chips[0], others = lax.optimization_barrier((x, chips[0], others))
        mine, theirs = weight_half(1, x)
        mine, chips, others = lax.optimization_barrier((mine, chips, others))
        mines.append(mine)
        others.append(swap(theirs, "slab", 1))

    chips = chips + passed_on(chips, count)

    mine, other = jnp.stack(mines, axis=1), jnp.stack(others, axis=1)
    rounded = (mine.astype(jnp.float32) + other.astype(jnp.float32)).astype(jnp.bfloat16)
    my_chip = me // 2
    weight_grad = sum(
        lax.dynamic_index_in_dim(term, my_chip, 0, keepdims=False).astype(jnp.float32)
        for term in (mine, other)
    )
    terms = []
    for k in range(1, count // 2):
        term = lax.dynamic_index_in_dim(rounded, my_chip ^ k, 0, keepdims=False)
        terms.append(swap(term, "slab", 2 * k))
    terms[0], chips = lax.optimization_barrier((terms[0], chips))
    for term in terms:
        weight_grad = weight_grad + term.astype(jnp.float32)
    block = channels // count
    weight_grad = weight_grad.astype(jnp.bfloat16).reshape(halves, 3, block, 9, group // halves)
    weight_grad = weight_grad.transpose(1, 3, 2, 0, 4).reshape(27, block, group)

    shape = (count // 2, heads, each)
    chip, place, row = (lax.broadcasted_iota(jnp.int32, shape, d) for d in range(3))
    packed_row = (2 * (chip ^ my_chip) + me % 2) * rows + (place ^ head) * each + row
    slab, slot = row_slot(
        clip_length, clip_slab_index, encoder_offset, packed_start, packed_row.reshape(-1)
    )
    targets = jnp.where(slab == me, slot, jnp.where(slab == me ^ 1, slots + slot, -1))
    here, there = pick_rows(chips, targets, slots)
    there = swap(there, "slab", 1)
    frames = jnp.where((side == 0)[:, None, None], here, there)
    input_grad = jnp.where((slot_row >= 0)[:, None, None], frames, jnp.zeros_like(frames))
    return (input_grad, weight_grad)


def solution(mesh):
    return jax.shard_map(
        shards,
        mesh=mesh,
        in_specs=(P("slab", None, None), P(), P("slab", "head", None), P(), P(), P()),
        out_specs=(P("slab", "head", None), P(None, "slab", "head")),
        check_vma=False,
    )
```

```python
import functools
import math

import jax
import jax.numpy as jnp
import numpy as np
from jax import lax
from jax.experimental import pallas as pl
from jax.experimental.pallas import tpu as pltpu
from jax.sharding import PartitionSpec as P

PIXEL_ROWS = 16
PIXEL_COLUMNS = 16
PIXELS = PIXEL_ROWS * PIXEL_COLUMNS
MIB = 1024 * 1024


def clip_places(clip_lengths, slabs, order):
    clip_ids = jnp.arange(clip_lengths.shape[0], dtype=jnp.int32)
    same_slab = slabs[None, :] == slabs[:, None]
    earlier = clip_ids[None, :] < clip_ids[:, None]
    encoder_offset = jnp.sum(jnp.where(same_slab & earlier, clip_lengths[None, :], 0), axis=1)
    matches = order[None, :] == clip_ids[:, None]
    placing = jnp.sum(jnp.where(matches, clip_ids[None, :], 0), axis=1)
    prior_frames = placing[None, :] < placing[:, None]
    packed_start = jnp.sum(jnp.where(prior_frames, clip_lengths[None, :], 0), axis=1)
    return encoder_offset, packed_start


def slot_lookup(clip_lengths, slabs, encoder_offset, packed_start, slab_number, slots):
    slot_list = jnp.arange(slots, dtype=jnp.int32)[:, None]
    lag = slot_list - encoder_offset[None, :]
    inside = (slabs[None, :] == slab_number) & (lag >= 0) & (lag < clip_lengths[None, :])
    age = jnp.sum(jnp.where(inside, lag + 1, 0), axis=1) - 1
    row = jnp.sum(jnp.where(inside, packed_start[None, :] + lag + 1, 0), axis=1) - 1
    return age, row


def row_ages(clip_lengths, packed_start, rows):
    lag = rows[:, None] - packed_start[None, :]
    inside = (lag >= 0) & (lag < clip_lengths[None, :])
    return jnp.sum(jnp.where(inside, lag + 1, 0), axis=1) - 1


def row_slot(clip_lengths, slabs, encoder_offset, packed_start, rows):
    lag = rows[:, None] - packed_start[None, :]
    inside = (lag >= 0) & (lag < clip_lengths[None, :])
    slab = jnp.sum(jnp.where(inside, slabs[None, :], 0), axis=1)
    slot = jnp.sum(jnp.where(inside, encoder_offset[None, :] + lag, 0), axis=1)
    return slab, slot


def tap_offsets():
    return [(1 - row_tap, 1 - col_tap) for row_tap in range(3) for col_tap in range(3)]


def tap_masks():
    row, column = np.divmod(np.arange(PIXELS), PIXEL_COLUMNS)
    masks = []
    for row_step, col_step in tap_offsets():
        good = (0 <= row + row_step) & (row + row_step < PIXEL_ROWS)
        good &= (0 <= column + col_step) & (column + col_step < PIXEL_COLUMNS)
        masks.append(np.broadcast_to(good, (16, PIXELS)))
    return jnp.asarray(np.stack(masks), jnp.bfloat16)


def pixel_taps(frame, masks):
    taps = []
    for t, (row_step, col_step) in enumerate(tap_offsets()):
        offset = row_step * PIXEL_COLUMNS + col_step
        if offset:
            moved = pltpu.roll(frame, (-offset) % PIXELS, 1).reshape(-1, 16, PIXELS)
            taps.append((moved * masks[t][None]).reshape(frame.shape))
        else:
            taps.append(frame)
    return taps


def input_kernel(heads, ages, places, masks, weight, *rest):
    pieces, (out, windows, taps, sems) = rest[:heads], rest[heads:]
    frames, group = out.shape[1:3]
    channels = heads * group
    copies = [
        pltpu.make_async_copy(pieces[k], windows.at[places[k]], sems.at[k]) for k in range(heads)
    ]
    for copy in copies:
        copy.start()
    for copy in copies:
        copy.wait()
    for r in range(frames + 2):
        for g in range(heads):
            for t, tap in enumerate(pixel_taps(windows[g, r], masks)):
                start = t * channels + g * group
                taps[r, start : start + group, :] = tap
        f = r - 2
        if f < 0:
            continue
        total = None
        for d in range(3):
            kernel = jnp.concatenate([weight[9 * (2 - d) + t] for t in range(9)], axis=1)
            term = jnp.dot(kernel, taps[f + d], preferred_element_type=jnp.float32)
            if d == 0:
                total = term
            else:
                total = total + jnp.where(ages[f + d] >= d, term, 0.0)
        for g in range(heads):
            out[g, f] = total[g * group : (g + 1) * group, :].astype(jnp.bfloat16)


def input_part(pieces, weight, ages, places, masks):
    heads = len(pieces)
    frames, group = pieces[0].shape[0] - 2, pieces[0].shape[1]
    channels = heads * group
    smem = pl.BlockSpec(memory_space=pltpu.SMEM)
    vmem = pl.BlockSpec(memory_space=pltpu.VMEM)
    anywhere = pl.BlockSpec(memory_space=pl.ANY)
    return pl.pallas_call(
        functools.partial(input_kernel, heads),
        out_shape=jax.ShapeDtypeStruct((heads, frames, group, PIXELS), jnp.bfloat16),
        in_specs=[smem, smem, vmem, vmem] + [anywhere] * heads,
        out_specs=vmem,
        scratch_shapes=[
            pltpu.VMEM((heads, frames + 2, group, PIXELS), jnp.bfloat16),
            pltpu.VMEM((frames + 2, 9 * channels, PIXELS), jnp.bfloat16),
            pltpu.SemaphoreType.DMA((heads,)),
        ],
        compiler_params=pltpu.CompilerParams(vmem_limit_bytes=32 * MIB),
        cost_estimate=pl.CostEstimate(
            flops=2 * frames * 27 * channels * channels * PIXELS,
            bytes_accessed=2 * 27 * channels * channels,
            transcendentals=0,
        ),
        name="input_grad_part",
    )(ages, places, masks, weight, *pieces)


def early_kernel(masks, weight, out):
    out[...] = masks[...]


def ask_early(masks, weight):
    vmem = pl.BlockSpec(memory_space=pltpu.VMEM)
    return pl.pallas_call(
        early_kernel,
        out_shape=jax.ShapeDtypeStruct(masks.shape, masks.dtype),
        in_specs=[vmem, vmem],
        out_specs=vmem,
        compiler_params=pltpu.CompilerParams(vmem_limit_bytes=16 * MIB),
        name="ask_early",
    )(masks, weight)


def fetch_rows(sources, rows, pieces, target, sems, start, first=0):
    def slot(j, carry):
        if start:
            for p, piece in enumerate(pieces):

                @pl.when(sources[j] == p)
                def _():
                    row = piece.at[rows[j], pl.ds(first, target.shape[1])]
                    pltpu.make_async_copy(row, target.at[j], sems.at[j]).start()

        else:

            @pl.when(sources[j] >= 0)
            def _():
                row = pieces[0].at[0, pl.ds(first, target.shape[1])]
                pltpu.make_async_copy(row, target.at[j], sems.at[j]).wait()

        return carry

    lax.fori_loop(0, target.shape[0], slot, 0)


def blank_rows(sources, target):
    def slot(j, carry):
        @pl.when(sources[j] < 0)
        def _():
            target[j] = jnp.zeros(target.shape[1:], target.dtype)

        return carry

    lax.fori_loop(0, target.shape[0], slot, 0)


def weight_kernel(chunk, scale, half, ages, sources, rows, parity, steps, masks, x, *rest):
    pieces, rest = rest[:-9], rest[-9:]
    mine, theirs, seen, grads, even, odd, total, sems, seen_sems = rest
    slots, group = grads.shape[0], grads.shape[1]
    channels = x.shape[1]
    span = 2 * chunk

    def fetch_seen(p):
        part = pl.ds(p * span, span)
        return pltpu.make_async_copy(x.at[part], seen.at[part], seen_sems.at[p])

    fetch_rows(sources, rows, pieces, grads, sems, True, half * group)
    for p in range(slots // span):
        fetch_seen(p).start()
    total[...] = jnp.zeros_like(total)
    blank_rows(sources, grads)
    fetch_rows(sources, rows, pieces, grads, sems, False, half * group)

    def build(first, taps):
        for f in range(chunk):
            frame = grads[jnp.minimum(first + f, slots - 1)]
            for t, tap in enumerate(pixel_taps(frame, masks)):
                taps[t * group : (t + 1) * group, f * PIXELS : (f + 1) * PIXELS] = tap

    def multiply(first, taps):
        parts = []
        for d in range(3):
            row = []
            for f in range(chunk):
                slot = first + f
                frame = seen[jnp.clip(slot - d, 0, slots - 1)]
                row.append(jnp.where(ages[slot] >= d, frame, jnp.zeros_like(frame)))
            parts.append(jnp.concatenate(row, axis=1))
        total[...] += lax.dot_general(
            jnp.concatenate(parts, axis=0),
            taps[...],
            (((1,), (1,)), ((), ())),
            preferred_element_type=jnp.float32,
        )

    build(0, even)

    def step(p, carry):
        first = 2 * p * chunk
        fetch_seen(p).wait()
        build(first + chunk, odd)
        multiply(first, even)
        build(first + 2 * chunk, even)
        multiply(first + chunk, odd)
        return carry

    def finish(p, carry):
        fetch_seen(p).wait()
        return carry

    lax.fori_loop(0, steps[0], step, 0)
    lax.fori_loop(steps[0], slots // span, finish, 0)
    chips, block = mine.shape[0], mine.shape[2]
    for j in range(chips):
        for target, side in ((mine, parity[0]), (theirs, 1 - parity[0])):
            start = pl.multiple_of((2 * j + side) * block, 8)
            for d in range(3):
                terms = total[pl.ds(d * channels + start, block), :] * scale
                target[j, 2 - d] = terms.astype(jnp.bfloat16)


def weight_part(half, halves, pieces, x, ages, sources, rows, parity, scale, count):
    slots, channels = x.shape[0], x.shape[1]
    group = pieces[0].shape[1] // halves
    chunk = 2
    assert slots % (2 * chunk) == 0
    filled = jnp.sum((ages >= 0).astype(jnp.int32))
    steps = ((filled + 2 * chunk - 1) // (2 * chunk)).reshape((1,))
    ages = jnp.concatenate([ages, jnp.full((2 * chunk,), -1, jnp.int32)])
    smem = pl.BlockSpec(memory_space=pltpu.SMEM)
    vmem = pl.BlockSpec(memory_space=pltpu.VMEM)
    anywhere = pl.BlockSpec(memory_space=pl.ANY)
    blocks = jax.ShapeDtypeStruct((count // 2, 3, channels // count, 9 * group), jnp.bfloat16)
    tap_buffer = pltpu.VMEM((9 * group, chunk * PIXELS), jnp.bfloat16)
    return pl.pallas_call(
        functools.partial(weight_kernel, chunk, scale, half),
        out_shape=(blocks, blocks),
        in_specs=[smem] * 5 + [vmem] + [anywhere] * (1 + len(pieces)),
        out_specs=(vmem, vmem),
        scratch_shapes=[
            pltpu.VMEM(x.shape, jnp.bfloat16),
            pltpu.VMEM((slots, group, PIXELS), jnp.bfloat16),
            tap_buffer,
            tap_buffer,
            pltpu.VMEM((3 * channels, 9 * group), jnp.float32),
            pltpu.SemaphoreType.DMA((slots,)),
            pltpu.SemaphoreType.DMA((slots // (2 * chunk),)),
        ],
        compiler_params=pltpu.CompilerParams(vmem_limit_bytes=59 * MIB),
        cost_estimate=pl.CostEstimate(
            flops=2 * slots * 27 * channels * group * PIXELS,
            bytes_accessed=2 * slots * channels * PIXELS,
            transcendentals=0,
        ),
        name="weight_grad_part",
    )(ages, sources, rows, parity, steps, tap_masks(), x, *pieces)


def pick_kernel(targets, *rest):
    pieces, (here, there, sems) = rest[:-3], rest[-3:]
    slots = here.shape[0]
    places = [(piece, r) for piece in pieces for r in range(piece.shape[0])]
    for start in (True, False):
        for i, (piece, r) in enumerate(places):
            target = targets[i]

            @pl.when((target >= 0) & (target < slots))
            def _():
                copy = pltpu.make_async_copy(piece.at[r], here.at[target], sems.at[i])
                copy.start() if start else copy.wait()

            @pl.when(target >= slots)
            def _():
                copy = pltpu.make_async_copy(piece.at[r], there.at[target - slots], sems.at[i])
                copy.start() if start else copy.wait()


def pick_rows(pieces, targets, slots):
    smem = pl.BlockSpec(memory_space=pltpu.SMEM)
    vmem = pl.BlockSpec(memory_space=pltpu.VMEM)
    anywhere = pl.BlockSpec(memory_space=pl.ANY)
    frames = jax.ShapeDtypeStruct((slots,) + pieces[0].shape[1:], jnp.bfloat16)
    return pl.pallas_call(
        pick_kernel,
        out_shape=(frames, frames),
        in_specs=[smem] + [anywhere] * len(pieces),
        out_specs=(vmem, vmem),
        scratch_shapes=[pltpu.SemaphoreType.DMA((targets.shape[0],))],
        compiler_params=pltpu.CompilerParams(vmem_limit_bytes=60 * MIB),
        cost_estimate=pl.CostEstimate(
            flops=0, bytes_accessed=16 * frames.size, transcendentals=0
        ),
        name="pick_rows",
    )(targets, *pieces)


def swap(value, axis, flip):
    return lax.ppermute(value, axis, [(i, i ^ flip) for i in range(lax.axis_size(axis))])


def to_chips(piece, count):
    flips = (2, 4) if count == 8 else range(2, count, 2)
    return [piece] + [swap(piece, "slab", k) for k in flips]


def passed_on(chips, count):
    if count != 8:
        return []
    half = chips[0].shape[0] // 2
    return [swap(chips[1][:half], "slab", 4), swap(chips[2][half:], "slab", 2)]


def piece_row(chip, row, rows, count):
    if count != 8:
        return chip, row
    half = rows // 2
    second = (chip == 3) & (row >= half)
    return chip + second.astype(jnp.int32), row - jnp.where(second, half, 0)


def joined(parts):
    shape = (len(parts),) + parts[0].shape
    place = lax.broadcasted_iota(jnp.int32, shape, 0)
    whole = jnp.broadcast_to(parts[0][None], shape)
    for k, part in enumerate(parts[1:], 1):
        whole = jnp.where(place == k, part[None], whole)
    return whole.reshape((-1,) + shape[2:])


def with_siblings(chips):
    return chips + [swap(piece, "slab", 1) for piece in chips]


def shards(
    section_activations,
    kernel_weight,
    packed_output_gradient,
    clip_length,
    clip_slab_index,
    packed_clip_order,
):
    slots, channels = section_activations.shape[:2]
    rows, group = packed_output_gradient.shape[:2]
    count, heads = lax.axis_size("slab"), lax.axis_size("head")
    me, head = lax.axis_index("slab"), lax.axis_index("head")
    each, frame = rows // heads, packed_output_gradient.shape[1:]

    after = lax.ppermute(
        packed_output_gradient[:2], "slab", [(i, (i - 1) % count) for i in range(count)]
    )
    longer = jnp.concatenate([packed_output_gradient, after], axis=0)
    windows = [
        lax.dynamic_slice_in_dim(longer, each * (head ^ k), each + 2, 0) for k in range(heads)
    ]
    piece, windows = lax.optimization_barrier((packed_output_gradient, windows))
    windows = windows[:1] + [swap(windows[k], "head", k) for k in range(1, heads)]
    gradient_chips = to_chips(piece, count)
    gradient_late = passed_on(gradient_chips, count)
    masks, windows[1] = lax.optimization_barrier((tap_masks(), windows[1]))
    masks = ask_early(masks, kernel_weight)

    encoder_offset, packed_start = clip_places(clip_length, clip_slab_index, packed_clip_order)
    parity = (me % 2).reshape((1,)).astype(jnp.int32)
    slot_age, slot_row = slot_lookup(
        clip_length, clip_slab_index, encoder_offset, packed_start, me, slots
    )
    shard, inner = jnp.maximum(slot_row, 0) // rows, jnp.maximum(slot_row, 0) % rows
    side, chip = (shard ^ me) % 2, (shard // 2) ^ (me // 2)
    source, source_row = piece_row(chip, inner, rows, count)
    source = jnp.where(slot_row >= 0, side * (5 if count == 8 else count // 2) + source, -1)
    places = head ^ jnp.arange(heads, dtype=jnp.int32)
    window_rows = rows * me + each * head + jnp.arange(each + 2, dtype=jnp.int32)
    window_age = row_ages(clip_length, packed_start, window_rows)

    shape = (count // 2, heads, each)
    chip, place, row = (lax.broadcasted_iota(jnp.int32, shape, d) for d in range(3))
    packed_row = (2 * (chip ^ (me // 2)) + me % 2) * rows + (place ^ head) * each + row
    slab, slot = row_slot(
        clip_length, clip_slab_index, encoder_offset, packed_start, packed_row.reshape(-1)
    )
    targets = jnp.where(slab == me, slot, jnp.where(slab == me ^ 1, slots + slot, -1))
    window_age, slot_age, source, source_row, targets = lax.optimization_barrier(
        (window_age, slot_age, source, source_row, targets)
    )

    parts = input_part(windows, kernel_weight, window_age, places, masks)
    parts, gradient_late = lax.optimization_barrier((parts, gradient_late))
    beside = with_siblings(gradient_chips)[len(gradient_chips) :]
    gradient_pieces = gradient_chips + gradient_late + beside
    gradient_pieces += with_siblings(gradient_late)[len(gradient_late) :]
    sent = [lax.dynamic_index_in_dim(parts, head ^ k, 0, keepdims=False) for k in range(heads)]
    arrived = sent[:1] + [swap(sent[k], "head", k) for k in range(1, heads)]

    scale = 1.0 / math.sqrt(rows * count * PIXELS)
    halves = 2 if group % 32 == 0 else 1

    def weight_half(half, x):
        return weight_part(
            half, halves, gradient_pieces, x, slot_age, source, source_row, parity, scale, count
        )

    x, sent = lax.optimization_barrier((section_activations, sent))
    mine, theirs = weight_half(0, x)
    mine, theirs, arrived = lax.optimization_barrier((mine, theirs, arrived))
    chips = to_chips(joined(arrived), count)
    mines, others = [mine], [swap(theirs, "slab", 1)]
    if halves == 2:
        x, chips[0], others = lax.optimization_barrier((x, chips[0], others))
        mine, theirs = weight_half(1, x)
        mine, chips, others = lax.optimization_barrier((mine, chips, others))
        mines.append(mine)
        others.append(swap(theirs, "slab", 1))

    chips = chips + passed_on(chips, count)

    mine, other = jnp.stack(mines, axis=1), jnp.stack(others, axis=1)
    rounded = (mine.astype(jnp.float32) + other.astype(jnp.float32)).astype(jnp.bfloat16)
    my_chip = me // 2
    weight_grad = sum(
        lax.dynamic_index_in_dim(term, my_chip, 0, keepdims=False).astype(jnp.float32)
        for term in (mine, other)
    )
    terms = []
    for k in range(1, count // 2):
        term = lax.dynamic_index_in_dim(rounded, my_chip ^ k, 0, keepdims=False)
        terms.append(swap(term, "slab", 2 * k))
    terms, chips = lax.optimization_barrier((terms, chips))
    for term in terms:
        weight_grad = weight_grad + term.astype(jnp.float32)
    block = channels // count
    weight_grad = weight_grad.astype(jnp.bfloat16).reshape(halves, 3, block, 9, group // halves)
    weight_grad = weight_grad.transpose(1, 3, 2, 0, 4).reshape(27, block, group)

    here, there = pick_rows(chips, targets, slots)
    there = swap(there, "slab", 1)
    frames = jnp.where((side == 0)[:, None, None], here, there)
    input_grad = jnp.where((slot_row >= 0)[:, None, None], frames, jnp.zeros_like(frames))
    return (input_grad, weight_grad)


def solution(mesh):
    return jax.shard_map(
        shards,
        mesh=mesh,
        in_specs=(P("slab", None, None), P(), P("slab", "head", None), P(), P(), P()),
        out_specs=(P("slab", "head", None), P(None, "slab", "head")),
        check_vma=False,
    )
```

```python
import functools
import math

import jax
import jax.numpy as jnp
import numpy as np
from jax import lax
from jax.experimental import pallas as pl
from jax.experimental.pallas import tpu as pltpu
from jax.sharding import PartitionSpec as P

PIXEL_ROWS = 16
PIXEL_COLUMNS = 16
PIXELS = PIXEL_ROWS * PIXEL_COLUMNS
MIB = 1024 * 1024


def clip_places(clip_lengths, slabs, order):
    clip_ids = jnp.arange(clip_lengths.shape[0], dtype=jnp.int32)
    same_slab = slabs[None, :] == slabs[:, None]
    earlier = clip_ids[None, :] < clip_ids[:, None]
    encoder_offset = jnp.sum(jnp.where(same_slab & earlier, clip_lengths[None, :], 0), axis=1)
    matches = order[None, :] == clip_ids[:, None]
    placing = jnp.sum(jnp.where(matches, clip_ids[None, :], 0), axis=1)
    prior_frames = placing[None, :] < placing[:, None]
    packed_start = jnp.sum(jnp.where(prior_frames, clip_lengths[None, :], 0), axis=1)
    return encoder_offset, packed_start


def slot_lookup(clip_lengths, slabs, encoder_offset, packed_start, slab_number, slots):
    slot_list = jnp.arange(slots, dtype=jnp.int32)[:, None]
    lag = slot_list - encoder_offset[None, :]
    inside = (slabs[None, :] == slab_number) & (lag >= 0) & (lag < clip_lengths[None, :])
    age = jnp.sum(jnp.where(inside, lag + 1, 0), axis=1) - 1
    row = jnp.sum(jnp.where(inside, packed_start[None, :] + lag + 1, 0), axis=1) - 1
    return age, row


def row_ages(clip_lengths, packed_start, rows):
    lag = rows[:, None] - packed_start[None, :]
    inside = (lag >= 0) & (lag < clip_lengths[None, :])
    return jnp.sum(jnp.where(inside, lag + 1, 0), axis=1) - 1


def row_slot(clip_lengths, slabs, encoder_offset, packed_start, rows):
    lag = rows[:, None] - packed_start[None, :]
    inside = (lag >= 0) & (lag < clip_lengths[None, :])
    slab = jnp.sum(jnp.where(inside, slabs[None, :], 0), axis=1)
    slot = jnp.sum(jnp.where(inside, encoder_offset[None, :] + lag, 0), axis=1)
    return slab, slot


def tap_offsets():
    return [(1 - row_tap, 1 - col_tap) for row_tap in range(3) for col_tap in range(3)]


def tap_masks():
    row, column = np.divmod(np.arange(PIXELS), PIXEL_COLUMNS)
    masks = []
    for row_step, col_step in tap_offsets():
        good = (0 <= row + row_step) & (row + row_step < PIXEL_ROWS)
        good &= (0 <= column + col_step) & (column + col_step < PIXEL_COLUMNS)
        masks.append(np.broadcast_to(good, (16, PIXELS)))
    return jnp.asarray(np.stack(masks), jnp.bfloat16)


def pixel_taps(frame, masks):
    taps = []
    for t, (row_step, col_step) in enumerate(tap_offsets()):
        offset = row_step * PIXEL_COLUMNS + col_step
        if offset:
            moved = pltpu.roll(frame, (-offset) % PIXELS, 1).reshape(-1, 16, PIXELS)
            taps.append((moved * masks[t][None]).reshape(frame.shape))
        else:
            taps.append(frame)
    return taps


def input_kernel(heads, ages, places, masks, weight, *rest):
    pieces, (out, windows, taps, sems) = rest[:heads], rest[heads:]
    frames, group = out.shape[1:3]
    channels = heads * group
    copies = [
        pltpu.make_async_copy(pieces[k], windows.at[places[k]], sems.at[k]) for k in range(heads)
    ]
    for copy in copies:
        copy.start()
    for copy in copies:
        copy.wait()
    for r in range(frames + 2):
        for g in range(heads):
            for t, tap in enumerate(pixel_taps(windows[g, r], masks)):
                start = t * channels + g * group
                taps[r, start : start + group, :] = tap
        f = r - 2
        if f < 0:
            continue
        total = None
        for d in range(3):
            kernel = jnp.concatenate([weight[9 * (2 - d) + t] for t in range(9)], axis=1)
            term = jnp.dot(kernel, taps[f + d], preferred_element_type=jnp.float32)
            if d == 0:
                total = term
            else:
                total = total + jnp.where(ages[f + d] >= d, term, 0.0)
        for g in range(heads):
            out[g, f] = total[g * group : (g + 1) * group, :].astype(jnp.bfloat16)


def input_part(pieces, weight, ages, places, masks):
    heads = len(pieces)
    frames, group = pieces[0].shape[0] - 2, pieces[0].shape[1]
    channels = heads * group
    smem = pl.BlockSpec(memory_space=pltpu.SMEM)
    vmem = pl.BlockSpec(memory_space=pltpu.VMEM)
    anywhere = pl.BlockSpec(memory_space=pl.ANY)
    return pl.pallas_call(
        functools.partial(input_kernel, heads),
        out_shape=jax.ShapeDtypeStruct((heads, frames, group, PIXELS), jnp.bfloat16),
        in_specs=[smem, smem, vmem, vmem] + [anywhere] * heads,
        out_specs=vmem,
        scratch_shapes=[
            pltpu.VMEM((heads, frames + 2, group, PIXELS), jnp.bfloat16),
            pltpu.VMEM((frames + 2, 9 * channels, PIXELS), jnp.bfloat16),
            pltpu.SemaphoreType.DMA((heads,)),
        ],
        compiler_params=pltpu.CompilerParams(vmem_limit_bytes=32 * MIB),
        cost_estimate=pl.CostEstimate(
            flops=2 * frames * 27 * channels * channels * PIXELS,
            bytes_accessed=2 * 27 * channels * channels,
            transcendentals=0,
        ),
        name="input_grad_part",
    )(ages, places, masks, weight, *pieces)


def early_kernel(masks, weight, out):
    out[...] = masks[...]


def ask_early(masks, weight):
    vmem = pl.BlockSpec(memory_space=pltpu.VMEM)
    return pl.pallas_call(
        early_kernel,
        out_shape=jax.ShapeDtypeStruct(masks.shape, masks.dtype),
        in_specs=[vmem, vmem],
        out_specs=vmem,
        compiler_params=pltpu.CompilerParams(vmem_limit_bytes=16 * MIB),
        name="ask_early",
    )(masks, weight)


def start_rows(targets, pieces, out, sems, first):
    index = 0
    for piece in pieces:
        for r in range(piece.shape[0]):
            target = targets[index]
            index += 1

            @pl.when(target >= 0)
            def _():
                row = piece.at[r, pl.ds(first, out.shape[1])]
                pltpu.make_async_copy(row, out.at[target], sems.at[target]).start()


def wait_rows(ages, pieces, out, sems, first):
    def slot(j, carry):
        @pl.when(ages[j] >= 0)
        def _():
            row = pieces[0].at[0, pl.ds(first, out.shape[1])]
            pltpu.make_async_copy(row, out.at[j], sems.at[j]).wait()

        return carry

    lax.fori_loop(0, out.shape[0], slot, 0)


def blank_rows(ages, target):
    def slot(j, carry):
        @pl.when(ages[j] < 0)
        def _():
            target[j] = jnp.zeros(target.shape[1:], target.dtype)

        return carry

    lax.fori_loop(0, target.shape[0], slot, 0)


def weight_kernel(chunk, scale, half, ages, targets, parity, steps, masks, x, *rest):
    pieces, rest = rest[:-9], rest[-9:]
    mine, theirs, seen, grads, even, odd, total, sems, seen_sems = rest
    slots, group = grads.shape[0], grads.shape[1]
    channels = x.shape[1]
    span = 2 * chunk

    def fetch_seen(p):
        part = pl.ds(p * span, span)
        return pltpu.make_async_copy(x.at[part], seen.at[part], seen_sems.at[p])

    for p in range(slots // span):
        fetch_seen(p).start()
    start_rows(targets, pieces, grads, sems, half * group)
    total[...] = jnp.zeros_like(total)
    blank_rows(ages, grads)
    wait_rows(ages, pieces, grads, sems, half * group)

    def build(first, taps):
        for f in range(chunk):
            frame = grads[jnp.minimum(first + f, slots - 1)]
            for t, tap in enumerate(pixel_taps(frame, masks)):
                taps[t * group : (t + 1) * group, f * PIXELS : (f + 1) * PIXELS] = tap

    def multiply(first, taps):
        parts = []
        for d in range(3):
            row = []
            for f in range(chunk):
                slot = first + f
                frame = seen[jnp.clip(slot - d, 0, slots - 1)]
                row.append(jnp.where(ages[slot] >= d, frame, jnp.zeros_like(frame)))
            parts.append(jnp.concatenate(row, axis=1))
        total[...] += lax.dot_general(
            jnp.concatenate(parts, axis=0),
            taps[...],
            (((1,), (1,)), ((), ())),
            preferred_element_type=jnp.float32,
        )

    build(0, even)

    def step(p, carry):
        first = 2 * p * chunk
        fetch_seen(p).wait()
        build(first + chunk, odd)
        multiply(first, even)
        build(first + 2 * chunk, even)
        multiply(first + chunk, odd)
        return carry

    def finish(p, carry):
        fetch_seen(p).wait()
        return carry

    lax.fori_loop(0, steps[0], step, 0)
    lax.fori_loop(steps[0], slots // span, finish, 0)
    chips, block = mine.shape[0], mine.shape[2]
    for j in range(chips):
        for target, side in ((mine, parity[0]), (theirs, 1 - parity[0])):
            start = pl.multiple_of((2 * j + side) * block, 8)
            for d in range(3):
                terms = total[pl.ds(d * channels + start, block), :] * scale
                target[j, 2 - d] = terms.astype(jnp.bfloat16)


def weight_part(half, halves, pieces, x, ages, targets, parity, scale, count):
    slots, channels = x.shape[0], x.shape[1]
    group = pieces[0].shape[1] // halves
    chunk = 2
    assert slots % (2 * chunk) == 0
    filled = jnp.sum((ages >= 0).astype(jnp.int32))
    steps = ((filled + 2 * chunk - 1) // (2 * chunk)).reshape((1,))
    ages = jnp.concatenate([ages, jnp.full((2 * chunk,), -1, jnp.int32)])
    smem = pl.BlockSpec(memory_space=pltpu.SMEM)
    vmem = pl.BlockSpec(memory_space=pltpu.VMEM)
    anywhere = pl.BlockSpec(memory_space=pl.ANY)
    blocks = jax.ShapeDtypeStruct((count // 2, 3, channels // count, 9 * group), jnp.bfloat16)
    tap_buffer = pltpu.VMEM((9 * group, chunk * PIXELS), jnp.bfloat16)
    return pl.pallas_call(
        functools.partial(weight_kernel, chunk, scale, half),
        out_shape=(blocks, blocks),
        in_specs=[smem] * 4 + [vmem] + [anywhere] * (1 + len(pieces)),
        out_specs=(vmem, vmem),
        scratch_shapes=[
            pltpu.VMEM(x.shape, jnp.bfloat16),
            pltpu.VMEM((slots, group, PIXELS), jnp.bfloat16),
            tap_buffer,
            tap_buffer,
            pltpu.VMEM((3 * channels, 9 * group), jnp.float32),
            pltpu.SemaphoreType.DMA((slots,)),
            pltpu.SemaphoreType.DMA((slots // (2 * chunk),)),
        ],
        compiler_params=pltpu.CompilerParams(vmem_limit_bytes=59 * MIB),
        cost_estimate=pl.CostEstimate(
            flops=2 * slots * 27 * channels * group * PIXELS,
            bytes_accessed=2 * slots * channels * PIXELS,
            transcendentals=0,
        ),
        name="weight_grad_part",
    )(ages, targets, parity, steps, tap_masks(), x, *pieces)


def pick_kernel(targets, *rest):
    pieces, (here, there, sems) = rest[:-3], rest[-3:]
    slots = here.shape[0]
    places = [(piece, r) for piece in pieces for r in range(piece.shape[0])]
    for start in (True, False):
        for i, (piece, r) in enumerate(places):
            target = targets[i]

            @pl.when((target >= 0) & (target < slots))
            def _():
                copy = pltpu.make_async_copy(piece.at[r], here.at[target], sems.at[i])
                copy.start() if start else copy.wait()

            @pl.when(target >= slots)
            def _():
                copy = pltpu.make_async_copy(piece.at[r], there.at[target - slots], sems.at[i])
                copy.start() if start else copy.wait()


def pick_rows(pieces, targets, slots):
    smem = pl.BlockSpec(memory_space=pltpu.SMEM)
    vmem = pl.BlockSpec(memory_space=pltpu.VMEM)
    anywhere = pl.BlockSpec(memory_space=pl.ANY)
    frames = jax.ShapeDtypeStruct((slots,) + pieces[0].shape[1:], jnp.bfloat16)
    return pl.pallas_call(
        pick_kernel,
        out_shape=(frames, frames),
        in_specs=[smem] + [anywhere] * len(pieces),
        out_specs=(vmem, vmem),
        scratch_shapes=[pltpu.SemaphoreType.DMA((targets.shape[0],))],
        compiler_params=pltpu.CompilerParams(vmem_limit_bytes=60 * MIB),
        cost_estimate=pl.CostEstimate(
            flops=0, bytes_accessed=16 * frames.size, transcendentals=0
        ),
        name="pick_rows",
    )(targets, *pieces)


def swap(value, axis, flip):
    return lax.ppermute(value, axis, [(i, i ^ flip) for i in range(lax.axis_size(axis))])


def to_chips(piece, count):
    flips = (2, 4) if count == 8 else range(2, count, 2)
    return [piece] + [swap(piece, "slab", k) for k in flips]


def passed_on(chips, count):
    if count != 8:
        return []
    half = chips[0].shape[0] // 2
    return [swap(chips[1][:half], "slab", 4), swap(chips[2][half:], "slab", 2)]


def joined(parts):
    shape = (len(parts),) + parts[0].shape
    place = lax.broadcasted_iota(jnp.int32, shape, 0)
    whole = jnp.broadcast_to(parts[0][None], shape)
    for k, part in enumerate(parts[1:], 1):
        whole = jnp.where(place == k, part[None], whole)
    return whole.reshape((-1,) + shape[2:])


def with_siblings(chips):
    return chips + [swap(piece, "slab", 1) for piece in chips]


def shards(
    section_activations,
    kernel_weight,
    packed_output_gradient,
    clip_length,
    clip_slab_index,
    packed_clip_order,
):
    slots, channels = section_activations.shape[:2]
    rows, group = packed_output_gradient.shape[:2]
    count, heads = lax.axis_size("slab"), lax.axis_size("head")
    me, head = lax.axis_index("slab"), lax.axis_index("head")
    each, frame = rows // heads, packed_output_gradient.shape[1:]

    after = lax.ppermute(
        packed_output_gradient[:2], "slab", [(i, (i - 1) % count) for i in range(count)]
    )
    longer = jnp.concatenate([packed_output_gradient, after], axis=0)
    windows = [
        lax.dynamic_slice_in_dim(longer, each * (head ^ k), each + 2, 0) for k in range(heads)
    ]
    piece, windows = lax.optimization_barrier((packed_output_gradient, windows))
    windows = windows[:1] + [swap(windows[k], "head", k) for k in range(1, heads)]
    gradient_chips = to_chips(piece, count)
    gradient_late = passed_on(gradient_chips, count)
    masks, windows[1] = lax.optimization_barrier((tap_masks(), windows[1]))
    masks = ask_early(masks, kernel_weight)

    encoder_offset, packed_start = clip_places(clip_length, clip_slab_index, packed_clip_order)
    parity = (me % 2).reshape((1,)).astype(jnp.int32)
    slot_age, slot_row = slot_lookup(
        clip_length, clip_slab_index, encoder_offset, packed_start, me, slots
    )
    shard, inner = jnp.maximum(slot_row, 0) // rows, jnp.maximum(slot_row, 0) % rows
    side, chip = (shard ^ me) % 2, (shard // 2) ^ (me // 2)
    places = head ^ jnp.arange(heads, dtype=jnp.int32)
    window_rows = rows * me + each * head + jnp.arange(each + 2, dtype=jnp.int32)
    window_age = row_ages(clip_length, packed_start, window_rows)

    shape = (count // 2, heads, each)
    chip, place, row = (lax.broadcasted_iota(jnp.int32, shape, d) for d in range(3))
    packed_row = (2 * (chip ^ (me // 2)) + me % 2) * rows + (place ^ head) * each + row
    slab, slot = row_slot(
        clip_length, clip_slab_index, encoder_offset, packed_start, packed_row.reshape(-1)
    )
    targets = jnp.where(slab == me, slot, jnp.where(slab == me ^ 1, slots + slot, -1))
    shape = (2, count // 2, rows)
    beside, chip, row = (lax.broadcasted_iota(jnp.int32, shape, d) for d in range(3))
    packed_row = (2 * (chip ^ (me // 2)) + (beside ^ (me % 2))) * rows + row
    slab, slot = row_slot(
        clip_length, clip_slab_index, encoder_offset, packed_start, packed_row.reshape(-1)
    )
    gradient_targets = jnp.where(slab == me, slot, -1)
    window_age, slot_age, targets, gradient_targets = lax.optimization_barrier(
        (window_age, slot_age, targets, gradient_targets)
    )

    parts = input_part(windows, kernel_weight, window_age, places, masks)
    parts, gradient_late = lax.optimization_barrier((parts, gradient_late))
    beside = with_siblings(gradient_chips)[len(gradient_chips) :]
    gradient_pieces = gradient_chips + gradient_late + beside
    gradient_pieces += with_siblings(gradient_late)[len(gradient_late) :]
    sent = [lax.dynamic_index_in_dim(parts, head ^ k, 0, keepdims=False) for k in range(heads)]
    arrived = sent[:1] + [swap(sent[k], "head", k) for k in range(1, heads)]

    scale = 1.0 / math.sqrt(rows * count * PIXELS)
    halves = 2 if group % 32 == 0 else 1

    def weight_half(half, x):
        return weight_part(
            half, halves, gradient_pieces, x, slot_age, gradient_targets, parity, scale, count
        )

    x, sent = lax.optimization_barrier((section_activations, sent))
    mine, theirs = weight_half(0, x)
    mine, theirs, arrived = lax.optimization_barrier((mine, theirs, arrived))
    chips = to_chips(joined(arrived), count)
    mines, others = [mine], [swap(theirs, "slab", 1)]
    if halves == 2:
        x, chips[0], others = lax.optimization_barrier((x, chips[0], others))
        mine, theirs = weight_half(1, x)
        mine, chips, others = lax.optimization_barrier((mine, chips, others))
        mines.append(mine)
        others.append(swap(theirs, "slab", 1))

    chips = chips + passed_on(chips, count)

    mine, other = jnp.stack(mines, axis=1), jnp.stack(others, axis=1)
    rounded = (mine.astype(jnp.float32) + other.astype(jnp.float32)).astype(jnp.bfloat16)
    my_chip = me // 2
    weight_grad = sum(
        lax.dynamic_index_in_dim(term, my_chip, 0, keepdims=False).astype(jnp.float32)
        for term in (mine, other)
    )
    terms = []
    for k in range(1, count // 2):
        term = lax.dynamic_index_in_dim(rounded, my_chip ^ k, 0, keepdims=False)
        terms.append(swap(term, "slab", 2 * k))
    terms, chips = lax.optimization_barrier((terms, chips))
    for term in terms:
        weight_grad = weight_grad + term.astype(jnp.float32)
    block = channels // count
    weight_grad = weight_grad.astype(jnp.bfloat16).reshape(halves, 3, block, 9, group // halves)
    weight_grad = weight_grad.transpose(1, 3, 2, 0, 4).reshape(27, block, group)

    here, there = pick_rows(chips, targets, slots)
    there = swap(there, "slab", 1)
    frames = jnp.where((side == 0)[:, None, None], here, there)
    input_grad = jnp.where((slot_row >= 0)[:, None, None], frames, jnp.zeros_like(frames))
    return (input_grad, weight_grad)


def solution(mesh):
    return jax.shard_map(
        shards,
        mesh=mesh,
        in_specs=(P("slab", None, None), P(), P("slab", "head", None), P(), P(), P()),
        out_specs=(P("slab", "head", None), P(None, "slab", "head")),
        check_vma=False,
    )
```
